256 devices in a mesh: az: 16 (over z, x_hi), ax: 8 (over y, core), rad: 2 (over x_lo).
Axes of the slice: x: 4 (x_hi: 2, x_lo: 2; x = x_hi * 2 + x_lo), y: 4, z: 8, core: 2. Of those that a mesh axis runs over, the one named last changes fastest.
Arguments:
- fields: float32 [5, 64, 1024, 256], P(None, 'ax', 'az', 'rad'), may hold values from -6 to 6
- coeffs: float32 [5, 6], replicated, may hold values from 0.05 to 0.4
- parcels: float32 [4, 256, 16, 256], P(None, 'ax', 'az', 'rad'), may hold values from -6 to 6, as said below
- cells: int32 [256, 16, 256], P('ax', 'az', 'rad'), may hold values from 0 to 65535
- counts: int32 [8, 16, 2], P('ax', 'az', 'rad'), may hold values from 1024 to 4096, as said below
- moves: int32 [256, 16, 2], P('ax', 'az', 'rad'), may hold values from -1 to 1, as said below
- widths: int32 [16], replicated, may hold values from 2 to 65
Outputs:
- gas_out: float32 [5, 64, 1024, 256], P(None, 'ax', 'az', 'rad')
- parcels_out: float32 [4, 320, 16, 256], P(None, 'ax', 'az', 'rad')
The draws below stay inside these ranges and needn't reach their ends.
Inputs may be any that keep to these rules, and one draw needn't show every extreme that they name: `parcels`: squared diameters (property 3) lie between 0.25 and 2; velocities lie within the range. `counts`: some device holds exactly 4096 live parcels. `moves`: every device sends exactly 4 blocks to the next axial device and 4 to the previous one, except that nothing leaves the first or last axial device across the end.
All inputs are finite; a program needn't handle non-finite values.
Results may differ from the reference program's by a relative error of at most 0.00005.
Values sent between devices are 32-bit elements; how exact they have to be, the bound alone decides.
No kernel may reach another device: no remote copies, remote signals or barrier semaphores. Data moves between devices by JAX's collectives and lax.ppermute only.
A program may use at most 256 MiB of HBM per device.

```python
import math
import jax
import jax.numpy as jnp
from jax import lax

FIELDS = 5
PROPS = 4
CAX = 8
CAZ = 64
CR = 128
CYCLES = 16
MODES = 128
BLK = 128
BLK_DEV = 32
MOVEB = 4
NAX = 64
NAZ = 1024
NR = 256
N_AZ = 16
N_AX = 8
N_RAD = 2


def draw_parcels(key, part):
    key_vel, key_diam = jax.random.split(jax.random.fold_in(key, 11))
    shape = (3, BLK_DEV * N_AX, N_AZ, N_RAD * BLK)
    diam_shape = (BLK_DEV * N_AX, N_AZ, N_RAD * BLK)
    velocity = jnp.clip(jax.random.normal(key_vel, shape, jnp.float32), -4.0, 4.0)
    diam_sq = jnp.exp(jax.random.uniform(key_diam, diam_shape, jnp.float32, jnp.log(0.25), jnp.log(2.0)))
    return jnp.concatenate([velocity, diam_sq[None]], axis=0)


def draw_counts(key, part):
    full_load = BLK_DEV * BLK
    drawn = jax.random.randint(jax.random.fold_in(key, 23), (N_AX, N_AZ, N_RAD), full_load // 4, full_load + 1)
    return drawn.at[0, 0, 0].set(full_load)


def draw_moves(key, part):
    device_total = N_AX * N_AZ * N_RAD
    keys = jax.random.split(jax.random.fold_in(key, 37), device_total)
    orders = jax.vmap(lambda single: jax.random.permutation(single, BLK_DEV))(keys)
    base = jnp.where(orders < MOVEB, 1, jnp.where(orders < 2 * MOVEB, -1, 0)).astype(jnp.int32)
    base = base.reshape(N_AX, N_AZ, N_RAD, BLK_DEV)
    ax_ids = jnp.arange(N_AX, dtype=jnp.int32)[:, None, None, None]
    base = jnp.where((ax_ids == 0) & (base == -1), 0, base)
    base = jnp.where((ax_ids == N_AX - 1) & (base == 1), 0, base)
    return base.transpose(0, 3, 1, 2).reshape(N_AX * BLK_DEV, N_AZ, N_RAD)


def set_ends(values, rng, smallest, top_value):
    spot = [jax.random.randint(jax.random.fold_in(rng, axis), (), 0, length) for axis, length in enumerate(values.shape)]
    longest = values.shape.index(max(values.shape))
    neighbour = spot[:longest] + [(spot[longest] + 1) % values.shape[longest]] + spot[longest + 1:]
    return values.at[tuple(spot)].set(smallest).at[tuple(neighbour)].set(top_value)


def levels(key, dims, cuts, low, largest):
    level, own = 1.0, jax.random.fold_in(key, 6)
    for axis_at, shards_of in cuts:
        steps = jnp.exp(jax.random.uniform(jax.random.fold_in(own, axis_at), (shards_of,), jnp.float32, low / len(cuts), largest / len(cuts)))
        level = level * jnp.repeat(steps, dims[axis_at] // shards_of).reshape([-1 if axis == axis_at else 1 for axis in range(len(dims))])
    return level


def normal_values(stream_key, extent, deviation, most, pieces=(), kind=jnp.bfloat16):
    level = levels(stream_key, extent, pieces, -0.22, 0.18) if pieces else 1.0
    values = jax.random.normal(stream_key, extent, jnp.float32) * deviation * level
    return jnp.minimum(jnp.maximum(values, -most), most).astype(kind)


def setup_inputs(seed: int = 0) -> dict:
    streams_of = jax.random.split(jax.random.key(seed), 8)
    return {
        "fields": normal_values(streams_of[0], (FIELDS, NAX, NAZ, NR), 1.0, 6.0, ((1, 8), (2, 16), (3, 2)), jnp.float32),
        "coeffs": jnp.clip(jax.random.uniform(streams_of[1], (FIELDS, 6), jnp.float32, 0.05, 0.4), 0.05, 0.4),
        "parcels": draw_parcels(jax.random.fold_in(streams_of[7], 71), 0),
        "cells": set_ends(jax.random.randint(streams_of[3], (BLK_DEV * N_AX, N_AZ, N_RAD * BLK), 0, CAX * CAZ * CR), jax.random.fold_in(streams_of[3], 1), 0, (CAX * CAZ * CR) - 1).astype(jnp.int32),
        "counts": draw_counts(jax.random.fold_in(streams_of[7], 71), 0),
        "moves": draw_moves(jax.random.fold_in(streams_of[7], 71), 0),
        "widths": set_ends(jax.random.randint(streams_of[6], (CYCLES,), 2, MODES // 2 + 2), jax.random.fold_in(streams_of[6], 1), 2, (MODES // 2 + 2) - 1).astype(jnp.int32),
    }


STEP_SIZE = 0.5
EVAP_RATE = 0.5
COUPLING = 0.5


def basis_table(positions, total_cells):
    column = jnp.arange(MODES, dtype=jnp.int32)
    half_modes = MODES // 2
    mode_number = jnp.where(column < half_modes, column, column - half_modes + 1)
    phases = (positions[:, None] * mode_number[None, :]) % total_cells
    angles = phases.astype(jnp.float32) * jnp.float32(2.0 * math.pi / total_cells)
    table = jnp.where(column[None, :] < half_modes, jnp.cos(angles), jnp.sin(angles))
    weight = jnp.where(mode_number == 0, 1.0 / total_cells, 2.0 / total_cells).astype(jnp.float32)
    return table, mode_number, weight


def parcel_step(state, gas_vel):
    drop_vel = state[0:3]
    diam_sq = state[3]
    slip = gas_vel - drop_vel
    slip_sq = jnp.sum(slip * slip, axis=0)
    new_vel = (drop_vel * diam_sq + STEP_SIZE * gas_vel) / (diam_sq + STEP_SIZE)
    new_diam = diam_sq / (1.0 + STEP_SIZE * EVAP_RATE * (1.0 + slip_sq))
    mass_loss = diam_sq - new_diam
    momentum = diam_sq * (new_vel - drop_vel)
    sources = jnp.concatenate([mass_loss[None], -momentum, mass_loss[None]], axis=0) * COUPLING
    return jnp.concatenate([new_vel, new_diam[None]], axis=0), sources


def advance(packed):
    one_field, coeff_row = packed
    zero_ax = jnp.zeros_like(one_field[:1])
    ahead_ax = jnp.concatenate([one_field[1:], zero_ax], axis=0)
    behind_ax = jnp.concatenate([zero_ax, one_field[:-1]], axis=0)
    ahead_az = jnp.roll(one_field, -1, axis=1)
    behind_az = jnp.roll(one_field, 1, axis=1)
    zero_rad = jnp.zeros_like(one_field[:, :, :1])
    ahead_rad = jnp.concatenate([one_field[:, :, 1:], zero_rad], axis=2)
    behind_rad = jnp.concatenate([zero_rad, one_field[:, :, :-1]], axis=2)
    metric = 4.0 / (jnp.arange(NR, dtype=jnp.float32) + 4.0)
    twice = 2.0 * one_field
    rhs_terms = coeff_row[0] * (ahead_ax - behind_ax) + coeff_row[1] * (ahead_ax + behind_ax - twice)
    rhs_terms = rhs_terms + metric * (coeff_row[2] * (ahead_az - behind_az) + coeff_row[3] * (ahead_az + behind_az - twice))
    rhs_terms = rhs_terms + coeff_row[4] * (ahead_rad - behind_rad) + coeff_row[5] * (ahead_rad + behind_rad - twice)
    return one_field + STEP_SIZE * rhs_terms


def reference(fields, coeffs, parcels, cells, counts, moves, widths):
    sectioned = lax.map(advance, (fields, coeffs))
    block_ids = jnp.arange(BLK_DEV * N_AX, dtype=jnp.int32)
    ax_dev = (block_ids // BLK_DEV)[:, None, None]
    local_block = (block_ids % BLK_DEV)[:, None, None]
    az_dev = jnp.arange(N_AZ, dtype=jnp.int32)[None, :, None]
    lanes = jnp.arange(N_RAD * BLK, dtype=jnp.int32)[None, None, :]
    rad_dev = lanes // BLK
    slot_index = local_block * BLK + lanes % BLK
    alive = slot_index < counts[ax_dev, az_dev, rad_dev]
    grid_ax = ax_dev * CAX + cells // (CAZ * CR)
    grid_az = az_dev * CAZ + (cells // CR) % CAZ
    grid_rad = rad_dev * CR + cells % CR
    flat_index = ((grid_ax * NAZ + grid_az) * NR + grid_rad).astype(jnp.int32)
    gas_vel = fields[1:4].reshape(3, -1)[:, flat_index]
    new_state, sources = parcel_step(parcels, gas_vel)
    new_state = jnp.where(alive[None], new_state, 0.0)
    sources = jnp.where(alive[None], sources, 0.0)
    sectioned = sectioned.reshape(FIELDS, -1).at[:, flat_index.reshape(-1)].add(sources.reshape(FIELDS, -1))
    sectioned = sectioned.reshape(FIELDS, NAX, NAZ, NR)

    table, mode_number, weight = basis_table(jnp.arange(NAZ, dtype=jnp.int32), NAZ)
    scale = jnp.where(mode_number[None, :] < widths[:, None], weight[None, :], 0.0)
    near_cycles = sectioned[..., :CYCLES]
    coefficients = jnp.einsum("fxzr,zk->fxrk", near_cycles, table, precision=lax.Precision.HIGHEST)
    filtered = jnp.einsum("fxrk,zk->fxzr", coefficients * scale[None, None], table, precision=lax.Precision.HIGHEST)
    gas_out = jnp.concatenate([filtered, sectioned[..., CYCLES:]], axis=3)

    state_dev = new_state.reshape(PROPS, N_AX, BLK_DEV, N_AZ, N_RAD, BLK)
    move_dev = moves.reshape(N_AX, BLK_DEV, N_AZ, N_RAD)
    slots = jnp.arange(MOVEB, dtype=jnp.int32)[:, None, None, None, None]

    def pick_blocks(chosen):
        flags = chosen.astype(jnp.int32)
        ranks = jnp.cumsum(flags, axis=1) - 1
        select = ((ranks[None] == slots) & (flags[None] == 1)).astype(jnp.float32)
        return jnp.einsum("sibzk,pibzkl->pisbzkl", select, state_dev, precision=lax.Precision.HIGHEST).sum(axis=3)

    sent_up = pick_blocks(move_dev == 1)
    sent_down = pick_blocks(move_dev == -1)
    empty_row = jnp.zeros_like(sent_up[:, :1])
    from_below = jnp.concatenate([empty_row, sent_up[:, :-1]], axis=1)
    from_above = jnp.concatenate([sent_down[:, 1:], empty_row], axis=1)
    staying = jnp.where((move_dev == 0)[None, :, :, :, :, None], state_dev, 0.0)
    assembled = jnp.concatenate([staying, from_below, from_above], axis=2)
    parcels_out = assembled.reshape(PROPS, (BLK_DEV + 2 * MOVEB) * N_AX, N_AZ, N_RAD * BLK)
    return gas_out, parcels_out
```

```python
import math

import jax
import jax.numpy as jnp
import numpy as np
from jax import lax
from jax.experimental import pallas as pl
from jax.experimental.pallas import tpu as pltpu
from jax.sharding import PartitionSpec as P

FIELDS = 5
CYCLES = 16
MODES = 128
HALF = MODES // 2
BLK = 128
BLK_DEV = 32
MOVEB = 4
CAX, CAZ, CR = 8, 64, 128
ROWS = CAX * CAZ
PARCELS = BLK * BLK_DEV
NAZ = 1024
N_AZ = 16
PAIRS = CAX // 2
QUADS = CYCLES // 4
LINES = FIELDS * 4

STEP_SIZE = 0.5
EVAP_RATE = 0.5
COUPLING = 0.5

F32 = jnp.float32
BF16 = jnp.bfloat16
HIGHEST = lax.Precision.HIGHEST
VMEM = pl.BlockSpec(memory_space=pltpu.VMEM)
SMEM = pl.BlockSpec(memory_space=pltpu.SMEM)
NT = (((1,), (1,)), ((), ()))


def basis_rows():
    column = np.arange(MODES)
    mode = np.where(column < HALF, column, column - HALF + 1)
    phases = (mode[:, None] * np.arange(NAZ)[None, :]) % NAZ
    angles = phases.astype(np.float32) * np.float32(2.0 * math.pi / NAZ)
    return np.where(column[:, None] < HALF, np.cos(angles), np.sin(angles)).astype(np.float32)


def iota(shape, axis):
    return lax.broadcasted_iota(jnp.int32, shape, axis)


def halves(value):
    high = value.astype(BF16)
    return high, (value - high.astype(F32)).astype(BF16)


def call(body, out_shape, in_specs, flops, nbytes, scratch=(), mib=24):
    return pl.pallas_call(
        body,
        out_shape=[jax.ShapeDtypeStruct(shape, F32) for shape in out_shape],
        in_specs=in_specs,
        out_specs=[VMEM] * len(out_shape),
        scratch_shapes=list(scratch),
        compiler_params=pltpu.CompilerParams(vmem_limit_bytes=mib * 2**20),
        cost_estimate=pl.CostEstimate(flops=flops, bytes_accessed=nbytes, transcendentals=0),
    )


def edges_body(rad_ref, q_ref, ax_lo, ax_hi, az_lo, az_hi, rad_out):
    ax_lo[...] = q_ref[:, 0]
    ax_hi[...] = q_ref[:, CAX - 1]
    az_lo[...] = q_ref[:, :, 0, :]
    az_hi[...] = q_ref[:, :, CAZ - 1, :]
    extra = jnp.where(rad_ref[0] == 0, 1, 0)
    lane = iota((32, CR), 1)
    packed = jnp.zeros((32, CR), F32)
    for f in range(FIELDS):
        for g in range(16):
            part = q_ref[f, g // 2, (g % 2) * 32 : (g % 2) * 32 + 32, :]
            spot = g * 8 + f
            packed = jnp.where(lane == spot, pltpu.roll(part, spot + extra, 1), packed)
    rad_out[...] = packed


def one_hot_rows(cells_ref, first, blocks):
    cells = jnp.concatenate([cells_ref[first + i : first + i + 1, :] for i in range(blocks)], axis=1)
    width = blocks * BLK
    hit = iota((ROWS, width), 0) == (cells >> 7)
    return jnp.where(hit, 1.0, 0.0).astype(BF16), cells & (CR - 1)


def parcels_body(
    count_ref, move_ref, q_ref, parcel_ref, cells_ref,
    src_out, stay_out, up_out, down_out, near_out,
    hot_ref, gas_ref, state_ref, spread_ref,
):
    parts = [[], [], []]
    for f in range(3):
        table = q_ref[f + 1].reshape(ROWS, CR).T
        high = table.astype(BF16)
        rest = table - high.astype(F32)
        mid = rest.astype(BF16)
        parts[0].append(high)
        parts[1].append(mid)
        parts[2].append((rest - mid.astype(F32)).astype(BF16))
    parts = [jnp.concatenate(part, axis=0) for part in parts]
    for first in range(0, BLK_DEV, 4):
        width = 4 * BLK
        hot, lanes = one_hot_rows(cells_ref, first, 4)
        hot_ref[:, first * BLK : first * BLK + width] = hot
        rows = sum(jnp.dot(part, hot, preferred_element_type=F32) for part in parts)
        mask = iota((CR, width), 0) == lanes
        for f in range(3):
            found = jnp.sum(jnp.where(mask, rows[f * CR : (f + 1) * CR], 0.0), axis=0, keepdims=True)
            for i in range(4):
                gas_ref[f, first + i : first + i + 1, :] = found[:, i * BLK : (i + 1) * BLK]
    slot = iota((BLK_DEV, BLK), 0) * BLK + iota((BLK_DEV, BLK), 1)
    alive = slot < count_ref[0]
    diam = parcel_ref[3]
    vel = [parcel_ref[i] for i in range(3)]
    gas = [gas_ref[i] for i in range(3)]
    slip = [g - u for g, u in zip(gas, vel)]
    slip_sq = slip[0] * slip[0] + slip[1] * slip[1] + slip[2] * slip[2]
    new_vel = [(u * diam + STEP_SIZE * g) / (diam + STEP_SIZE) for u, g in zip(vel, gas)]
    new_diam = diam / (1.0 + STEP_SIZE * EVAP_RATE * (1.0 + slip_sq))
    sources = [(diam - new_diam) * COUPLING] + [
        -(diam * (v - u)) * COUPLING for v, u in zip(new_vel, vel)
    ]
    sources = [jnp.where(alive, s, 0.0) for s in sources]
    for i in range(4):
        src_out[i] = sources[i]
        state_ref[i] = jnp.where(alive, (new_vel + [new_diam])[i], 0.0)
    up_out[...] = jnp.zeros_like(up_out)
    down_out[...] = jnp.zeros_like(down_out)

    def place(block, ranks):
        up, down = ranks
        move = move_ref[block]
        row = state_ref[:, pl.ds(block, 1), :]
        stay_out[:, pl.ds(block, 1), :] = jnp.where(move == 0, row, 0.0)

        @pl.when(move == 1)
        def _():
            up_out[:, pl.ds(jnp.minimum(up, MOVEB - 1), 1), :] = row

        @pl.when(move == -1)
        def _():
            down_out[:, pl.ds(jnp.minimum(down, MOVEB - 1), 1), :] = row

        return up + (move == 1).astype(jnp.int32), down + (move == -1).astype(jnp.int32)

    lax.fori_loop(0, BLK_DEV, place, (jnp.int32(0), jnp.int32(0)))
    split = []
    for s in sources:
        high = s.astype(BF16).astype(F32)
        split.append((high, s - high))
    for block in range(BLK_DEV):
        mask = iota((CYCLES, BLK), 0) == (cells_ref[block : block + 1, :] & (CR - 1))
        for i in range(4):
            for half in range(2):
                row = split[i][half][block : block + 1, :]
                first = (half * 4 + i) * CYCLES
                spread_ref[first : first + CYCLES, block * BLK : (block + 1) * BLK] = jnp.where(
                    mask, row, 0.0
                ).astype(BF16)
    total = lax.dot_general(spread_ref[...], hot_ref[...], NT, preferred_element_type=F32)
    near_out[...] = total[: 4 * CYCLES] + total[4 * CYCLES :]


SOURCE_OF = (0, 1, 2, 3, 0)


def section_body(
    rad_ref, coef_ref, q_ref, ax_prev, ax_next, az_prev, az_next, rad_in, near_ref, sect_out, send_out
):
    rad = rad_ref[0]
    lane = iota((CAZ, CR), 1)
    row = iota((CAZ, CR), 0)
    metric = 4.0 / ((rad * CR + lane).astype(F32) + 4.0)
    last = (lane == CR - 1) & (rad == 0)
    first = (lane == 0) & (rad == 1)
    ends = (lane == CR - 1) | (lane == 0)
    for f in range(FIELDS):
        c = [coef_ref[f, i] for i in range(6)]
        mid = (1.0 - c[1] - c[5]) - c[3] * metric
        az_up = (0.5 * (c[2] + c[3])) * metric
        az_down = (0.5 * (c[3] - c[2])) * metric
        ax_up, ax_down = 0.5 * (c[0] + c[1]), 0.5 * (c[1] - c[0])
        rad_up, rad_down = 0.5 * (c[4] + c[5]), 0.5 * (c[5] - c[4])
        for a in range(CAX):
            q = q_ref[f, a]
            ahead = q_ref[f, a + 1] if a + 1 < CAX else ax_next[f]
            behind = q_ref[f, a - 1] if a else ax_prev[f]
            az_a = jnp.where(row == CAZ - 1, az_next[f, a : a + 1, :], pltpu.roll(q, CAZ - 1, 0))
            az_b = jnp.where(row == 0, az_prev[f, a : a + 1, :], pltpu.roll(q, 1, 0))
            edge = jnp.concatenate(
                [rad_in[:, (2 * a + h) * 8 + f : (2 * a + h) * 8 + f + 1] for h in range(2)], axis=0
            )
            edge = jnp.broadcast_to(edge, (CAZ, CR))
            r_a = jnp.where(last, edge, jnp.where(lane == CR - 1, 0.0, pltpu.roll(q, CR - 1, 1)))
            r_b = jnp.where(first, edge, jnp.where(lane == 0, 0.0, pltpu.roll(q, 1, 1)))
            out = (
                mid * q + ax_up * ahead + ax_down * behind + az_up * az_a + az_down * az_b
                + rad_up * r_a + rad_down * r_b
            )
            sect_out[f, a] = out
        for pair in range(PAIRS):
            block = sect_out[f, 2 * pair : 2 * pair + 2].reshape(2 * CAZ, CR).T[:CYCLES]
            s = SOURCE_OF[f] * CYCLES
            block = block + near_ref[s : s + CYCLES, pair * 2 * CAZ : (pair + 1) * 2 * CAZ]
            for quad in range(QUADS):
                send_out[pair * QUADS + quad, f * 4 : f * 4 + 4, :] = block[quad * 4 : quad * 4 + 4]


def scatter_body(sect_ref, src_ref, cells_ref, sect_out, acc_ref):
    step = 8
    for first in range(0, BLK_DEV, step):
        hot, lanes = one_hot_rows(cells_ref, first, step)
        mask = iota((CR, step * BLK), 0) == lanes
        spread = [[], []]
        for i in range(4):
            row = jnp.concatenate([src_ref[i, first + j : first + j + 1, :] for j in range(step)], axis=1)
            high = row.astype(BF16).astype(F32)
            spread[0].append(jnp.where(mask, high, 0.0).astype(BF16))
            spread[1].append(jnp.where(mask, row - high, 0.0).astype(BF16))
        total = sum(
            lax.dot_general(hot, jnp.concatenate(part, axis=0), NT, preferred_element_type=F32)
            for part in spread
        )
        if first == 0:
            acc_ref[...] = total
        else:
            acc_ref[...] += total
    for f in range(FIELDS):
        s = SOURCE_OF[f] * CR
        added = acc_ref[:, s : s + CR].reshape(CAX, CAZ, CR)
        sect_out[f] = sect_ref[f] + added


def filter_body(az_ref, width_ref, basis_ref, got_ref, send_out, line_ref):
    quad = az_ref[0] % QUADS
    lane = iota((LINES, 2 * CAZ), 1)
    low = lane < CAZ
    line_ref[...] = jnp.zeros_like(line_ref)
    for i in range(N_AZ // 2):
        t0, t1 = got_ref[2 * i], got_ref[2 * i + 1]
        cols = slice(i * 2 * CAZ, (i + 1) * 2 * CAZ)
        line_ref[0:LINES, cols] = jnp.where(low, t0, pltpu.roll(t1, CAZ, 1))
        line_ref[24 : 24 + LINES, cols] = jnp.where(low, pltpu.roll(t0, CAZ, 1), t1)
    basis = basis_ref[...]
    coefs = lax.dot_general(line_ref[...], basis, NT, precision=HIGHEST, preferred_element_type=F32)
    column = iota((48, MODES), 1)
    row = iota((48, MODES), 0) % 4
    mode = jnp.where(column < HALF, column, column - HALF + 1)
    width = jnp.zeros((48, MODES), jnp.int32)
    for i in range(4):
        width = jnp.where(row == i, width_ref[quad * 4 + i], width)
    weight = jnp.where(mode == 0, 1.0 / NAZ, 2.0 / NAZ)
    coefs = coefs * jnp.where(mode < width, weight, 0.0)
    line_ref[...] = jnp.dot(coefs, basis, precision=HIGHEST, preferred_element_type=F32)
    for i in range(N_AZ // 2):
        cols = slice(i * 2 * CAZ, (i + 1) * 2 * CAZ)
        t0, t1 = line_ref[0:LINES, cols], line_ref[24 : 24 + LINES, cols]
        send_out[2 * i] = jnp.where(low, t0, pltpu.roll(t1, CAZ, 1))
        send_out[2 * i + 1] = jnp.where(low, pltpu.roll(t0, CAZ, 1), t1)


def merge_body(rad_ref, sect_ref, got_ref, stay_ref, below_ref, above_ref, gas_out, parcels_out, flip_ref):
    near = (iota((2 * CAZ, CR), 1) < CYCLES) & (rad_ref[0] == 0)
    flip_ref[...] = jnp.zeros_like(flip_ref)
    for pair in range(PAIRS):
        for f in range(FIELDS):
            for quad in range(QUADS):
                first = f * CYCLES + quad * 4
                flip_ref[first : first + 4, :] = got_ref[pair * QUADS + quad, f * 4 : f * 4 + 4, :]
        turned = flip_ref[...].T
        for f in range(FIELDS):
            moved = pltpu.roll(turned, (CR - f * CYCLES) % CR, 1) if f else turned
            kept = sect_ref[f, 2 * pair : 2 * pair + 2].reshape(2 * CAZ, CR)
            gas_out[f, 2 * pair : 2 * pair + 2] = jnp.where(near, moved, kept).reshape(2, CAZ, CR)
    parcels_out[:, 0:BLK_DEV, :] = stay_ref[...]
    parcels_out[:, BLK_DEV : BLK_DEV + MOVEB, :] = below_ref[...]
    parcels_out[:, BLK_DEV + MOVEB :, :] = above_ref[...]


def shards(fields, coeffs, parcels, cells, counts, moves, widths):
    rad_index = lax.axis_index("rad").astype(jnp.int32).reshape(1)
    az_index = lax.axis_index("az").astype(jnp.int32).reshape(1)
    n_ax, n_az, n_rad = (lax.axis_size(axis) for axis in ("ax", "az", "rad"))
    parcels = parcels.reshape(4, BLK_DEV, BLK)
    cells = cells.reshape(BLK_DEV, BLK)
    counts = counts.reshape(1)
    moves = moves.reshape(BLK_DEV)
    up = [(i, i + 1) for i in range(n_ax - 1)]
    down = [(i + 1, i) for i in range(n_ax - 1)]
    ahead = [(i, (i + 1) % n_az) for i in range(n_az)]
    back = [((i + 1) % n_az, i) for i in range(n_az)]
    across = [(i, i ^ 1) for i in range(n_rad)]

    ax_lo, ax_hi, az_lo, az_hi, rad_edge = call(
        edges_body,
        [(FIELDS, CAZ, CR)] * 2 + [(FIELDS, CAX, CR)] * 2 + [(32, CR)],
        [SMEM, VMEM], 10**6, 2 * 10**6,
    )(rad_index, fields)
    ax_prev = lax.ppermute(ax_hi, "ax", up)
    ax_next = lax.ppermute(ax_lo, "ax", down)
    az_prev = lax.ppermute(az_hi, "az", ahead)
    az_next = lax.ppermute(az_lo, "az", back)
    rad_got = lax.ppermute(rad_edge, "rad", across)

    src, stay, sent_up, sent_down, near = call(
        parcels_body,
        [(4, BLK_DEV, BLK), (4, BLK_DEV, BLK), (4, MOVEB, BLK), (4, MOVEB, BLK), (4 * CYCLES, ROWS)],
        [SMEM, SMEM, VMEM, VMEM, VMEM], 6 * 10**9, 2 * 10**6,
        [
            pltpu.VMEM((ROWS, PARCELS), BF16),
            pltpu.VMEM((3, BLK_DEV, BLK), F32),
            pltpu.VMEM((4, BLK_DEV, BLK), F32),
            pltpu.VMEM((8 * CYCLES, PARCELS), BF16),
        ],
    )(counts, moves, fields, parcels, cells)
    from_below = lax.ppermute(sent_up, "ax", up)
    from_above = lax.ppermute(sent_down, "ax", down)

    sect, to_owner = call(
        section_body,
        [(FIELDS, CAX, CAZ, CR), (N_AZ, LINES, 2 * CAZ)],
        [SMEM, SMEM] + [VMEM] * 7, 10**7, 4 * 10**6,
    )(rad_index, coeffs, fields, ax_prev, ax_next, az_prev, az_next, rad_got, near)
    lines = lax.all_to_all(to_owner, "az", 0, 0, tiled=True)

    (sect,) = call(
        scatter_body,
        [(FIELDS, CAX, CAZ, CR)],
        [VMEM] * 3, 8 * 10**9, 4 * 10**6,
        [pltpu.VMEM((ROWS, 4 * CR), F32)],
    )(sect, src, cells)

    (to_home,) = call(
        filter_body,
        [(N_AZ, LINES, 2 * CAZ)],
        [SMEM, SMEM, VMEM, VMEM], 10**8, 10**6,
        [pltpu.VMEM((48, NAZ), F32)],
    )(az_index, widths, jnp.asarray(basis_rows()), lines)
    filtered = lax.all_to_all(to_home, "az", 0, 0, tiled=True)

    gas_out, parcels_out = call(
        merge_body,
        [(FIELDS, CAX, CAZ, CR), (4, BLK_DEV + 2 * MOVEB, BLK)],
        [SMEM] + [VMEM] * 5, 10**6, 4 * 10**6,
        [pltpu.VMEM((CR, CR), F32)],
    )(rad_index, sect, filtered, stay, from_below, from_above)
    return gas_out, parcels_out.reshape(4, BLK_DEV + 2 * MOVEB, 1, BLK)


def solution(mesh):
    block = P(None, "ax", "az", "rad")
    flat = P("ax", "az", "rad")
    return jax.shard_map(
        shards,
        mesh=mesh,
        in_specs=(block, P(), block, flat, flat, flat, P()),
        out_specs=(block, block),
        check_vma=False,
    )
```

```python
import math

import jax
import jax.numpy as jnp
import ml_dtypes
import numpy as np
from jax import lax
from jax.experimental import pallas as pl
from jax.experimental.pallas import tpu as pltpu
from jax.sharding import PartitionSpec as P

FIELDS = 5
CYCLES = 16
MODES = 128
HALF = MODES // 2
BLK = 128
BLK_DEV = 32
MOVEB = 4
CAX, CAZ, CR = 8, 64, 128
ROWS = CAX * CAZ
PARCELS = BLK * BLK_DEV
NAZ = 1024
N_AZ = 16
PAIRS = CAX // 2
QUADS = CYCLES // 4
LINES = FIELDS * 4

STEP_SIZE = 0.5
EVAP_RATE = 0.5
COUPLING = 0.5

F32 = jnp.float32
BF16 = jnp.bfloat16
HIGHEST = lax.Precision.HIGHEST
VMEM = pl.BlockSpec(memory_space=pltpu.VMEM)
SMEM = pl.BlockSpec(memory_space=pltpu.SMEM)
NT = (((1,), (1,)), ((), ()))


def basis_rows():
    column = np.arange(MODES)
    mode = np.where(column < HALF, column, column - HALF + 1)
    phases = (mode[:, None] * np.arange(NAZ)[None, :]) % NAZ
    angles = phases.astype(np.float32) * np.float32(2.0 * math.pi / NAZ)
    table = np.where(column[:, None] < HALF, np.cos(angles), np.sin(angles)).astype(np.float32)
    high = table.astype(ml_dtypes.bfloat16)
    low = (table - high.astype(np.float32)).astype(ml_dtypes.bfloat16)
    return np.concatenate([high, low])


def iota(shape, axis):
    return lax.broadcasted_iota(jnp.int32, shape, axis)


def halves(value):
    high = value.astype(BF16)
    return high, (value - high.astype(F32)).astype(BF16)


def call(body, out_shape, in_specs, flops, nbytes, scratch=(), mib=24):
    return pl.pallas_call(
        body,
        out_shape=[jax.ShapeDtypeStruct(shape, F32) for shape in out_shape],
        in_specs=in_specs,
        out_specs=[VMEM] * len(out_shape),
        scratch_shapes=list(scratch),
        compiler_params=pltpu.CompilerParams(vmem_limit_bytes=mib * 2**20),
        cost_estimate=pl.CostEstimate(flops=flops, bytes_accessed=nbytes, transcendentals=0),
    )


def edges_body(odd_ref, q_ref, first_out, second_out):
    odd = odd_ref[0] == 1
    low, high = q_ref[:, 0], q_ref[:, CAX - 1]
    first_out[...] = jnp.where(odd, low, high)
    second_out[...] = jnp.where(odd, high, low)


def one_hot_rows(cells_ref, first, blocks):
    cells = jnp.concatenate([cells_ref[first + i : first + i + 1, :] for i in range(blocks)], axis=1)
    width = blocks * BLK
    hit = iota((ROWS, width), 0) == (cells >> 7)
    return jnp.where(hit, 1.0, 0.0).astype(BF16), cells & (CR - 1)


def parcels_body(
    count_ref, move_ref, q_ref, parcel_ref, cells_ref,
    src_out, stay_out, up_out, down_out, near_out,
    hot_ref, gas_ref, state_ref, spread_ref,
):
    parts = [[], []]
    for f in range(3):
        table = q_ref[f + 1].reshape(ROWS, CR).T
        high, low = halves(table)
        parts[0].append(high)
        parts[1].append(low)
    parts = [jnp.concatenate(part, axis=0) for part in parts]
    for first in range(0, BLK_DEV, 4):
        width = 4 * BLK
        hot, lanes = one_hot_rows(cells_ref, first, 4)
        hot_ref[:, first * BLK : first * BLK + width] = hot
        rows = sum(jnp.dot(part, hot, preferred_element_type=F32) for part in parts)
        mask = iota((CR, width), 0) == lanes
        for f in range(3):
            found = jnp.sum(jnp.where(mask, rows[f * CR : (f + 1) * CR], 0.0), axis=0, keepdims=True)
            for i in range(4):
                gas_ref[f, first + i : first + i + 1, :] = found[:, i * BLK : (i + 1) * BLK]
    slot = iota((BLK_DEV, BLK), 0) * BLK + iota((BLK_DEV, BLK), 1)
    alive = slot < count_ref[0]
    diam = parcel_ref[3]
    vel = [parcel_ref[i] for i in range(3)]
    gas = [gas_ref[i] for i in range(3)]
    slip = [g - u for g, u in zip(gas, vel)]
    slip_sq = slip[0] * slip[0] + slip[1] * slip[1] + slip[2] * slip[2]
    new_vel = [(u * diam + STEP_SIZE * g) / (diam + STEP_SIZE) for u, g in zip(vel, gas)]
    new_diam = diam / (1.0 + STEP_SIZE * EVAP_RATE * (1.0 + slip_sq))
    sources = [(diam - new_diam) * COUPLING] + [
        -(diam * (v - u)) * COUPLING for v, u in zip(new_vel, vel)
    ]
    sources = [jnp.where(alive, s, 0.0) for s in sources]
    for i in range(4):
        src_out[i] = sources[i]
        state_ref[i] = jnp.where(alive, (new_vel + [new_diam])[i], 0.0)
    up_out[...] = jnp.zeros_like(up_out)
    down_out[...] = jnp.zeros_like(down_out)

    def place(block, ranks):
        up, down = ranks
        move = move_ref[block]
        row = state_ref[:, pl.ds(block, 1), :]
        stay_out[:, pl.ds(block, 1), :] = jnp.where(move == 0, row, 0.0)

        @pl.when(move == 1)
        def _():
            up_out[:, pl.ds(jnp.minimum(up, MOVEB - 1), 1), :] = row

        @pl.when(move == -1)
        def _():
            down_out[:, pl.ds(jnp.minimum(down, MOVEB - 1), 1), :] = row

        return up + (move == 1).astype(jnp.int32), down + (move == -1).astype(jnp.int32)

    lax.fori_loop(0, BLK_DEV, place, (jnp.int32(0), jnp.int32(0)))
    split = []
    for s in sources:
        high = s.astype(BF16).astype(F32)
        split.append((high, s - high))
    for block in range(BLK_DEV):
        mask = iota((CYCLES, BLK), 0) == (cells_ref[block : block + 1, :] & (CR - 1))
        for i in range(4):
            for half in range(2):
                row = split[i][half][block : block + 1, :]
                first = (half * 4 + i) * CYCLES
                spread_ref[first : first + CYCLES, block * BLK : (block + 1) * BLK] = jnp.where(
                    mask, row, 0.0
                ).astype(BF16)
    total = lax.dot_general(spread_ref[...], hot_ref[...], NT, preferred_element_type=F32)
    near_out[...] = total[: 4 * CYCLES] + total[4 * CYCLES :]


SOURCE_OF = (0, 1, 2, 3, 0)


BAND = 24


def near_body(
    rad_ref, odd_ref, coef_ref, q_ref, first_ref, second_ref, near_ref,
    send_out, az_lo, az_hi, rad_out,
):
    lane = iota((CR, 2 * CAZ), 1)
    row = iota((CR, 2 * CAZ), 0)
    z = lane % CAZ

    def turned(parts):
        packed = jnp.zeros((2 * CAZ, CR), F32)
        for f, part in enumerate(parts):
            moved = pltpu.roll(part, f * BAND, 1) if f else part
            packed = jnp.where((lane >= f * BAND) & (lane < (f + 1) * BAND), moved, packed)
        return packed.T

    tiles = [
        turned([q_ref[f, 2 * p : 2 * p + 2].reshape(2 * CAZ, CR) for f in range(FIELDS)])
        for p in range(PAIRS)
    ]
    odd = odd_ref[0] == 1
    first, second = first_ref[...], second_ref[...]
    before, after = jnp.where(odd, first, second), jnp.where(odd, second, first)
    halo = turned([jnp.concatenate([before[f], after[f]], axis=0) for f in range(FIELDS)])

    column = iota((CR, 1), 0)
    radius = column
    c = [jnp.zeros((CR, 1), F32) for _ in range(6)]
    for f in range(FIELDS):
        here = (column >= f * BAND) & (column < (f + 1) * BAND)
        radius = jnp.where(here, column - f * BAND, radius)
        c = [jnp.where(here, coef_ref[f, i], c[i]) for i in range(6)]
    metric = 4.0 / (radius.astype(F32) + 4.0)
    mid = (1.0 - c[1] - c[5]) - c[3] * metric
    az_up, az_down = (0.5 * (c[2] + c[3])) * metric, (0.5 * (c[3] - c[2])) * metric
    ax_up, ax_down = 0.5 * (c[0] + c[1]), 0.5 * (c[1] - c[0])
    rad_up = 0.5 * (c[4] + c[5])
    rad_down = jnp.where(radius == 0, 0.0, 0.5 * (c[5] - c[4]))
    low = lane < CAZ
    swapped = [pltpu.roll(t, CAZ, 1) for t in tiles]
    for p in range(PAIRS):
        q = tiles[p]
        ahead = jnp.where(low, swapped[p], swapped[p + 1] if p + 1 < PAIRS else halo)
        behind = jnp.where(low, swapped[p - 1] if p else halo, swapped[p])
        az_a = jnp.where(z == CAZ - 1, 0.0, pltpu.roll(q, 2 * CAZ - 1, 1))
        az_b = jnp.where(z == 0, 0.0, pltpu.roll(q, 1, 1))
        r_a = pltpu.roll(q, CR - 1, 0)
        r_b = pltpu.roll(q, 1, 0)
        out = (
            mid * q + ax_up * ahead + ax_down * behind + az_up * az_a + az_down * az_b
            + rad_up * r_a + rad_down * r_b
        )
        ends = jnp.where(z == 0, az_up * q, jnp.where(z == CAZ - 1, az_down * q, 0.0))
        ends = sum(
            pltpu.roll(ends[f * BAND : f * BAND + CYCLES], 2 * f, 1) if f else ends[:CYCLES]
            for f in range(FIELDS)
        )
        for f in range(FIELDS):
            s = SOURCE_OF[f] * CYCLES
            block = out[f * BAND : f * BAND + CYCLES] + near_ref[
                s : s + CYCLES, p * 2 * CAZ : (p + 1) * 2 * CAZ
            ]
            for quad in range(QUADS):
                send_out[p * QUADS + quad, f * 4 : f * 4 + 4, :] = block[quad * 4 : quad * 4 + 4]
        for quad in range(QUADS):
            send_out[p * QUADS + quad, LINES : LINES + 4, :] = ends[quad * 4 : quad * 4 + 4]
    az_lo[...] = q_ref[:, :, 0, :]
    az_hi[...] = q_ref[:, :, CAZ - 1, :]
    rad_edges(rad_ref[0], q_ref, rad_out)


def rad_edges(rad, q_ref, rad_out):
    extra = jnp.where(rad == 0, 1, 0)
    lane = iota((32, CR), 1)
    packed = jnp.zeros((32, CR), F32)
    for f in range(FIELDS):
        for g in range(16):
            part = q_ref[f, g // 2, (g % 2) * 32 : (g % 2) * 32 + 32, :]
            spot = g * 8 + f
            packed = jnp.where(lane == spot, pltpu.roll(part, spot + extra, 1), packed)
    rad_out[...] = packed


def scatter_body(src_ref, cells_ref, acc_ref):
    step = 8
    for first in range(0, BLK_DEV, step):
        hot, lanes = one_hot_rows(cells_ref, first, step)
        mask = iota((CR, step * BLK), 0) == lanes
        spread = [[], []]
        for i in range(4):
            row = jnp.concatenate([src_ref[i, first + j : first + j + 1, :] for j in range(step)], axis=1)
            high = row.astype(BF16).astype(F32)
            spread[0].append(jnp.where(mask, high, 0.0).astype(BF16))
            spread[1].append(jnp.where(mask, row - high, 0.0).astype(BF16))
        total = sum(
            lax.dot_general(hot, jnp.concatenate(part, axis=0), NT, preferred_element_type=F32)
            for part in spread
        )
        if first == 0:
            acc_ref[...] = total
        else:
            acc_ref[...] += total


def section_body(
    rad_ref, odd_ref, coef_ref, q_ref, first_ref, second_ref, az_prev, az_next, rad_in, acc_ref, sect_out
):
    rad = rad_ref[0]
    odd = odd_ref[0] == 1
    lane = iota((CAZ, CR), 1)
    row = iota((CAZ, CR), 0)
    metric = 4.0 / ((rad * CR + iota((1, CR), 1)).astype(F32) + 4.0)
    target = jnp.where(rad == 0, CR - 1, 0)
    for f in range(FIELDS):
        c = [coef_ref[f, i] for i in range(6)]
        mid = (1.0 - c[1] - c[5]) - c[3] * metric
        az_up = (0.5 * (c[2] + c[3])) * metric
        az_down = (0.5 * (c[3] - c[2])) * metric
        az_up_in = jnp.where(row == CAZ - 1, 0.0, az_up)
        az_down_in = jnp.where(row == 0, 0.0, az_down)
        ax_up, ax_down = 0.5 * (c[0] + c[1]), 0.5 * (c[1] - c[0])
        rad_up, rad_down = 0.5 * (c[4] + c[5]), 0.5 * (c[5] - c[4])
        rad_up_in = jnp.where(iota((1, CR), 1) == CR - 1, 0.0, rad_up)
        rad_down_in = jnp.where(iota((1, CR), 1) == 0, 0.0, rad_down)
        rad_edge = jnp.where(rad == 0, rad_up, rad_down)
        s = SOURCE_OF[f] * CR
        for a in range(CAX):
            q = q_ref[f, a]
            ahead = q_ref[f, a + 1] if a + 1 < CAX else jnp.where(odd, second_ref[f], first_ref[f])
            behind = q_ref[f, a - 1] if a else jnp.where(odd, first_ref[f], second_ref[f])
            out = (
                mid * q + ax_up * ahead + ax_down * behind
                + az_up_in * pltpu.roll(q, CAZ - 1, 0) + az_down_in * pltpu.roll(q, 1, 0)
                + rad_up_in * pltpu.roll(q, CR - 1, 1) + rad_down_in * pltpu.roll(q, 1, 1)
                + acc_ref[a * CAZ : (a + 1) * CAZ, s : s + CR]
            )
            edge = jnp.concatenate(
                [pltpu.roll(rad_in[...], (target + (2 * CR - ((2 * a + h) * 8 + f))) % CR, 1) for h in range(2)],
                axis=0,
            )
            sect_out[f, a] = out + jnp.where(lane == target, rad_edge * edge, 0.0)
            sect_out[f, a, 0:1] += az_down * az_prev[f, a : a + 1]
            sect_out[f, a, CAZ - 1 : CAZ] += az_up * az_next[f, a : a + 1]


def lined(pieces, line_ref):
    low = iota((LINES, 2 * CAZ), 1) < CAZ
    for i in range(N_AZ // 2):
        t0, t1 = pieces(2 * i), pieces(2 * i + 1)
        cols = slice(i * 2 * CAZ, (i + 1) * 2 * CAZ)
        line_ref[0:LINES, cols] = jnp.where(low, t0, pltpu.roll(t1, CAZ, 1))
        line_ref[BAND : BAND + LINES, cols] = jnp.where(low, pltpu.roll(t0, CAZ, 1), t1)


def filter_body(
    az_ref, width_ref, basis_ref, got_ref, up_ref, down_ref,
    send_out, up_out, down_out, line_ref, ends_ref, piece_ref,
):
    up_out[...] = up_ref[...]
    down_out[...] = down_ref[...]
    quad = az_ref[0] % QUADS
    low = iota((LINES, 2 * CAZ), 1) < CAZ
    line_ref[...] = jnp.zeros_like(line_ref)
    ends_ref[...] = jnp.zeros_like(ends_ref)
    for s in range(N_AZ):
        packed = got_ref[s, LINES : LINES + 4, :]
        for f in range(FIELDS):
            piece_ref[s, f * 4 : f * 4 + 4, :] = pltpu.roll(packed, 2 * CAZ - 2 * f, 1) if f else packed
    lined(lambda s: got_ref[s, 0:LINES, :], line_ref)
    lined(lambda s: piece_ref[s], ends_ref)
    z = iota((2 * BAND, NAZ), 1) % CAZ
    ends = ends_ref[...]
    lines = (
        line_ref[...]
        + jnp.where(z == CAZ - 1, pltpu.roll(ends, NAZ - 1, 1), 0.0)
        + jnp.where(z == 0, pltpu.roll(ends, 1, 1), 0.0)
    )
    rows = 2 * BAND
    high, rest = halves(lines)
    both = jnp.concatenate([high, rest], axis=0)
    whole = lax.dot_general(both, basis_ref[:MODES], NT, preferred_element_type=F32)
    part = lax.dot_general(high, basis_ref[MODES:], NT, preferred_element_type=F32)
    coefs = whole[:rows] + whole[rows:] + part
    column = iota((rows, MODES), 1)
    cycle = iota((rows, MODES), 0) % 4
    mode = jnp.where(column < HALF, column, column - HALF + 1)
    width = jnp.zeros((rows, MODES), jnp.int32)
    for i in range(4):
        width = jnp.where(cycle == i, width_ref[quad * 4 + i], width)
    weight = jnp.where(mode == 0, 1.0 / NAZ, 2.0 / NAZ)
    coefs = coefs * jnp.where(mode < width, weight, 0.0)
    high, rest = halves(coefs)
    both = jnp.concatenate([high, rest], axis=0)
    whole = jnp.dot(both, basis_ref[:MODES], preferred_element_type=F32)
    part = jnp.dot(high, basis_ref[MODES:], preferred_element_type=F32)
    line_ref[...] = whole[:rows] + whole[rows:] + part
    for i in range(N_AZ // 2):
        cols = slice(i * 2 * CAZ, (i + 1) * 2 * CAZ)
        t0, t1 = line_ref[0:LINES, cols], line_ref[BAND : BAND + LINES, cols]
        send_out[2 * i] = jnp.where(low, t0, pltpu.roll(t1, CAZ, 1))
        send_out[2 * i + 1] = jnp.where(low, pltpu.roll(t0, CAZ, 1), t1)


def merge_body(rad_ref, sect_ref, got_ref, stay_ref, below_ref, above_ref, gas_out, parcels_out, flip_ref):
    near = (iota((2 * CAZ, CR), 1) < CYCLES) & (rad_ref[0] == 0)
    flip_ref[...] = jnp.zeros_like(flip_ref)
    for pair in range(PAIRS):
        for f in range(FIELDS):
            for quad in range(QUADS):
                first = f * CYCLES + quad * 4
                flip_ref[first : first + 4, :] = got_ref[pair * QUADS + quad, f * 4 : f * 4 + 4, :]
        turned = flip_ref[...].T
        for f in range(FIELDS):
            moved = pltpu.roll(turned, (CR - f * CYCLES) % CR, 1) if f else turned
            kept = sect_ref[f, 2 * pair : 2 * pair + 2].reshape(2 * CAZ, CR)
            gas_out[f, 2 * pair : 2 * pair + 2] = jnp.where(near, moved, kept).reshape(2, CAZ, CR)
    parcels_out[:, 0:BLK_DEV, :] = stay_ref[...]
    parcels_out[:, BLK_DEV : BLK_DEV + MOVEB, :] = below_ref[...]
    parcels_out[:, BLK_DEV + MOVEB :, :] = above_ref[...]


def shards(fields, coeffs, parcels, cells, counts, moves, widths):
    rad_index = lax.axis_index("rad").astype(jnp.int32).reshape(1)
    az_index = lax.axis_index("az").astype(jnp.int32).reshape(1)
    odd = (lax.axis_index("ax").astype(jnp.int32) % 2).reshape(1)
    n_ax, n_az, n_rad = (lax.axis_size(axis) for axis in ("ax", "az", "rad"))
    parcels = parcels.reshape(4, BLK_DEV, BLK)
    cells = cells.reshape(BLK_DEV, BLK)
    counts = counts.reshape(1)
    moves = moves.reshape(BLK_DEV)
    up = [(i, i + 1) for i in range(n_ax - 1)]
    down = [(i + 1, i) for i in range(n_ax - 1)]
    inner = [(i, i ^ 1) for i in range(n_ax)]
    outer = [(i, ((i + 1) ^ 1) - 1) for i in range(1, n_ax - 1)]
    ahead = [(i, (i + 1) % n_az) for i in range(n_az)]
    back = [((i + 1) % n_az, i) for i in range(n_az)]
    across = [(i, i ^ 1) for i in range(n_rad)]

    first, second = call(
        edges_body, [(FIELDS, CAZ, CR)] * 2, [SMEM, VMEM], 10**6, 2 * 10**6, mib=4
    )(odd, fields)
    first = lax.ppermute(first, "ax", inner)
    second = lax.ppermute(second, "ax", outer)

    src, stay, sent_up, sent_down, near = call(
        parcels_body,
        [(4, BLK_DEV, BLK), (4, BLK_DEV, BLK), (4, MOVEB, BLK), (4, MOVEB, BLK), (4 * CYCLES, ROWS)],
        [SMEM, SMEM, VMEM, VMEM, VMEM], 6 * 10**9, 2 * 10**6,
        [
            pltpu.VMEM((ROWS, PARCELS), BF16),
            pltpu.VMEM((3, BLK_DEV, BLK), F32),
            pltpu.VMEM((4, BLK_DEV, BLK), F32),
            pltpu.VMEM((8 * CYCLES, PARCELS), BF16),
        ],
    )(counts, moves, fields, parcels, cells)

    to_owner, az_lo, az_hi, rad_edge = call(
        near_body,
        [(N_AZ, LINES + 4, 2 * CAZ), (FIELDS, CAX, CR), (FIELDS, CAX, CR), (32, CR)],
        [SMEM, SMEM, SMEM] + [VMEM] * 4, 10**7, 4 * 10**6, mib=8,
    )(rad_index, odd, coeffs, fields, first, second, near)
    lines = lax.all_to_all(to_owner, "az", 0, 0, tiled=True)
    az_prev = lax.ppermute(az_hi, "az", ahead)
    az_next = lax.ppermute(az_lo, "az", back)
    rad_got = lax.ppermute(rad_edge, "rad", across)

    (added,) = call(
        scatter_body, [(ROWS, 4 * CR)], [VMEM] * 2, 8 * 10**9, 10**6, mib=16
    )(src, cells)

    to_home, sent_up, sent_down = call(
        filter_body,
        [(N_AZ, LINES, 2 * CAZ), (4, MOVEB, BLK), (4, MOVEB, BLK)],
        [SMEM, SMEM] + [VMEM] * 4, 10**8, 10**6,
        [
            pltpu.VMEM((2 * BAND, NAZ), F32),
            pltpu.VMEM((2 * BAND, NAZ), F32),
            pltpu.VMEM((N_AZ, LINES, 2 * CAZ), F32),
        ],
        mib=6,
    )(az_index, widths, jnp.asarray(basis_rows()), lines, sent_up, sent_down)
    filtered = lax.all_to_all(to_home, "az", 0, 0, tiled=True)
    from_below = lax.ppermute(sent_up, "ax", up)
    from_above = lax.ppermute(sent_down, "ax", down)

    (sect,) = call(
        section_body, [(FIELDS, CAX, CAZ, CR)], [SMEM, SMEM, SMEM] + [VMEM] * 7, 4 * 10**9, 4 * 10**6, mib=8
    )(rad_index, odd, coeffs, fields, first, second, az_prev, az_next, rad_got, added)

    gas_out, parcels_out = call(
        merge_body,
        [(FIELDS, CAX, CAZ, CR), (4, BLK_DEV + 2 * MOVEB, BLK)],
        [SMEM] + [VMEM] * 5, 10**6, 4 * 10**6,
        [pltpu.VMEM((CR, CR), F32)],
        mib=8,
    )(rad_index, sect, filtered, stay, from_below, from_above)
    return gas_out, parcels_out.reshape(4, BLK_DEV + 2 * MOVEB, 1, BLK)


def solution(mesh):
    block = P(None, "ax", "az", "rad")
    flat = P("ax", "az", "rad")
    return jax.shard_map(
        shards,
        mesh=mesh,
        in_specs=(block, P(), block, flat, flat, flat, P()),
        out_specs=(block, block),
        check_vma=False,
    )
```

```python
import math

import jax
import jax.numpy as jnp
import ml_dtypes
import numpy as np
from jax import lax
from jax.experimental import pallas as pl
from jax.experimental.pallas import tpu as pltpu
from jax.sharding import PartitionSpec as P

FIELDS = 5
CYCLES = 16
MODES = 128
HALF = MODES // 2
BLK = 128
BLK_DEV = 32
MOVEB = 4
CAX, CAZ, CR = 8, 64, 128
ROWS = CAX * CAZ
PARCELS = BLK * BLK_DEV
NAZ = 1024
N_AZ = 16
PAIRS = CAX // 2
QUADS = CYCLES // 4
LINES = FIELDS * 4

STEP_SIZE = 0.5
EVAP_RATE = 0.5
COUPLING = 0.5

F32 = jnp.float32
BF16 = jnp.bfloat16
HIGHEST = lax.Precision.HIGHEST
VMEM = pl.BlockSpec(memory_space=pltpu.VMEM)
SMEM = pl.BlockSpec(memory_space=pltpu.SMEM)
ANY = pl.BlockSpec(memory_space=pl.ANY)
HBM = pl.BlockSpec(memory_space=pltpu.HBM)
NT = (((1,), (1,)), ((), ()))


def basis_rows():
    column = np.arange(MODES)
    mode = np.where(column < HALF, column, column - HALF + 1)
    phases = (mode[:, None] * np.arange(NAZ)[None, :]) % NAZ
    angles = phases.astype(np.float32) * np.float32(2.0 * math.pi / NAZ)
    table = np.where(column[:, None] < HALF, np.cos(angles), np.sin(angles)).astype(np.float32)
    high = table.astype(ml_dtypes.bfloat16)
    low = (table - high.astype(np.float32)).astype(ml_dtypes.bfloat16)
    return np.concatenate([high, low])


def iota(shape, axis):
    return lax.broadcasted_iota(jnp.int32, shape, axis)


def halves(value):
    high = value.astype(BF16)
    return high, (value - high.astype(F32)).astype(BF16)


def call(body, out_shape, in_specs, flops, nbytes, scratch=(), mib=24):
    return pl.pallas_call(
        body,
        out_shape=[jax.ShapeDtypeStruct(shape, F32) for shape in out_shape],
        in_specs=in_specs,
        out_specs=[VMEM] * len(out_shape),
        scratch_shapes=list(scratch),
        compiler_params=pltpu.CompilerParams(vmem_limit_bytes=mib * 2**20),
        cost_estimate=pl.CostEstimate(flops=flops, bytes_accessed=nbytes, transcendentals=0),
    )


def one_hot_rows(cells_ref, first, blocks):
    cells = jnp.concatenate([cells_ref[first + i : first + i + 1, :] for i in range(blocks)], axis=1)
    width = blocks * BLK
    hit = iota((ROWS, width), 0) == (cells >> 7)
    return jnp.where(hit, 1.0, 0.0).astype(BF16), cells & (CR - 1)


def parcels_body(
    odd_ref, count_ref, move_ref, q_hbm, parcel_ref, cells_ref,
    src_out, stay_out, first_out, second_out,
    q_ref, hot_ref, gas_ref, state_ref, leave_ref, sems,
):
    odd = odd_ref[0]
    last = CAX - 1
    copies = [
        pltpu.make_async_copy(q_hbm.at[pl.ds(1, 3)], q_ref, sems.at[0]),
        pltpu.make_async_copy(
            q_hbm.at[:, last * (1 - odd)], first_out.at[pl.ds(0, FIELDS)], sems.at[1]
        ),
        pltpu.make_async_copy(q_hbm.at[:, last * odd], second_out.at[pl.ds(0, FIELDS)], sems.at[2]),
    ]
    for copy in copies:
        copy.start()
    for first in range(0, BLK_DEV, 4):
        hot_ref[:, first * BLK : (first + 4) * BLK] = one_hot_rows(cells_ref, first, 4)[0]
    copies[0].wait()
    parts = [[], []]
    for f in range(3):
        table = q_ref[f].reshape(ROWS, CR).T
        high, low = halves(table)
        parts[0].append(high)
        parts[1].append(low)
    parts = [jnp.concatenate(part, axis=0) for part in parts]
    for first in range(0, BLK_DEV, 4):
        width = 4 * BLK
        hot = hot_ref[:, first * BLK : first * BLK + width]
        lanes = jnp.concatenate([cells_ref[first + i : first + i + 1, :] for i in range(4)], axis=1)
        lanes = lanes & (CR - 1)
        rows = sum(jnp.dot(part, hot, preferred_element_type=F32) for part in parts)
        mask = iota((CR, width), 0) == lanes
        for f in range(3):
            found = jnp.sum(jnp.where(mask, rows[f * CR : (f + 1) * CR], 0.0), axis=0, keepdims=True)
            for i in range(4):
                gas_ref[f, first + i : first + i + 1, :] = found[:, i * BLK : (i + 1) * BLK]
    slot = iota((BLK_DEV, BLK), 0) * BLK + iota((BLK_DEV, BLK), 1)
    alive = slot < count_ref[0]
    diam = parcel_ref[3]
    vel = [parcel_ref[i] for i in range(3)]
    gas = [gas_ref[i] for i in range(3)]
    slip = [g - u for g, u in zip(gas, vel)]
    slip_sq = slip[0] * slip[0] + slip[1] * slip[1] + slip[2] * slip[2]
    new_vel = [(u * diam + STEP_SIZE * g) / (diam + STEP_SIZE) for u, g in zip(vel, gas)]
    new_diam = diam / (1.0 + STEP_SIZE * EVAP_RATE * (1.0 + slip_sq))
    sources = [(diam - new_diam) * COUPLING] + [
        -(diam * (v - u)) * COUPLING for v, u in zip(new_vel, vel)
    ]
    sources = [jnp.where(alive, s, 0.0) for s in sources]
    for i in range(4):
        src_out[i] = sources[i]
        state_ref[i] = jnp.where(alive, (new_vel + [new_diam])[i], 0.0)
    leave_ref[...] = jnp.zeros_like(leave_ref)

    def place(block, ranks):
        up, down = ranks
        move = move_ref[block]
        row = state_ref[:, pl.ds(block, 1), :]
        stay_out[:, pl.ds(block, 1), :] = jnp.where(move == 0, row, 0.0)

        @pl.when(move == 1)
        def _():
            leave_ref[0, :, pl.ds(jnp.minimum(up, MOVEB - 1), 1), :] = row

        @pl.when(move == -1)
        def _():
            leave_ref[1, :, pl.ds(jnp.minimum(down, MOVEB - 1), 1), :] = row

        return up + (move == 1).astype(jnp.int32), down + (move == -1).astype(jnp.int32)

    lax.fori_loop(0, BLK_DEV, place, (jnp.int32(0), jnp.int32(0)))
    for out, flag in ((first_out, 0), (second_out, 1)):
        out[FIELDS] = jnp.zeros((CAZ, CR), F32)
        for i in range(4):
            out[FIELDS, 4 * i : 4 * i + 4, :] = jnp.where(odd == flag, leave_ref[0, i], leave_ref[1, i])
    copies[1].wait()
    copies[2].wait()


SOURCE_OF = (0, 1, 2, 3, 0)


BAND = 24
SHARE = 2 * FIELDS * CAX // N_AZ


def near_body(
    rad_ref, odd_ref, coef_ref, q_ref, first_ref, second_ref, near_ref,
    send_out, rad_out, az_ref,
):
    lane = iota((CR, 2 * CAZ), 1)
    row = iota((CR, 2 * CAZ), 0)
    z = lane % CAZ

    def turned(parts):
        packed = jnp.zeros((2 * CAZ, CR), F32)
        for f, part in enumerate(parts):
            moved = pltpu.roll(part, f * BAND, 1) if f else part
            packed = jnp.where((lane >= f * BAND) & (lane < (f + 1) * BAND), moved, packed)
        return packed.T

    tiles = [
        turned([q_ref[f, 2 * p : 2 * p + 2].reshape(2 * CAZ, CR) for f in range(FIELDS)])
        for p in range(PAIRS)
    ]
    odd = odd_ref[0] == 1
    first, second = first_ref[0:FIELDS], second_ref[0:FIELDS]
    before, after = jnp.where(odd, first, second), jnp.where(odd, second, first)
    halo = turned([jnp.concatenate([before[f], after[f]], axis=0) for f in range(FIELDS)])

    column = iota((CR, 1), 0)
    radius = column
    c = [jnp.zeros((CR, 1), F32) for _ in range(6)]
    for f in range(FIELDS):
        here = (column >= f * BAND) & (column < (f + 1) * BAND)
        radius = jnp.where(here, column - f * BAND, radius)
        c = [jnp.where(here, coef_ref[f, i], c[i]) for i in range(6)]
    metric = 4.0 / (radius.astype(F32) + 4.0)
    mid = (1.0 - c[1] - c[5]) - c[3] * metric
    az_up, az_down = (0.5 * (c[2] + c[3])) * metric, (0.5 * (c[3] - c[2])) * metric
    ax_up, ax_down = 0.5 * (c[0] + c[1]), 0.5 * (c[1] - c[0])
    rad_up = 0.5 * (c[4] + c[5])
    rad_down = jnp.where(radius == 0, 0.0, 0.5 * (c[5] - c[4]))
    low = lane < CAZ
    swapped = [pltpu.roll(t, CAZ, 1) for t in tiles]
    for p in range(PAIRS):
        q = tiles[p]
        ahead = jnp.where(low, swapped[p], swapped[p + 1] if p + 1 < PAIRS else halo)
        behind = jnp.where(low, swapped[p - 1] if p else halo, swapped[p])
        az_a = jnp.where(z == CAZ - 1, 0.0, pltpu.roll(q, 2 * CAZ - 1, 1))
        az_b = jnp.where(z == 0, 0.0, pltpu.roll(q, 1, 1))
        r_a = pltpu.roll(q, CR - 1, 0)
        r_b = pltpu.roll(q, 1, 0)
        out = (
            mid * q + ax_up * ahead + ax_down * behind + az_up * az_a + az_down * az_b
            + rad_up * r_a + rad_down * r_b
        )
        ends = jnp.where(z == 0, az_up * q, jnp.where(z == CAZ - 1, az_down * q, 0.0))
        ends = sum(
            pltpu.roll(ends[f * BAND : f * BAND + CYCLES], 2 * f, 1) if f else ends[:CYCLES]
            for f in range(FIELDS)
        )
        for f in range(FIELDS):
            s = SOURCE_OF[f] * CYCLES
            block = out[f * BAND : f * BAND + CYCLES] + near_ref[
                s : s + CYCLES, p * 2 * CAZ : (p + 1) * 2 * CAZ
            ]
            for quad in range(QUADS):
                send_out[p * QUADS + quad, f * 4 : f * 4 + 4, :] = block[quad * 4 : quad * 4 + 4]
        for quad in range(QUADS):
            send_out[p * QUADS + quad, LINES : LINES + 4, :] = ends[quad * 4 : quad * 4 + 4]
    for f in range(FIELDS):
        az_ref[f * CAX : (f + 1) * CAX] = q_ref[f, :, 0, :]
        az_ref[(FIELDS + f) * CAX : (FIELDS + f + 1) * CAX] = q_ref[f, :, CAZ - 1, :]
    for owner in range(N_AZ):
        send_out[owner, LINES + 4 :, :] = az_ref[owner * SHARE : (owner + 1) * SHARE]
    rad_edges(rad_ref[0], q_ref, rad_out)


def rad_edges(rad, q_ref, rad_out):
    extra = jnp.where(rad == 0, 1, 0)
    lane = iota((32, CR), 1)
    packed = jnp.zeros((32, CR), F32)
    for f in range(FIELDS):
        for g in range(16):
            part = q_ref[f, g // 2, (g % 2) * 32 : (g % 2) * 32 + 32, :]
            spot = g * 8 + f
            packed = jnp.where(lane == spot, pltpu.roll(part, spot + extra, 1), packed)
    rad_out[...] = packed


def scattered(src_ref, cells_ref, acc_ref, start, stop, near_ref=None):
    step = 8
    for first in range(0 if near_ref is not None else start, BLK_DEV if near_ref is not None else stop, step):
        hot, lanes = one_hot_rows(cells_ref, first, step)
        rows = [[], []]
        for i in range(4):
            row = jnp.concatenate([src_ref[i, first + j : first + j + 1, :] for j in range(step)], axis=1)
            high = row.astype(BF16).astype(F32)
            rows[0].append(high)
            rows[1].append(row - high)
        if near_ref is not None:
            mask = iota((CYCLES, step * BLK), 0) == lanes
            spread = jnp.concatenate(
                [jnp.where(mask, row, 0.0).astype(BF16) for row in rows[0] + rows[1]], axis=0
            )
            total = lax.dot_general(spread, hot, NT, preferred_element_type=F32)
            total = total[: 4 * CYCLES] + total[4 * CYCLES :]
            if first == 0:
                near_ref[...] = total
            else:
                near_ref[...] += total
        if not start <= first < stop:
            continue
        mask = iota((CR, step * BLK), 0) == lanes
        total = sum(
            lax.dot_general(
                hot,
                jnp.concatenate([jnp.where(mask, row, 0.0).astype(BF16) for row in part], axis=0),
                NT,
                preferred_element_type=F32,
            )
            for part in rows
        )
        if first == start:
            acc_ref[...] = total
        else:
            acc_ref[...] += total


def first_half_body(src_ref, cells_ref, acc_out, near_out):
    scattered(src_ref, cells_ref, acc_out, 0, BLK_DEV // 2, near_out)


def section_body(rad_ref, odd_ref, coef_ref, q_ref, first_ref, second_ref, acc_ref, sect_out):
    rad = rad_ref[0]
    odd = odd_ref[0] == 1
    row = iota((CAZ, CR), 0)
    lane = iota((1, CR), 1)
    metric = 4.0 / ((rad * CR + lane).astype(F32) + 4.0)
    for f in range(FIELDS):
        c = [coef_ref[f, i] for i in range(6)]
        mid = (1.0 - c[1] - c[5]) - c[3] * metric
        az_up = jnp.where(row == CAZ - 1, 0.0, (0.5 * (c[2] + c[3])) * metric)
        az_down = jnp.where(row == 0, 0.0, (0.5 * (c[3] - c[2])) * metric)
        ax_up, ax_down = 0.5 * (c[0] + c[1]), 0.5 * (c[1] - c[0])
        rad_up = jnp.where(lane == CR - 1, 0.0, 0.5 * (c[4] + c[5]))
        rad_down = jnp.where(lane == 0, 0.0, 0.5 * (c[5] - c[4]))
        s = SOURCE_OF[f] * CR
        for a in range(CAX):
            q = q_ref[f, a]
            ahead = q_ref[f, a + 1] if a + 1 < CAX else jnp.where(odd, second_ref[f], first_ref[f])
            behind = q_ref[f, a - 1] if a else jnp.where(odd, first_ref[f], second_ref[f])
            sect_out[f, a] = (
                mid * q + ax_up * ahead + ax_down * behind
                + az_up * pltpu.roll(q, CAZ - 1, 0) + az_down * pltpu.roll(q, 1, 0)
                + rad_up * pltpu.roll(q, CR - 1, 1) + rad_down * pltpu.roll(q, 1, 1)
                + acc_ref[a * CAZ : (a + 1) * CAZ, s : s + CR]
            )


def second_half_body(rad_ref, coef_ref, sect_ref, src_ref, cells_ref, rad_in, sect_out, acc_ref):
    scattered(src_ref, cells_ref, acc_ref, BLK_DEV // 2, BLK_DEV)
    rad = rad_ref[0]
    lane = iota((CAZ, CR), 1)
    target = jnp.where(rad == 0, CR - 1, 0)
    for f in range(FIELDS):
        c4, c5 = coef_ref[f, 4], coef_ref[f, 5]
        weight = 0.5 * jnp.where(rad == 0, c4 + c5, c5 - c4)
        weight = jnp.where(lane == target, weight, 0.0)
        s = SOURCE_OF[f] * CR
        for a in range(CAX):
            edge = jnp.concatenate(
                [pltpu.roll(rad_in[...], (target + (2 * CR - ((2 * a + h) * 8 + f))) % CR, 1) for h in range(2)],
                axis=0,
            )
            sect_out[f, a] = sect_ref[f, a] + acc_ref[a * CAZ : (a + 1) * CAZ, s : s + CR] + weight * edge


def lined(pieces, line_ref):
    low = iota((LINES, 2 * CAZ), 1) < CAZ
    for i in range(N_AZ // 2):
        t0, t1 = pieces(2 * i), pieces(2 * i + 1)
        cols = slice(i * 2 * CAZ, (i + 1) * 2 * CAZ)
        line_ref[0:LINES, cols] = jnp.where(low, t0, pltpu.roll(t1, CAZ, 1))
        line_ref[BAND : BAND + LINES, cols] = jnp.where(low, pltpu.roll(t0, CAZ, 1), t1)


def filter_body(
    az_ref, width_ref, basis_ref, got_ref, _, send_out, line_ref, ends_ref, piece_ref
):
    for home in range(N_AZ):
        send_out[home, LINES:, :] = jnp.where(
            az_ref[0] < N_AZ // 2,
            got_ref[(home + 1) % N_AZ, LINES + 4 :, :],
            got_ref[(home - 1) % N_AZ, LINES + 4 :, :],
        )
    quad = az_ref[0] % QUADS
    low = iota((LINES, 2 * CAZ), 1) < CAZ
    line_ref[...] = jnp.zeros_like(line_ref)
    ends_ref[...] = jnp.zeros_like(ends_ref)
    for s in range(N_AZ):
        packed = got_ref[s, LINES : LINES + 4, :]
        for f in range(FIELDS):
            piece_ref[s, f * 4 : f * 4 + 4, :] = pltpu.roll(packed, 2 * CAZ - 2 * f, 1) if f else packed
    lined(lambda s: got_ref[s, 0:LINES, :], line_ref)
    lined(lambda s: piece_ref[s], ends_ref)
    z = iota((2 * BAND, NAZ), 1) % CAZ
    ends = ends_ref[...]
    lines = (
        line_ref[...]
        + jnp.where(z == CAZ - 1, pltpu.roll(ends, NAZ - 1, 1), 0.0)
        + jnp.where(z == 0, pltpu.roll(ends, 1, 1), 0.0)
    )
    rows = 2 * BAND
    high, rest = halves(lines)
    both = jnp.concatenate([high, rest], axis=0)
    whole = lax.dot_general(both, basis_ref[:MODES], NT, preferred_element_type=F32)
    part = lax.dot_general(high, basis_ref[MODES:], NT, preferred_element_type=F32)
    coefs = whole[:rows] + whole[rows:] + part
    column = iota((rows, MODES), 1)
    cycle = iota((rows, MODES), 0) % 4
    mode = jnp.where(column < HALF, column, column - HALF + 1)
    width = jnp.zeros((rows, MODES), jnp.int32)
    for i in range(4):
        width = jnp.where(cycle == i, width_ref[quad * 4 + i], width)
    weight = jnp.where(mode == 0, 1.0 / NAZ, 2.0 / NAZ)
    coefs = coefs * jnp.where(mode < width, weight, 0.0)
    high, rest = halves(coefs)
    both = jnp.concatenate([high, rest], axis=0)
    whole = jnp.dot(both, basis_ref[:MODES], preferred_element_type=F32)
    part = jnp.dot(high, basis_ref[MODES:], preferred_element_type=F32)
    line_ref[...] = whole[:rows] + whole[rows:] + part
    for i in range(N_AZ // 2):
        cols = slice(i * 2 * CAZ, (i + 1) * 2 * CAZ)
        t0, t1 = line_ref[0:LINES, cols], line_ref[BAND : BAND + LINES, cols]
        send_out[2 * i, 0:LINES] = jnp.where(low, t0, pltpu.roll(t1, CAZ, 1))
        send_out[2 * i + 1, 0:LINES] = jnp.where(low, pltpu.roll(t0, CAZ, 1), t1)


def merge_body(
    rad_ref, odd_ref, coef_ref, sect_ref, got_ref, stay_ref, first_ref, second_ref,
    gas_out, parcels_out, flip_ref, az_ref,
):
    near = (iota((2 * CAZ, CR), 1) < CYCLES) & (rad_ref[0] == 0)
    flip_ref[...] = jnp.zeros_like(flip_ref)
    for owner in range(N_AZ):
        az_ref[owner * SHARE : (owner + 1) * SHARE] = got_ref[owner, LINES:, :]
    for pair in range(PAIRS):
        for f in range(FIELDS):
            for quad in range(QUADS):
                first = f * CYCLES + quad * 4
                flip_ref[first : first + 4, :] = got_ref[pair * QUADS + quad, f * 4 : f * 4 + 4, :]
        turned = flip_ref[...].T
        for f in range(FIELDS):
            moved = pltpu.roll(turned, (CR - f * CYCLES) % CR, 1) if f else turned
            kept = sect_ref[f, 2 * pair : 2 * pair + 2].reshape(2 * CAZ, CR)
            gas_out[f, 2 * pair : 2 * pair + 2] = jnp.where(near, moved, kept).reshape(2, CAZ, CR)
    lane = iota((1, CR), 1)
    metric = 4.0 / ((rad_ref[0] * CR + lane).astype(F32) + 4.0)
    metric = jnp.where((lane < CYCLES) & (rad_ref[0] == 0), 0.0, metric)
    for f in range(FIELDS):
        az_up = (0.5 * (coef_ref[f, 2] + coef_ref[f, 3])) * metric
        az_down = (0.5 * (coef_ref[f, 3] - coef_ref[f, 2])) * metric
        after = az_up * az_ref[f * CAX : (f + 1) * CAX]
        before = az_down * az_ref[(FIELDS + f) * CAX : (FIELDS + f + 1) * CAX]
        for a in range(CAX):
            gas_out[f, a, 0:1] += before[a : a + 1]
            gas_out[f, a, CAZ - 1 : CAZ] += after[a : a + 1]
    odd = odd_ref[0] == 1
    parcels_out[:, 0:BLK_DEV, :] = stay_ref[...]
    for i in range(4):
        first, second = first_ref[FIELDS, 4 * i : 4 * i + 4, :], second_ref[FIELDS, 4 * i : 4 * i + 4, :]
        parcels_out[i, BLK_DEV : BLK_DEV + MOVEB, :] = jnp.where(odd, first, second)
        parcels_out[i, BLK_DEV + MOVEB :, :] = jnp.where(odd, second, first)


def shards(fields, coeffs, parcels, cells, counts, moves, widths):
    rad_index = lax.axis_index("rad").astype(jnp.int32).reshape(1)
    az_index = lax.axis_index("az").astype(jnp.int32).reshape(1)
    odd = (lax.axis_index("ax").astype(jnp.int32) % 2).reshape(1)
    n_ax, n_rad = lax.axis_size("ax"), lax.axis_size("rad")
    parcels = parcels.reshape(4, BLK_DEV, BLK)
    cells = cells.reshape(BLK_DEV, BLK)
    counts = counts.reshape(1)
    moves = moves.reshape(BLK_DEV)
    inner = [(i, i ^ 1) for i in range(n_ax)]
    outer = [(i, ((i + 1) ^ 1) - 1) for i in range(1, n_ax - 1)]
    across = [(i, i ^ 1) for i in range(n_rad)]
    gas_shape = (FIELDS, CAX, CAZ, CR)

    src, stay, first, second = call(
        parcels_body,
        [(4, BLK_DEV, BLK), (4, BLK_DEV, BLK)] + [(FIELDS + 1, CAZ, CR)] * 2,
        [SMEM, SMEM, SMEM, HBM, VMEM, VMEM], 6 * 10**9, 2 * 10**6,
        [
            pltpu.VMEM((3, CAX, CAZ, CR), F32),
            pltpu.VMEM((ROWS, PARCELS), BF16),
            pltpu.VMEM((3, BLK_DEV, BLK), F32),
            pltpu.VMEM((4, BLK_DEV, BLK), F32),
            pltpu.VMEM((2, 4, MOVEB, BLK), F32),
            pltpu.SemaphoreType.DMA((3,)),
        ],
        mib=62,
    )(odd, counts, moves, fields, parcels, cells)
    first = lax.ppermute(first, "ax", inner)
    second = lax.ppermute(second, "ax", outer)

    added, near = call(
        first_half_body, [(ROWS, 4 * CR), (4 * CYCLES, ROWS)], [VMEM] * 2, 4 * 10**9, 10**6, mib=16
    )(src, cells)

    to_owner, rad_edge = call(
        near_body,
        [(N_AZ, LINES + 4 + SHARE, 2 * CAZ), (32, CR)],
        [SMEM, SMEM, SMEM] + [VMEM] * 4, 10**7, 4 * 10**6,
        [pltpu.VMEM((2 * FIELDS * CAX, CR), F32)],
        mib=8,
    )(rad_index, odd, coeffs, fields, first, second, near)
    lines = lax.all_to_all(to_owner, "az", 0, 0, tiled=True)
    rad_got = lax.ppermute(rad_edge, "rad", across)

    (sect,) = call(
        section_body, [gas_shape], [SMEM, SMEM, SMEM] + [VMEM] * 4, 2 * 10**9, 4 * 10**6, mib=8
    )(rad_index, odd, coeffs, fields, first, second, added)

    (to_home,) = call(
        filter_body,
        [(N_AZ, LINES + SHARE, 2 * CAZ)],
        [SMEM, SMEM] + [VMEM] * 2 + [ANY], 10**8, 10**6,
        [
            pltpu.VMEM((2 * BAND, NAZ), F32),
            pltpu.VMEM((2 * BAND, NAZ), F32),
            pltpu.VMEM((N_AZ, LINES, 2 * CAZ), F32),
        ],
        mib=6,
    )(az_index, widths, jnp.asarray(basis_rows()), lines, sect)
    filtered = lax.all_to_all(to_home, "az", 0, 0, tiled=True)

    (sect,) = call(
        second_half_body, [gas_shape], [SMEM, SMEM] + [VMEM] * 4, 4 * 10**9, 4 * 10**6,
        [pltpu.VMEM((ROWS, 4 * CR), F32)],
        mib=16,
    )(rad_index, coeffs, sect, src, cells, rad_got)

    gas_out, parcels_out = call(
        merge_body,
        [gas_shape, (4, BLK_DEV + 2 * MOVEB, BLK)],
        [SMEM, SMEM, SMEM] + [VMEM] * 5, 10**6, 4 * 10**6,
        [pltpu.VMEM((CR, CR), F32), pltpu.VMEM((2 * FIELDS * CAX, CR), F32)],
        mib=8,
    )(rad_index, odd, coeffs, sect, filtered, stay, first, second)
    return gas_out, parcels_out.reshape(4, BLK_DEV + 2 * MOVEB, 1, BLK)


def solution(mesh):
    block = P(None, "ax", "az", "rad")
    flat = P("ax", "az", "rad")
    return jax.shard_map(
        shards,
        mesh=mesh,
        in_specs=(block, P(), block, flat, flat, flat, P()),
        out_specs=(block, block),
        check_vma=False,
    )
```

```python
import math

import jax
import jax.numpy as jnp
import ml_dtypes
import numpy as np
from jax import lax
from jax.experimental import pallas as pl
from jax.experimental.pallas import tpu as pltpu
from jax.sharding import PartitionSpec as P

FIELDS = 5
CYCLES = 16
MODES = 128
HALF = MODES // 2
BLK = 128
BLK_DEV = 32
MOVEB = 4
CAX, CAZ, CR = 8, 64, 128
ROWS = CAX * CAZ
PARCELS = BLK * BLK_DEV
NAZ = 1024
N_AZ = 16
PAIRS = CAX // 2
QUADS = CYCLES // 4
LINES = FIELDS * 4

STEP_SIZE = 0.5
EVAP_RATE = 0.5
COUPLING = 0.5

F32 = jnp.float32
BF16 = jnp.bfloat16
HIGHEST = lax.Precision.HIGHEST
VMEM = pl.BlockSpec(memory_space=pltpu.VMEM)
SMEM = pl.BlockSpec(memory_space=pltpu.SMEM)
ANY = pl.BlockSpec(memory_space=pl.ANY)
HBM = pl.BlockSpec(memory_space=pltpu.HBM)
NT = (((1,), (1,)), ((), ()))


def basis_rows():
    column = np.arange(MODES)
    mode = np.where(column < HALF, column, column - HALF + 1)
    phases = (mode[:, None] * np.arange(NAZ)[None, :]) % NAZ
    angles = phases.astype(np.float32) * np.float32(2.0 * math.pi / NAZ)
    table = np.where(column[:, None] < HALF, np.cos(angles), np.sin(angles)).astype(np.float32)
    high = table.astype(ml_dtypes.bfloat16)
    low = (table - high.astype(np.float32)).astype(ml_dtypes.bfloat16)
    return np.concatenate([high, low])


def iota(shape, axis):
    return lax.broadcasted_iota(jnp.int32, shape, axis)


def halves(value):
    high = value.astype(BF16)
    return high, (value - high.astype(F32)).astype(BF16)


def call(body, out_shape, in_specs, flops, nbytes, scratch=(), mib=24):
    return pl.pallas_call(
        body,
        out_shape=[jax.ShapeDtypeStruct(shape, F32) for shape in out_shape],
        in_specs=in_specs,
        out_specs=[VMEM] * len(out_shape),
        scratch_shapes=list(scratch),
        compiler_params=pltpu.CompilerParams(vmem_limit_bytes=mib * 2**20),
        cost_estimate=pl.CostEstimate(flops=flops, bytes_accessed=nbytes, transcendentals=0),
    )


def edges_body(odd_ref, q_hbm, first_out, second_out, sems):
    odd, last = odd_ref[0], CAX - 1
    copies = [
        pltpu.make_async_copy(q_hbm.at[:, last * (1 - odd)], first_out, sems.at[0]),
        pltpu.make_async_copy(q_hbm.at[:, last * odd], second_out, sems.at[1]),
    ]
    for copy in copies:
        copy.start()
    for copy in copies:
        copy.wait()


def one_hot_rows(cells_ref, first, blocks):
    cells = jnp.concatenate([cells_ref[first + i : first + i + 1, :] for i in range(blocks)], axis=1)
    width = blocks * BLK
    hit = iota((ROWS, width), 0) == (cells >> 7)
    return jnp.where(hit, 1.0, 0.0).astype(BF16), cells & (CR - 1)


def lane_row(cells_ref, first, blocks):
    return jnp.concatenate([cells_ref[first + i : first + i + 1, :] for i in range(blocks)], axis=1) & (CR - 1)


def step(count_ref, parcel_ref, gas_ref):
    slot = iota((BLK_DEV, BLK), 0) * BLK + iota((BLK_DEV, BLK), 1)
    alive = slot < count_ref[0]
    diam = parcel_ref[3]
    vel = [parcel_ref[i] for i in range(3)]
    gas = [gas_ref[i] for i in range(3)]
    slip = [g - u for g, u in zip(gas, vel)]
    slip_sq = slip[0] * slip[0] + slip[1] * slip[1] + slip[2] * slip[2]
    new_vel = [(u * diam + STEP_SIZE * g) / (diam + STEP_SIZE) for u, g in zip(vel, gas)]
    new_diam = diam / (1.0 + STEP_SIZE * EVAP_RATE * (1.0 + slip_sq))
    sources = [(diam - new_diam) * COUPLING] + [
        -(diam * (v - u)) * COUPLING for v, u in zip(new_vel, vel)
    ]
    state = [jnp.where(alive, s, 0.0) for s in new_vel + [new_diam]]
    return state, [jnp.where(alive, s, 0.0) for s in sources]


def pick(rows, first, spans, mask, gas_ref):
    for f, (start, stop) in enumerate(spans):
        found = jnp.sum(jnp.where(mask, rows[start:stop], 0.0), axis=0, keepdims=True)
        for i in range(4):
            gas_ref[f, first + i : first + i + 1, :] = found[:, i * BLK : (i + 1) * BLK]


def parcels_body(
    odd_ref, count_ref, move_ref, q_ref, parcel_ref, cells_ref,
    src_out, stay_out, first_out, second_out, gas_ref, state_ref, leave_ref,
):
    parts = [[], []]
    for f in range(3):
        high, low = halves(q_ref[f + 1].reshape(ROWS, CR).T)
        parts[0].append(high)
        parts[1].append(low)
    parts = [jnp.concatenate(part, axis=0) for part in parts]
    spans = [(f * CR, (f + 1) * CR) for f in range(3)]
    for first in range(0, BLK_DEV, 4):
        hot, lanes = one_hot_rows(cells_ref, first, 4)
        rows = sum(jnp.dot(part, hot, preferred_element_type=F32) for part in parts)
        pick(rows, first, spans, iota((CR, 4 * BLK), 0) == lanes, gas_ref)
    state, sources = step(count_ref, parcel_ref, gas_ref)
    for i in range(4):
        src_out[i] = sources[i]
        state_ref[i] = state[i]
    leave_ref[...] = jnp.zeros_like(leave_ref)

    def place(block, ranks):
        up, down = ranks
        move = move_ref[block]
        row = state_ref[:, pl.ds(block, 1), :]
        stay_out[:, pl.ds(block, 1), :] = jnp.where(move == 0, row, 0.0)

        @pl.when(move == 1)
        def _():
            leave_ref[0, :, pl.ds(jnp.minimum(up, MOVEB - 1), 1), :] = row

        @pl.when(move == -1)
        def _():
            leave_ref[1, :, pl.ds(jnp.minimum(down, MOVEB - 1), 1), :] = row

        return up + (move == 1).astype(jnp.int32), down + (move == -1).astype(jnp.int32)

    lax.fori_loop(0, BLK_DEV, place, (jnp.int32(0), jnp.int32(0)))
    odd = odd_ref[0] == 1
    up, down = leave_ref[0], leave_ref[1]
    first_out[...] = jnp.where(odd, down, up)
    second_out[...] = jnp.where(odd, up, down)


SOURCE_OF = (0, 1, 2, 3, 0)


BAND = 24
SHARE = 2 * FIELDS * CAX // N_AZ


def turned(parts):
    lane = iota((2 * CAZ, CR), 1)
    packed = jnp.zeros((2 * CAZ, CR), F32)
    for f, part in enumerate(parts):
        moved = pltpu.roll(part, f * BAND, 1) if f else part
        packed = jnp.where((lane >= f * BAND) & (lane < (f + 1) * BAND), moved, packed)
    return packed.T


def near_parcels_body(count_ref, q_ref, parcel_ref, cells_ref, tiles_out, near_out, gas_ref, hot_ref, spread_ref):
    for p in range(PAIRS):
        tiles_out[:, p * 2 * CAZ : (p + 1) * 2 * CAZ] = turned(
            [q_ref[f, 2 * p : 2 * p + 2].reshape(2 * CAZ, CR) for f in range(FIELDS)]
        )
    start = 16
    high, low = halves(tiles_out[start : 4 * BAND])
    spans = [((f + 1) * BAND - start, (f + 1) * BAND - start + CYCLES) for f in range(3)]
    for first in range(0, BLK_DEV, 4):
        hot, lanes = one_hot_rows(cells_ref, first, 4)
        hot_ref[:, first * BLK : (first + 4) * BLK] = hot
        rows = jnp.dot(high, hot, preferred_element_type=F32) + jnp.dot(low, hot, preferred_element_type=F32)
        pick(rows, first, spans, iota((CYCLES, 4 * BLK), 0) == lanes, gas_ref)
    _, sources = step(count_ref, parcel_ref, gas_ref)
    rows = [s.astype(BF16).astype(F32) for s in sources]
    rows = rows + [s - r for s, r in zip(sources, rows)]
    for block in range(BLK_DEV):
        mask = iota((CYCLES, BLK), 0) == (cells_ref[block : block + 1, :] & (CR - 1))
        for i, row in enumerate(rows):
            spread_ref[i * CYCLES : (i + 1) * CYCLES, block * BLK : (block + 1) * BLK] = jnp.where(
                mask, row[block : block + 1, :], 0.0
            ).astype(BF16)
    total = lax.dot_general(spread_ref[...], hot_ref[...], NT, preferred_element_type=F32)
    near_out[...] = total[: 4 * CYCLES] + total[4 * CYCLES :]


def near_body(
    rad_ref, odd_ref, coef_ref, q_ref, first_ref, second_ref, tiles_ref, near_ref,
    send_out, rad_out, az_ref,
):
    lane = iota((CR, 2 * CAZ), 1)
    z = lane % CAZ
    tiles = [tiles_ref[:, p * 2 * CAZ : (p + 1) * 2 * CAZ] for p in range(PAIRS)]
    odd = odd_ref[0] == 1
    first, second = first_ref[...], second_ref[...]
    before, after = jnp.where(odd, first, second), jnp.where(odd, second, first)
    halo = turned([jnp.concatenate([before[f], after[f]], axis=0) for f in range(FIELDS)])

    column = iota((CR, 1), 0)
    radius = column
    c = [jnp.zeros((CR, 1), F32) for _ in range(6)]
    for f in range(FIELDS):
        here = (column >= f * BAND) & (column < (f + 1) * BAND)
        radius = jnp.where(here, column - f * BAND, radius)
        c = [jnp.where(here, coef_ref[f, i], c[i]) for i in range(6)]
    metric = 4.0 / (radius.astype(F32) + 4.0)
    mid = (1.0 - c[1] - c[5]) - c[3] * metric
    az_up, az_down = (0.5 * (c[2] + c[3])) * metric, (0.5 * (c[3] - c[2])) * metric
    ax_up, ax_down = 0.5 * (c[0] + c[1]), 0.5 * (c[1] - c[0])
    rad_up = 0.5 * (c[4] + c[5])
    rad_down = jnp.where(radius == 0, 0.0, 0.5 * (c[5] - c[4]))
    low = lane < CAZ
    swapped = [pltpu.roll(t, CAZ, 1) for t in tiles]
    for p in range(PAIRS):
        q = tiles[p]
        ahead = jnp.where(low, swapped[p], swapped[p + 1] if p + 1 < PAIRS else halo)
        behind = jnp.where(low, swapped[p - 1] if p else halo, swapped[p])
        az_a = jnp.where(z == CAZ - 1, 0.0, pltpu.roll(q, 2 * CAZ - 1, 1))
        az_b = jnp.where(z == 0, 0.0, pltpu.roll(q, 1, 1))
        r_a = pltpu.roll(q, CR - 1, 0)
        r_b = pltpu.roll(q, 1, 0)
        out = (
            mid * q + ax_up * ahead + ax_down * behind + az_up * az_a + az_down * az_b
            + rad_up * r_a + rad_down * r_b
        )
        ends = jnp.where(z == 0, az_up * q, jnp.where(z == CAZ - 1, az_down * q, 0.0))
        ends = sum(
            pltpu.roll(ends[f * BAND : f * BAND + CYCLES], 2 * f, 1) if f else ends[:CYCLES]
            for f in range(FIELDS)
        )
        for f in range(FIELDS):
            s = SOURCE_OF[f] * CYCLES
            block = out[f * BAND : f * BAND + CYCLES] + near_ref[
                s : s + CYCLES, p * 2 * CAZ : (p + 1) * 2 * CAZ
            ]
            for quad in range(QUADS):
                send_out[p * QUADS + quad, f * 4 : f * 4 + 4, :] = block[quad * 4 : quad * 4 + 4]
        for quad in range(QUADS):
            send_out[p * QUADS + quad, LINES : LINES + 4, :] = ends[quad * 4 : quad * 4 + 4]
    for f in range(FIELDS):
        az_ref[f * CAX : (f + 1) * CAX] = q_ref[f, :, 0, :]
        az_ref[(FIELDS + f) * CAX : (FIELDS + f + 1) * CAX] = q_ref[f, :, CAZ - 1, :]
    for owner in range(N_AZ):
        send_out[owner, LINES + 4 :, :] = az_ref[owner * SHARE : (owner + 1) * SHARE]
    rad_edges(rad_ref[0], q_ref, rad_out)


def rad_edges(rad, q_ref, rad_out):
    extra = jnp.where(rad == 0, 1, 0)
    lane = iota((32, CR), 1)
    packed = jnp.zeros((32, CR), F32)
    for f in range(FIELDS):
        for g in range(16):
            part = q_ref[f, g // 2, (g % 2) * 32 : (g % 2) * 32 + 32, :]
            spot = g * 8 + f
            packed = jnp.where(lane == spot, pltpu.roll(part, spot + extra, 1), packed)
    rad_out[...] = packed


def gas_body(
    rad_ref, odd_ref, coef_ref, q_ref, first_ref, second_ref, rad_in, src_ref, cells_ref, _, sect_out, acc_ref
):
    width = 8
    for first in range(0, BLK_DEV, width):
        hot, lanes = one_hot_rows(cells_ref, first, width)
        mask = iota((CR, width * BLK), 0) == lanes
        spread = [[], []]
        for i in range(4):
            row = jnp.concatenate([src_ref[i, first + j : first + j + 1, :] for j in range(width)], axis=1)
            high = row.astype(BF16).astype(F32)
            spread[0].append(jnp.where(mask, high, 0.0).astype(BF16))
            spread[1].append(jnp.where(mask, row - high, 0.0).astype(BF16))
        total = sum(
            lax.dot_general(hot, jnp.concatenate(part, axis=0), NT, preferred_element_type=F32)
            for part in spread
        )
        if first == 0:
            acc_ref[...] = total
        else:
            acc_ref[...] += total
    rad = rad_ref[0]
    odd = odd_ref[0] == 1
    row = iota((CAZ, CR), 0)
    lane = iota((1, CR), 1)
    metric = 4.0 / ((rad * CR + lane).astype(F32) + 4.0)
    target = jnp.where(rad == 0, CR - 1, 0)
    for f in range(FIELDS):
        c = [coef_ref[f, i] for i in range(6)]
        mid = (1.0 - c[1] - c[5]) - c[3] * metric
        az_up = jnp.where(row == CAZ - 1, 0.0, (0.5 * (c[2] + c[3])) * metric)
        az_down = jnp.where(row == 0, 0.0, (0.5 * (c[3] - c[2])) * metric)
        ax_up, ax_down = 0.5 * (c[0] + c[1]), 0.5 * (c[1] - c[0])
        rad_up = jnp.where(lane == CR - 1, 0.0, 0.5 * (c[4] + c[5]))
        rad_down = jnp.where(lane == 0, 0.0, 0.5 * (c[5] - c[4]))
        across = 0.5 * jnp.where(rad == 0, c[4] + c[5], c[5] - c[4])
        across = jnp.where(lane == target, across, 0.0)
        s = SOURCE_OF[f] * CR
        for a in range(CAX):
            q = q_ref[f, a]
            ahead = q_ref[f, a + 1] if a + 1 < CAX else jnp.where(odd, second_ref[f], first_ref[f])
            behind = q_ref[f, a - 1] if a else jnp.where(odd, first_ref[f], second_ref[f])
            edge = jnp.concatenate(
                [pltpu.roll(rad_in[...], (target + (2 * CR - ((2 * a + h) * 8 + f))) % CR, 1) for h in range(2)],
                axis=0,
            )
            sect_out[f, a] = (
                mid * q + ax_up * ahead + ax_down * behind
                + az_up * pltpu.roll(q, CAZ - 1, 0) + az_down * pltpu.roll(q, 1, 0)
                + rad_up * pltpu.roll(q, CR - 1, 1) + rad_down * pltpu.roll(q, 1, 1)
                + across * edge
                + acc_ref[a * CAZ : (a + 1) * CAZ, s : s + CR]
            )


def lined(pieces, line_ref):
    low = iota((LINES, 2 * CAZ), 1) < CAZ
    for i in range(N_AZ // 2):
        t0, t1 = pieces(2 * i), pieces(2 * i + 1)
        cols = slice(i * 2 * CAZ, (i + 1) * 2 * CAZ)
        line_ref[0:LINES, cols] = jnp.where(low, t0, pltpu.roll(t1, CAZ, 1))
        line_ref[BAND : BAND + LINES, cols] = jnp.where(low, pltpu.roll(t0, CAZ, 1), t1)


def filter_body(
    az_ref, width_ref, basis_ref, got_ref, first_ref, second_ref,
    send_out, first_out, second_out, line_ref, ends_ref, piece_ref,
):
    first_out[...] = first_ref[...]
    second_out[...] = second_ref[...]
    for home in range(N_AZ):
        send_out[home, LINES:, :] = jnp.where(
            az_ref[0] < N_AZ // 2,
            got_ref[(home + 1) % N_AZ, LINES + 4 :, :],
            got_ref[(home - 1) % N_AZ, LINES + 4 :, :],
        )
    quad = az_ref[0] % QUADS
    low = iota((LINES, 2 * CAZ), 1) < CAZ
    line_ref[...] = jnp.zeros_like(line_ref)
    ends_ref[...] = jnp.zeros_like(ends_ref)
    for s in range(N_AZ):
        packed = got_ref[s, LINES : LINES + 4, :]
        for f in range(FIELDS):
            piece_ref[s, f * 4 : f * 4 + 4, :] = pltpu.roll(packed, 2 * CAZ - 2 * f, 1) if f else packed
    lined(lambda s: got_ref[s, 0:LINES, :], line_ref)
    lined(lambda s: piece_ref[s], ends_ref)
    z = iota((2 * BAND, NAZ), 1) % CAZ
    ends = ends_ref[...]
    lines = (
        line_ref[...]
        + jnp.where(z == CAZ - 1, pltpu.roll(ends, NAZ - 1, 1), 0.0)
        + jnp.where(z == 0, pltpu.roll(ends, 1, 1), 0.0)
    )
    rows = 2 * BAND
    high, rest = halves(lines)
    both = jnp.concatenate([high, rest], axis=0)
    whole = lax.dot_general(both, basis_ref[:MODES], NT, preferred_element_type=F32)
    part = lax.dot_general(high, basis_ref[MODES:], NT, preferred_element_type=F32)
    coefs = whole[:rows] + whole[rows:] + part
    column = iota((rows, MODES), 1)
    cycle = iota((rows, MODES), 0) % 4
    mode = jnp.where(column < HALF, column, column - HALF + 1)
    width = jnp.zeros((rows, MODES), jnp.int32)
    for i in range(4):
        width = jnp.where(cycle == i, width_ref[quad * 4 + i], width)
    weight = jnp.where(mode == 0, 1.0 / NAZ, 2.0 / NAZ)
    coefs = coefs * jnp.where(mode < width, weight, 0.0)
    high, rest = halves(coefs)
    both = jnp.concatenate([high, rest], axis=0)
    whole = jnp.dot(both, basis_ref[:MODES], preferred_element_type=F32)
    part = jnp.dot(high, basis_ref[MODES:], preferred_element_type=F32)
    line_ref[...] = whole[:rows] + whole[rows:] + part
    for i in range(N_AZ // 2):
        cols = slice(i * 2 * CAZ, (i + 1) * 2 * CAZ)
        t0, t1 = line_ref[0:LINES, cols], line_ref[BAND : BAND + LINES, cols]
        send_out[2 * i, 0:LINES] = jnp.where(low, t0, pltpu.roll(t1, CAZ, 1))
        send_out[2 * i + 1, 0:LINES] = jnp.where(low, pltpu.roll(t0, CAZ, 1), t1)


def merge_body(
    rad_ref, odd_ref, coef_ref, sect_ref, got_ref, stay_ref, first_ref, second_ref,
    gas_out, parcels_out, flip_ref, az_ref,
):
    near = (iota((2 * CAZ, CR), 1) < CYCLES) & (rad_ref[0] == 0)
    flip_ref[...] = jnp.zeros_like(flip_ref)
    for owner in range(N_AZ):
        az_ref[owner * SHARE : (owner + 1) * SHARE] = got_ref[owner, LINES:, :]
    for pair in range(PAIRS):
        for f in range(FIELDS):
            for quad in range(QUADS):
                first = f * CYCLES + quad * 4
                flip_ref[first : first + 4, :] = got_ref[pair * QUADS + quad, f * 4 : f * 4 + 4, :]
        turned = flip_ref[...].T
        for f in range(FIELDS):
            moved = pltpu.roll(turned, (CR - f * CYCLES) % CR, 1) if f else turned
            kept = sect_ref[f, 2 * pair : 2 * pair + 2].reshape(2 * CAZ, CR)
            gas_out[f, 2 * pair : 2 * pair + 2] = jnp.where(near, moved, kept).reshape(2, CAZ, CR)
    lane = iota((1, CR), 1)
    metric = 4.0 / ((rad_ref[0] * CR + lane).astype(F32) + 4.0)
    metric = jnp.where((lane < CYCLES) & (rad_ref[0] == 0), 0.0, metric)
    for f in range(FIELDS):
        az_up = (0.5 * (coef_ref[f, 2] + coef_ref[f, 3])) * metric
        az_down = (0.5 * (coef_ref[f, 3] - coef_ref[f, 2])) * metric
        after = az_up * az_ref[f * CAX : (f + 1) * CAX]
        before = az_down * az_ref[(FIELDS + f) * CAX : (FIELDS + f + 1) * CAX]
        for a in range(CAX):
            gas_out[f, a, 0:1] += before[a : a + 1]
            gas_out[f, a, CAZ - 1 : CAZ] += after[a : a + 1]
    odd = odd_ref[0] == 1
    parcels_out[:, 0:BLK_DEV, :] = stay_ref[...]
    first, second = first_ref[...], second_ref[...]
    parcels_out[:, BLK_DEV : BLK_DEV + MOVEB, :] = jnp.where(odd, first, second)
    parcels_out[:, BLK_DEV + MOVEB :, :] = jnp.where(odd, second, first)


def shards(fields, coeffs, parcels, cells, counts, moves, widths):
    rad_index = lax.axis_index("rad").astype(jnp.int32).reshape(1)
    az_index = lax.axis_index("az").astype(jnp.int32).reshape(1)
    odd = (lax.axis_index("ax").astype(jnp.int32) % 2).reshape(1)
    n_ax, n_rad = lax.axis_size("ax"), lax.axis_size("rad")
    parcels = parcels.reshape(4, BLK_DEV, BLK)
    cells = cells.reshape(BLK_DEV, BLK)
    counts = counts.reshape(1)
    moves = moves.reshape(BLK_DEV)
    inner = [(i, i ^ 1) for i in range(n_ax)]
    outer = [(i, ((i + 1) ^ 1) - 1) for i in range(1, n_ax - 1)]
    across = [(i, i ^ 1) for i in range(n_rad)]
    gas_shape = (FIELDS, CAX, CAZ, CR)

    first, second = call(
        edges_body, [(FIELDS, CAZ, CR)] * 2, [SMEM, HBM], 10**6, 10**6,
        [pltpu.SemaphoreType.DMA((2,))], mib=62,
    )(odd, fields)
    first = lax.ppermute(first, "ax", inner)
    second = lax.ppermute(second, "ax", outer)

    tiles, near = call(
        near_parcels_body,
        [(CR, ROWS), (4 * CYCLES, ROWS)],
        [SMEM] + [VMEM] * 3, 3 * 10**9, 2 * 10**6,
        [
            pltpu.VMEM((3, BLK_DEV, BLK), F32),
            pltpu.VMEM((ROWS, PARCELS), BF16),
            pltpu.VMEM((8 * CYCLES, PARCELS), BF16),
        ],
        mib=16,
    )(counts, fields, parcels, cells)

    to_owner, rad_edge = call(
        near_body,
        [(N_AZ, LINES + 4 + SHARE, 2 * CAZ), (32, CR)],
        [SMEM, SMEM, SMEM] + [VMEM] * 5, 10**7, 4 * 10**6,
        [pltpu.VMEM((2 * FIELDS * CAX, CR), F32)],
        mib=8,
    )(rad_index, odd, coeffs, fields, first, second, tiles, near)
    lines = lax.all_to_all(to_owner, "az", 0, 0, tiled=True)
    rad_got = lax.ppermute(rad_edge, "rad", across)

    src, stay, first_moved, second_moved = call(
        parcels_body,
        [(4, BLK_DEV, BLK), (4, BLK_DEV, BLK), (4, MOVEB, BLK), (4, MOVEB, BLK)],
        [SMEM, SMEM, SMEM] + [VMEM] * 3 , 6 * 10**9, 2 * 10**6,
        [
            pltpu.VMEM((3, BLK_DEV, BLK), F32),
            pltpu.VMEM((4, BLK_DEV, BLK), F32),
            pltpu.VMEM((2, 4, MOVEB, BLK), F32),
        ],
        mib=16,
    )(odd, counts, moves, fields, parcels, cells)

    to_home, first_moved, second_moved = call(
        filter_body,
        [(N_AZ, LINES + SHARE, 2 * CAZ), (4, MOVEB, BLK), (4, MOVEB, BLK)],
        [SMEM, SMEM] + [VMEM] * 4, 10**8, 10**6,
        [
            pltpu.VMEM((2 * BAND, NAZ), F32),
            pltpu.VMEM((2 * BAND, NAZ), F32),
            pltpu.VMEM((N_AZ, LINES, 2 * CAZ), F32),
        ],
        mib=6,
    )(az_index, widths, jnp.asarray(basis_rows()), lines, first_moved, second_moved)
    filtered = lax.all_to_all(to_home, "az", 0, 0, tiled=True)
    first_moved = lax.ppermute(first_moved, "ax", inner)
    second_moved = lax.ppermute(second_moved, "ax", outer)

    (sect,) = call(
        gas_body, [gas_shape], [SMEM, SMEM, SMEM] + [VMEM] * 6 + [ANY], 8 * 10**9, 4 * 10**6,
        [pltpu.VMEM((ROWS, 4 * CR), F32)],
        mib=16,
    )(rad_index, odd, coeffs, fields, first, second, rad_got, src, cells, to_home)

    gas_out, parcels_out = call(
        merge_body,
        [gas_shape, (4, BLK_DEV + 2 * MOVEB, BLK)],
        [SMEM, SMEM, SMEM] + [VMEM] * 5, 10**6, 4 * 10**6,
        [pltpu.VMEM((CR, CR), F32), pltpu.VMEM((2 * FIELDS * CAX, CR), F32)],
        mib=8,
    )(rad_index, odd, coeffs, sect, filtered, stay, first_moved, second_moved)
    return gas_out, parcels_out.reshape(4, BLK_DEV + 2 * MOVEB, 1, BLK)


def solution(mesh):
    block = P(None, "ax", "az", "rad")
    flat = P("ax", "az", "rad")
    return jax.shard_map(
        shards,
        mesh=mesh,
        in_specs=(block, P(), block, flat, flat, flat, P()),
        out_specs=(block, block),
        check_vma=False,
    )
```

```python
import math

import jax
import jax.numpy as jnp
import ml_dtypes
import numpy as np
from jax import lax
from jax.experimental import pallas as pl
from jax.experimental.pallas import tpu as pltpu
from jax.sharding import PartitionSpec as P

FIELDS = 5
CYCLES = 16
MODES = 128
HALF = MODES // 2
BLK = 128
BLK_DEV = 32
MOVEB = 4
CAX, CAZ, CR = 8, 64, 128
ROWS = CAX * CAZ
PARCELS = BLK * BLK_DEV
NAZ = 1024
N_AZ = 16
PAIRS = CAX // 2
QUADS = CYCLES // 4
LINES = FIELDS * 4

STEP_SIZE = 0.5
EVAP_RATE = 0.5
COUPLING = 0.5

F32 = jnp.float32
BF16 = jnp.bfloat16
HIGHEST = lax.Precision.HIGHEST
VMEM = pl.BlockSpec(memory_space=pltpu.VMEM)
SMEM = pl.BlockSpec(memory_space=pltpu.SMEM)
ANY = pl.BlockSpec(memory_space=pl.ANY)
HBM = pl.BlockSpec(memory_space=pltpu.HBM)
NT = (((1,), (1,)), ((), ()))


def basis_rows():
    column = np.arange(MODES)
    mode = np.where(column < HALF, column, column - HALF + 1)
    phases = (mode[:, None] * np.arange(NAZ)[None, :]) % NAZ
    angles = phases.astype(np.float32) * np.float32(2.0 * math.pi / NAZ)
    table = np.where(column[:, None] < HALF, np.cos(angles), np.sin(angles)).astype(np.float32)
    high = table.astype(ml_dtypes.bfloat16)
    low = (table - high.astype(np.float32)).astype(ml_dtypes.bfloat16)
    return np.concatenate([high, low])


def iota(shape, axis):
    return lax.broadcasted_iota(jnp.int32, shape, axis)


def halves(value):
    high = value.astype(BF16)
    return high, (value - high.astype(F32)).astype(BF16)


def call(body, out_shape, in_specs, flops, nbytes, scratch=(), mib=24, hbm_first=False):
    return pl.pallas_call(
        body,
        out_shape=[jax.ShapeDtypeStruct(shape, F32) for shape in out_shape],
        in_specs=in_specs,
        out_specs=[HBM if hbm_first and i == 0 else VMEM for i in range(len(out_shape))],
        scratch_shapes=list(scratch),
        compiler_params=pltpu.CompilerParams(vmem_limit_bytes=mib * 2**20),
        cost_estimate=pl.CostEstimate(flops=flops, bytes_accessed=nbytes, transcendentals=0),
    )


def edges_body(odd_ref, q_ref, first_out, second_out):
    odd = odd_ref[0] == 1
    low, high = q_ref[:, 0], q_ref[:, CAX - 1]
    first_out[...] = jnp.where(odd, low, high)
    second_out[...] = jnp.where(odd, high, low)


def one_hot_rows(cells_ref, first, blocks):
    cells = jnp.concatenate([cells_ref[first + i : first + i + 1, :] for i in range(blocks)], axis=1)
    width = blocks * BLK
    hit = iota((ROWS, width), 0) == (cells >> 7)
    return jnp.where(hit, 1.0, 0.0).astype(BF16), cells & (CR - 1)


def lane_row(cells_ref, first, blocks):
    return jnp.concatenate([cells_ref[first + i : first + i + 1, :] for i in range(blocks)], axis=1) & (CR - 1)


def step(count_ref, parcel_ref, gas_ref):
    slot = iota((BLK_DEV, BLK), 0) * BLK + iota((BLK_DEV, BLK), 1)
    alive = slot < count_ref[0]
    diam = parcel_ref[3]
    vel = [parcel_ref[i] for i in range(3)]
    gas = [gas_ref[i] for i in range(3)]
    slip = [g - u for g, u in zip(gas, vel)]
    slip_sq = slip[0] * slip[0] + slip[1] * slip[1] + slip[2] * slip[2]
    new_vel = [(u * diam + STEP_SIZE * g) / (diam + STEP_SIZE) for u, g in zip(vel, gas)]
    new_diam = diam / (1.0 + STEP_SIZE * EVAP_RATE * (1.0 + slip_sq))
    sources = [(diam - new_diam) * COUPLING] + [
        -(diam * (v - u)) * COUPLING for v, u in zip(new_vel, vel)
    ]
    state = [jnp.where(alive, s, 0.0) for s in new_vel + [new_diam]]
    return state, [jnp.where(alive, s, 0.0) for s in sources]


def pick(rows, first, spans, mask, gas_ref):
    for f, (start, stop) in enumerate(spans):
        found = jnp.sum(jnp.where(mask, rows[start:stop], 0.0), axis=0, keepdims=True)
        for i in range(4):
            gas_ref[f, first + i : first + i + 1, :] = found[:, i * BLK : (i + 1) * BLK]


def parcels_body(
    rad_ref, odd_ref, count_ref, move_ref, q_ref, parcel_ref, cells_ref,
    src_out, stay_out, first_out, second_out, rad_out, gas_ref, state_ref, leave_ref,
):
    rad_edges(rad_ref[0], q_ref, rad_out)
    parts = [[], []]
    for f in range(3):
        high, low = halves(q_ref[f + 1].reshape(ROWS, CR).T)
        parts[0].append(high)
        parts[1].append(low)
    parts = [jnp.concatenate(part, axis=0) for part in parts]
    spans = [(f * CR, (f + 1) * CR) for f in range(3)]
    for first in range(0, BLK_DEV, 4):
        hot, lanes = one_hot_rows(cells_ref, first, 4)
        rows = sum(jnp.dot(part, hot, preferred_element_type=F32) for part in parts)
        pick(rows, first, spans, iota((CR, 4 * BLK), 0) == lanes, gas_ref)
    state, sources = step(count_ref, parcel_ref, gas_ref)
    for i in range(4):
        src_out[i] = sources[i]
        state_ref[i] = state[i]
    leave_ref[...] = jnp.zeros_like(leave_ref)

    def place(block, ranks):
        up, down = ranks
        move = move_ref[block]
        row = state_ref[:, pl.ds(block, 1), :]
        stay_out[:, pl.ds(block, 1), :] = jnp.where(move == 0, row, 0.0)

        @pl.when(move == 1)
        def _():
            leave_ref[0, :, pl.ds(jnp.minimum(up, MOVEB - 1), 1), :] = row

        @pl.when(move == -1)
        def _():
            leave_ref[1, :, pl.ds(jnp.minimum(down, MOVEB - 1), 1), :] = row

        return up + (move == 1).astype(jnp.int32), down + (move == -1).astype(jnp.int32)

    lax.fori_loop(0, BLK_DEV, place, (jnp.int32(0), jnp.int32(0)))
    odd = odd_ref[0] == 1
    up, down = leave_ref[0], leave_ref[1]
    first_out[...] = jnp.where(odd, down, up)
    second_out[...] = jnp.where(odd, up, down)


SOURCE_OF = (0, 1, 2, 3, 0)


BAND = 24
SHARE = 2 * FIELDS * CAX // N_AZ


def turned(parts):
    lane = iota((2 * CAZ, CR), 1)
    packed = jnp.zeros((2 * CAZ, CR), F32)
    for f, part in enumerate(parts):
        moved = pltpu.roll(part, f * BAND, 1) if f else part
        packed = jnp.where((lane >= f * BAND) & (lane < (f + 1) * BAND), moved, packed)
    return packed.T


def near_parcels_body(count_ref, q_ref, parcel_ref, cells_ref, tiles_out, near_out, gas_ref, hot_ref, spread_ref):
    for p in range(PAIRS):
        tiles_out[:, p * 2 * CAZ : (p + 1) * 2 * CAZ] = turned(
            [q_ref[f, 2 * p : 2 * p + 2].reshape(2 * CAZ, CR) for f in range(FIELDS)]
        )
    start = 16
    table = jnp.concatenate(halves(tiles_out[start : 4 * BAND]), axis=0)
    depth = 4 * BAND - start
    spans = [((f + 1) * BAND - start, (f + 1) * BAND - start + CYCLES) for f in range(3)]
    for first in range(0, BLK_DEV, 4):
        hot, lanes = one_hot_rows(cells_ref, first, 4)
        hot_ref[:, first * BLK : (first + 4) * BLK] = hot
        rows = jnp.dot(table, hot, preferred_element_type=F32)
        rows = rows[:depth] + rows[depth:]
        pick(rows, first, spans, iota((CYCLES, 4 * BLK), 0) == lanes, gas_ref)
    _, sources = step(count_ref, parcel_ref, gas_ref)
    rows = [s.astype(BF16).astype(F32) for s in sources]
    rows = rows + [s - r for s, r in zip(sources, rows)]
    for block in range(BLK_DEV):
        mask = iota((CYCLES, BLK), 0) == (cells_ref[block : block + 1, :] & (CR - 1))
        for i, row in enumerate(rows):
            spread_ref[i * CYCLES : (i + 1) * CYCLES, block * BLK : (block + 1) * BLK] = jnp.where(
                mask, row[block : block + 1, :], 0.0
            ).astype(BF16)
    total = lax.dot_general(spread_ref[...], hot_ref[...], NT, preferred_element_type=F32)
    near_out[...] = total[: 4 * CYCLES] + total[4 * CYCLES :]


def near_body(
    odd_ref, coef_ref, q_ref, first_ref, second_ref, tiles_ref, near_ref, send_hbm, az_ref, send_out, sems
):
    for f in range(FIELDS):
        az_ref[f * CAX : (f + 1) * CAX] = q_ref[f, :, 0, :]
        az_ref[(FIELDS + f) * CAX : (FIELDS + f + 1) * CAX] = q_ref[f, :, CAZ - 1, :]
    for owner in range(N_AZ):
        send_out[owner, LINES + 4 :, :] = az_ref[owner * SHARE : (owner + 1) * SHARE]
    copies = []
    lane = iota((CR, 2 * CAZ), 1)
    z = lane % CAZ
    tiles = [tiles_ref[:, p * 2 * CAZ : (p + 1) * 2 * CAZ] for p in range(PAIRS)]
    odd = odd_ref[0] == 1
    first, second = first_ref[...], second_ref[...]
    before, after = jnp.where(odd, first, second), jnp.where(odd, second, first)
    halo = turned([jnp.concatenate([before[f], after[f]], axis=0) for f in range(FIELDS)])

    column = iota((CR, 1), 0)
    radius = column
    c = [jnp.zeros((CR, 1), F32) for _ in range(6)]
    for f in range(FIELDS):
        here = (column >= f * BAND) & (column < (f + 1) * BAND)
        radius = jnp.where(here, column - f * BAND, radius)
        c = [jnp.where(here, coef_ref[f, i], c[i]) for i in range(6)]
    metric = 4.0 / (radius.astype(F32) + 4.0)
    mid = (1.0 - c[1] - c[5]) - c[3] * metric
    az_up, az_down = (0.5 * (c[2] + c[3])) * metric, (0.5 * (c[3] - c[2])) * metric
    ax_up, ax_down = 0.5 * (c[0] + c[1]), 0.5 * (c[1] - c[0])
    rad_up = 0.5 * (c[4] + c[5])
    rad_down = jnp.where(radius == 0, 0.0, 0.5 * (c[5] - c[4]))
    low = lane < CAZ
    swapped = [pltpu.roll(t, CAZ, 1) for t in tiles]
    for p in range(PAIRS):
        q = tiles[p]
        ahead = jnp.where(low, swapped[p], swapped[p + 1] if p + 1 < PAIRS else halo)
        behind = jnp.where(low, swapped[p - 1] if p else halo, swapped[p])
        az_a = jnp.where(z == CAZ - 1, 0.0, pltpu.roll(q, 2 * CAZ - 1, 1))
        az_b = jnp.where(z == 0, 0.0, pltpu.roll(q, 1, 1))
        r_a = pltpu.roll(q, CR - 1, 0)
        r_b = pltpu.roll(q, 1, 0)
        out = (
            mid * q + ax_up * ahead + ax_down * behind + az_up * az_a + az_down * az_b
            + rad_up * r_a + rad_down * r_b
        )
        ends = jnp.where(z == 0, az_up * q, jnp.where(z == CAZ - 1, az_down * q, 0.0))
        ends = sum(
            pltpu.roll(ends[f * BAND : f * BAND + CYCLES], 2 * f, 1) if f else ends[:CYCLES]
            for f in range(FIELDS)
        )
        for f in range(FIELDS):
            s = SOURCE_OF[f] * CYCLES
            block = out[f * BAND : f * BAND + CYCLES] + near_ref[
                s : s + CYCLES, p * 2 * CAZ : (p + 1) * 2 * CAZ
            ]
            for quad in range(QUADS):
                send_out[p * QUADS + quad, f * 4 : f * 4 + 4, :] = block[quad * 4 : quad * 4 + 4]
        for quad in range(QUADS):
            send_out[p * QUADS + quad, LINES : LINES + 4, :] = ends[quad * 4 : quad * 4 + 4]
        span = pl.ds(p * QUADS, QUADS)
        copies.append(pltpu.make_async_copy(send_out.at[span], send_hbm.at[span], sems.at[p]))
        copies[p].start()
    for copy in copies:
        copy.wait()


def rad_edges(rad, q_ref, rad_out):
    extra = jnp.where(rad == 0, 1, 0)
    lane = iota((32, CR), 1)
    packed = jnp.zeros((32, CR), F32)
    for f in range(FIELDS):
        for g in range(16):
            part = q_ref[f, g // 2, (g % 2) * 32 : (g % 2) * 32 + 32, :]
            spot = g * 8 + f
            packed = jnp.where(lane == spot, pltpu.roll(part, spot + extra, 1), packed)
    rad_out[...] = packed


def gas_body(
    rad_ref, odd_ref, coef_ref, q_ref, first_ref, second_ref, rad_in, src_ref, cells_ref, _, sect_out, acc_ref
):
    width = 8
    for first in range(0, BLK_DEV, width):
        hot, lanes = one_hot_rows(cells_ref, first, width)
        mask = iota((CR, width * BLK), 0) == lanes
        spread = [[], []]
        for i in range(4):
            row = jnp.concatenate([src_ref[i, first + j : first + j + 1, :] for j in range(width)], axis=1)
            high = row.astype(BF16).astype(F32)
            spread[0].append(jnp.where(mask, high, 0.0).astype(BF16))
            spread[1].append(jnp.where(mask, row - high, 0.0).astype(BF16))
        total = sum(
            lax.dot_general(hot, jnp.concatenate(part, axis=0), NT, preferred_element_type=F32)
            for part in spread
        )
        if first == 0:
            acc_ref[...] = total
        else:
            acc_ref[...] += total
    rad = rad_ref[0]
    odd = odd_ref[0] == 1
    row = iota((CAZ, CR), 0)
    lane = iota((1, CR), 1)
    metric = 4.0 / ((rad * CR + lane).astype(F32) + 4.0)
    target = jnp.where(rad == 0, CR - 1, 0)
    for f in range(FIELDS):
        c = [coef_ref[f, i] for i in range(6)]
        mid = (1.0 - c[1] - c[5]) - c[3] * metric
        az_up = jnp.where(row == CAZ - 1, 0.0, (0.5 * (c[2] + c[3])) * metric)
        az_down = jnp.where(row == 0, 0.0, (0.5 * (c[3] - c[2])) * metric)
        ax_up, ax_down = 0.5 * (c[0] + c[1]), 0.5 * (c[1] - c[0])
        rad_up = jnp.where(lane == CR - 1, 0.0, 0.5 * (c[4] + c[5]))
        rad_down = jnp.where(lane == 0, 0.0, 0.5 * (c[5] - c[4]))
        across = 0.5 * jnp.where(rad == 0, c[4] + c[5], c[5] - c[4])
        across = jnp.where(lane == target, across, 0.0)
        s = SOURCE_OF[f] * CR
        for a in range(CAX):
            q = q_ref[f, a]
            ahead = q_ref[f, a + 1] if a + 1 < CAX else jnp.where(odd, second_ref[f], first_ref[f])
            behind = q_ref[f, a - 1] if a else jnp.where(odd, first_ref[f], second_ref[f])
            edge = jnp.concatenate(
                [pltpu.roll(rad_in[...], (target + (2 * CR - ((2 * a + h) * 8 + f))) % CR, 1) for h in range(2)],
                axis=0,
            )
            sect_out[f, a] = (
                mid * q + ax_up * ahead + ax_down * behind
                + az_up * pltpu.roll(q, CAZ - 1, 0) + az_down * pltpu.roll(q, 1, 0)
                + rad_up * pltpu.roll(q, CR - 1, 1) + rad_down * pltpu.roll(q, 1, 1)
                + across * edge
                + acc_ref[a * CAZ : (a + 1) * CAZ, s : s + CR]
            )


def lined(pieces, line_ref):
    low = iota((LINES, 2 * CAZ), 1) < CAZ
    for i in range(N_AZ // 2):
        t0, t1 = pieces(2 * i), pieces(2 * i + 1)
        cols = slice(i * 2 * CAZ, (i + 1) * 2 * CAZ)
        line_ref[0:LINES, cols] = jnp.where(low, t0, pltpu.roll(t1, CAZ, 1))
        line_ref[BAND : BAND + LINES, cols] = jnp.where(low, pltpu.roll(t0, CAZ, 1), t1)


def filter_body(
    az_ref, width_ref, basis_ref, got_ref, first_ref, second_ref,
    send_hbm, first_out, second_out, line_ref, ends_ref, piece_ref, send_out, sems,
):
    first_out[...] = first_ref[...]
    second_out[...] = second_ref[...]
    for home in range(N_AZ):
        send_out[home, LINES:, :] = jnp.where(
            az_ref[0] < N_AZ // 2,
            got_ref[(home + 1) % N_AZ, LINES + 4 :, :],
            got_ref[(home - 1) % N_AZ, LINES + 4 :, :],
        )
    quad = az_ref[0] % QUADS
    low = iota((LINES, 2 * CAZ), 1) < CAZ
    line_ref[...] = jnp.zeros_like(line_ref)
    ends_ref[...] = jnp.zeros_like(ends_ref)
    for s in range(N_AZ):
        packed = got_ref[s, LINES : LINES + 4, :]
        for f in range(FIELDS):
            piece_ref[s, f * 4 : f * 4 + 4, :] = pltpu.roll(packed, 2 * CAZ - 2 * f, 1) if f else packed
    lined(lambda s: got_ref[s, 0:LINES, :], line_ref)
    lined(lambda s: piece_ref[s], ends_ref)
    z = iota((2 * BAND, NAZ), 1) % CAZ
    ends = ends_ref[...]
    lines = (
        line_ref[...]
        + jnp.where(z == CAZ - 1, pltpu.roll(ends, NAZ - 1, 1), 0.0)
        + jnp.where(z == 0, pltpu.roll(ends, 1, 1), 0.0)
    )
    rows = 2 * BAND
    high, rest = halves(lines)
    both = jnp.concatenate([high, rest], axis=0)
    whole = lax.dot_general(both, basis_ref[:MODES], NT, preferred_element_type=F32)
    part = lax.dot_general(high, basis_ref[MODES:], NT, preferred_element_type=F32)
    coefs = whole[:rows] + whole[rows:] + part
    column = iota((rows, MODES), 1)
    cycle = iota((rows, MODES), 0) % 4
    mode = jnp.where(column < HALF, column, column - HALF + 1)
    width = jnp.zeros((rows, MODES), jnp.int32)
    for i in range(4):
        width = jnp.where(cycle == i, width_ref[quad * 4 + i], width)
    weight = jnp.where(mode == 0, 1.0 / NAZ, 2.0 / NAZ)
    coefs = coefs * jnp.where(mode < width, weight, 0.0)
    high, rest = halves(coefs)
    both = jnp.concatenate([high, rest], axis=0)
    whole = jnp.dot(both, basis_ref[:MODES], preferred_element_type=F32)
    part = jnp.dot(high, basis_ref[MODES:], preferred_element_type=F32)
    line_ref[...] = whole[:rows] + whole[rows:] + part
    copies = []
    for i in range(N_AZ // 2):
        cols = slice(i * 2 * CAZ, (i + 1) * 2 * CAZ)
        t0, t1 = line_ref[0:LINES, cols], line_ref[BAND : BAND + LINES, cols]
        send_out[2 * i, 0:LINES] = jnp.where(low, t0, pltpu.roll(t1, CAZ, 1))
        send_out[2 * i + 1, 0:LINES] = jnp.where(low, pltpu.roll(t0, CAZ, 1), t1)
        if i % 2:
            span = pl.ds(2 * i - 2, 4)
            copies.append(pltpu.make_async_copy(send_out.at[span], send_hbm.at[span], sems.at[i // 2]))
            copies[-1].start()
    for copy in copies:
        copy.wait()


def merge_body(
    rad_ref, odd_ref, coef_ref, sect_ref, got_ref, stay_ref, first_ref, second_ref,
    gas_hbm, parcels_out, flip_ref, az_ref, gas_out, sems,
):
    odd = odd_ref[0] == 1
    parcels_out[:, 0:BLK_DEV, :] = stay_ref[...]
    first, second = first_ref[...], second_ref[...]
    parcels_out[:, BLK_DEV : BLK_DEV + MOVEB, :] = jnp.where(odd, first, second)
    parcels_out[:, BLK_DEV + MOVEB :, :] = jnp.where(odd, second, first)
    near = (iota((2 * CAZ, CR), 1) < CYCLES) & (rad_ref[0] == 0)
    for owner in range(N_AZ):
        az_ref[owner * SHARE : (owner + 1) * SHARE] = got_ref[owner, LINES:, :]
    tiles = []
    for pair in range(PAIRS):
        flip_ref[pair, FIELDS * CYCLES :, :] = jnp.zeros((CR - FIELDS * CYCLES, CR), F32)
        for f in range(FIELDS):
            for quad in range(QUADS):
                first = f * CYCLES + quad * 4
                flip_ref[pair, first : first + 4, :] = got_ref[pair * QUADS + quad, f * 4 : f * 4 + 4, :]
        tiles.append(flip_ref[pair].T)
    lane = iota((1, CR), 1)
    metric = 4.0 / ((rad_ref[0] * CR + lane).astype(F32) + 4.0)
    metric = jnp.where((lane < CYCLES) & (rad_ref[0] == 0), 0.0, metric)
    copies = []
    for f in range(FIELDS):
        for pair in range(PAIRS):
            moved = pltpu.roll(tiles[pair], CR - f * CYCLES, 1) if f else tiles[pair]
            kept = sect_ref[f, 2 * pair : 2 * pair + 2].reshape(2 * CAZ, CR)
            gas_out[f, 2 * pair : 2 * pair + 2] = jnp.where(near, moved, kept).reshape(2, CAZ, CR)
        az_up = (0.5 * (coef_ref[f, 2] + coef_ref[f, 3])) * metric
        az_down = (0.5 * (coef_ref[f, 3] - coef_ref[f, 2])) * metric
        after = az_up * az_ref[f * CAX : (f + 1) * CAX]
        before = az_down * az_ref[(FIELDS + f) * CAX : (FIELDS + f + 1) * CAX]
        for a in range(CAX):
            gas_out[f, a, 0:1] += before[a : a + 1]
            gas_out[f, a, CAZ - 1 : CAZ] += after[a : a + 1]
        copies.append(pltpu.make_async_copy(gas_out.at[f], gas_hbm.at[f], sems.at[f]))
        copies[f].start()
    for copy in copies:
        copy.wait()


def shards(fields, coeffs, parcels, cells, counts, moves, widths):
    rad_index = lax.axis_index("rad").astype(jnp.int32).reshape(1)
    az_index = lax.axis_index("az").astype(jnp.int32).reshape(1)
    odd = (lax.axis_index("ax").astype(jnp.int32) % 2).reshape(1)
    n_ax, n_rad = lax.axis_size("ax"), lax.axis_size("rad")
    parcels = parcels.reshape(4, BLK_DEV, BLK)
    cells = cells.reshape(BLK_DEV, BLK)
    counts = counts.reshape(1)
    moves = moves.reshape(BLK_DEV)
    inner = [(i, i ^ 1) for i in range(n_ax)]
    outer = [(i, ((i + 1) ^ 1) - 1) for i in range(1, n_ax - 1)]
    across = [(i, i ^ 1) for i in range(n_rad)]
    gas_shape = (FIELDS, CAX, CAZ, CR)

    first, second = call(
        edges_body, [(FIELDS, CAZ, CR)] * 2, [SMEM, VMEM], 10**6, 10**6, mib=4
    )(odd, fields)
    first = lax.ppermute(first, "ax", inner)
    second = lax.ppermute(second, "ax", outer)

    tiles, near = call(
        near_parcels_body,
        [(CR, ROWS), (4 * CYCLES, ROWS)],
        [SMEM] + [VMEM] * 3, 3 * 10**9, 2 * 10**6,
        [
            pltpu.VMEM((3, BLK_DEV, BLK), F32),
            pltpu.VMEM((ROWS, PARCELS), BF16),
            pltpu.VMEM((8 * CYCLES, PARCELS), BF16),
        ],
        mib=16,
    )(counts, fields, parcels, cells)

    (to_owner,) = call(
        near_body,
        [(N_AZ, LINES + 4 + SHARE, 2 * CAZ)],
        [SMEM, SMEM] + [VMEM] * 5, 10**7, 4 * 10**6,
        [
            pltpu.VMEM((2 * FIELDS * CAX, CR), F32),
            pltpu.VMEM((N_AZ, LINES + 4 + SHARE, 2 * CAZ), F32),
            pltpu.SemaphoreType.DMA((PAIRS,)),
        ],
        mib=8,
        hbm_first=True,
    )(odd, coeffs, fields, first, second, tiles, near)
    lines = lax.all_to_all(to_owner, "az", 0, 0, tiled=True)

    src, stay, first_moved, second_moved, rad_edge = call(
        parcels_body,
        [(4, BLK_DEV, BLK), (4, BLK_DEV, BLK), (4, MOVEB, BLK), (4, MOVEB, BLK), (32, CR)],
        [SMEM] * 4 + [VMEM] * 3, 6 * 10**9, 2 * 10**6,
        [
            pltpu.VMEM((3, BLK_DEV, BLK), F32),
            pltpu.VMEM((4, BLK_DEV, BLK), F32),
            pltpu.VMEM((2, 4, MOVEB, BLK), F32),
        ],
        mib=16,
    )(rad_index, odd, counts, moves, fields, parcels, cells)
    rad_got = lax.ppermute(rad_edge, "rad", across)

    to_home, first_moved, second_moved = call(
        filter_body,
        [(N_AZ, LINES + SHARE, 2 * CAZ), (4, MOVEB, BLK), (4, MOVEB, BLK)],
        [SMEM, SMEM] + [VMEM] * 4, 10**8, 10**6,
        [
            pltpu.VMEM((2 * BAND, NAZ), F32),
            pltpu.VMEM((2 * BAND, NAZ), F32),
            pltpu.VMEM((N_AZ, LINES, 2 * CAZ), F32),
            pltpu.VMEM((N_AZ, LINES + SHARE, 2 * CAZ), F32),
            pltpu.SemaphoreType.DMA((4,)),
        ],
        mib=6,
        hbm_first=True,
    )(az_index, widths, jnp.asarray(basis_rows()), lines, first_moved, second_moved)
    filtered = lax.all_to_all(to_home, "az", 0, 0, tiled=True)
    first_moved = lax.ppermute(first_moved, "ax", inner)
    second_moved = lax.ppermute(second_moved, "ax", outer)

    (sect,) = call(
        gas_body, [gas_shape], [SMEM, SMEM, SMEM] + [VMEM] * 6 + [ANY], 8 * 10**9, 4 * 10**6,
        [pltpu.VMEM((ROWS, 4 * CR), F32)],
        mib=16,
    )(rad_index, odd, coeffs, fields, first, second, rad_got, src, cells, to_home)

    gas_out, parcels_out = call(
        merge_body,
        [gas_shape, (4, BLK_DEV + 2 * MOVEB, BLK)],
        [SMEM, SMEM, SMEM] + [VMEM] * 5, 10**6, 4 * 10**6,
        [
            pltpu.VMEM((PAIRS, CR, CR), F32),
            pltpu.VMEM((2 * FIELDS * CAX, CR), F32),
            pltpu.VMEM(gas_shape, F32),
            pltpu.SemaphoreType.DMA((FIELDS,)),
        ],
        mib=8,
        hbm_first=True,
    )(rad_index, odd, coeffs, sect, filtered, stay, first_moved, second_moved)
    return gas_out, parcels_out.reshape(4, BLK_DEV + 2 * MOVEB, 1, BLK)


def solution(mesh):
    block = P(None, "ax", "az", "rad")
    flat = P("ax", "az", "rad")
    return jax.shard_map(
        shards,
        mesh=mesh,
        in_specs=(block, P(), block, flat, flat, flat, P()),
        out_specs=(block, block),
        check_vma=False,
    )
```

```python
import math

import jax
import jax.numpy as jnp
import ml_dtypes
import numpy as np
from jax import lax
from jax.experimental import pallas as pl
from jax.experimental.pallas import tpu as pltpu
from jax.sharding import PartitionSpec as P

FIELDS = 5
CYCLES = 16
MODES = 128
HALF = MODES // 2
BLK = 128
BLK_DEV = 32
MOVEB = 4
CAX, CAZ, CR = 8, 64, 128
ROWS = CAX * CAZ
PARCELS = BLK * BLK_DEV
NAZ = 1024
N_AZ = 16
PAIRS = CAX // 2
QUADS = CYCLES // 4
LINES = FIELDS * 4

STEP_SIZE = 0.5
EVAP_RATE = 0.5
COUPLING = 0.5

F32 = jnp.float32
BF16 = jnp.bfloat16
HIGHEST = lax.Precision.HIGHEST
VMEM = pl.BlockSpec(memory_space=pltpu.VMEM)
SMEM = pl.BlockSpec(memory_space=pltpu.SMEM)
ANY = pl.BlockSpec(memory_space=pl.ANY)
HBM = pl.BlockSpec(memory_space=pltpu.HBM)
NT = (((1,), (1,)), ((), ()))


def basis_parts():
    column = np.arange(MODES)
    mode = np.where(column < HALF, column, column - HALF + 1)
    phases = (mode[:, None] * np.arange(NAZ)[None, :]) % NAZ
    angles = phases.astype(np.float32) * np.float32(2.0 * math.pi / NAZ)
    table = np.where(column[:, None] < HALF, np.cos(angles), np.sin(angles)).astype(np.float32)
    high = table.astype(ml_dtypes.bfloat16)
    low = (table - high.astype(np.float32)).astype(ml_dtypes.bfloat16)
    parts = np.concatenate([high, low])
    return jnp.asarray(parts), jnp.asarray(np.ascontiguousarray(parts.T))


def iota(shape, axis):
    return lax.broadcasted_iota(jnp.int32, shape, axis)


def halves(value):
    high = value.astype(BF16)
    return high, (value - high.astype(F32)).astype(BF16)


def call(body, out_shape, in_specs, flops, nbytes, scratch=(), mib=24, hbm_first=False):
    return pl.pallas_call(
        body,
        out_shape=[jax.ShapeDtypeStruct(shape, F32) for shape in out_shape],
        in_specs=in_specs,
        out_specs=[HBM if hbm_first and i == 0 else VMEM for i in range(len(out_shape))],
        scratch_shapes=list(scratch),
        compiler_params=pltpu.CompilerParams(vmem_limit_bytes=mib * 2**20),
        cost_estimate=pl.CostEstimate(flops=flops, bytes_accessed=nbytes, transcendentals=0),
    )


def edges_body(odd_ref, q_ref, first_out, second_out):
    odd = odd_ref[0] == 1
    low, high = q_ref[:, 0], q_ref[:, CAX - 1]
    first_out[...] = jnp.where(odd, low, high)
    second_out[...] = jnp.where(odd, high, low)


def one_hot_rows(cells_ref, first, blocks):
    cells = jnp.concatenate([cells_ref[first + i : first + i + 1, :] for i in range(blocks)], axis=1)
    width = blocks * BLK
    hit = iota((ROWS, width), 0) == (cells >> 7)
    return jnp.where(hit, 1.0, 0.0).astype(BF16), cells & (CR - 1)


def lane_row(cells_ref, first, blocks):
    return jnp.concatenate([cells_ref[first + i : first + i + 1, :] for i in range(blocks)], axis=1) & (CR - 1)


def step(count_ref, parcel_ref, gas_ref):
    slot = iota((BLK_DEV, BLK), 0) * BLK + iota((BLK_DEV, BLK), 1)
    alive = slot < count_ref[0]
    diam = parcel_ref[3]
    vel = [parcel_ref[i] for i in range(3)]
    gas = [gas_ref[i] for i in range(3)]
    slip = [g - u for g, u in zip(gas, vel)]
    slip_sq = slip[0] * slip[0] + slip[1] * slip[1] + slip[2] * slip[2]
    new_vel = [(u * diam + STEP_SIZE * g) / (diam + STEP_SIZE) for u, g in zip(vel, gas)]
    new_diam = diam / (1.0 + STEP_SIZE * EVAP_RATE * (1.0 + slip_sq))
    sources = [(diam - new_diam) * COUPLING] + [
        -(diam * (v - u)) * COUPLING for v, u in zip(new_vel, vel)
    ]
    state = [jnp.where(alive, s, 0.0) for s in new_vel + [new_diam]]
    return state, [jnp.where(alive, s, 0.0) for s in sources]


def pick(rows, first, spans, mask, gas_ref):
    for f, (start, stop) in enumerate(spans):
        found = jnp.sum(jnp.where(mask, rows[start:stop], 0.0), axis=0, keepdims=True)
        for i in range(4):
            gas_ref[f, first + i : first + i + 1, :] = found[:, i * BLK : (i + 1) * BLK]


def parcels_body(
    rad_ref, odd_ref, count_ref, move_ref, q_ref, parcel_ref, cells_ref,
    src_out, stay_out, leave_out, rad_out, gas_ref, state_ref, leave_ref,
):
    rad_edges(rad_ref[0], q_ref, rad_out)
    parts = [[], []]
    for f in range(3):
        high, low = halves(q_ref[f + 1].reshape(ROWS, CR).T)
        parts[0].append(high)
        parts[1].append(low)
    parts = [jnp.concatenate(part, axis=0) for part in parts]
    spans = [(f * CR, (f + 1) * CR) for f in range(3)]
    for first in range(0, BLK_DEV, 4):
        hot, lanes = one_hot_rows(cells_ref, first, 4)
        rows = sum(jnp.dot(part, hot, preferred_element_type=F32) for part in parts)
        pick(rows, first, spans, iota((CR, 4 * BLK), 0) == lanes, gas_ref)
    state, sources = step(count_ref, parcel_ref, gas_ref)
    for i in range(4):
        src_out[i] = sources[i]
        state_ref[i] = state[i]
    leave_ref[...] = jnp.zeros_like(leave_ref)

    def place(block, ranks):
        up, down = ranks
        move = move_ref[block]
        row = state_ref[:, pl.ds(block, 1), :]
        stay_out[:, pl.ds(block, 1), :] = jnp.where(move == 0, row, 0.0)

        @pl.when(move == 1)
        def _():
            leave_ref[0, :, pl.ds(jnp.minimum(up, MOVEB - 1), 1), :] = row

        @pl.when(move == -1)
        def _():
            leave_ref[1, :, pl.ds(jnp.minimum(down, MOVEB - 1), 1), :] = row

        return up + (move == 1).astype(jnp.int32), down + (move == -1).astype(jnp.int32)

    lax.fori_loop(0, BLK_DEV, place, (jnp.int32(0), jnp.int32(0)))
    odd = odd_ref[0] == 1
    up, down = leave_ref[0], leave_ref[1]
    leave_out[0] = jnp.where(odd, down, up)
    leave_out[1] = jnp.where(odd, up, down)


SOURCE_OF = (0, 1, 2, 3, 0)


BAND = 24
SHARE = 2 * FIELDS * CAX // N_AZ


def turned(parts):
    lane = iota((2 * CAZ, CR), 1)
    packed = jnp.zeros((2 * CAZ, CR), F32)
    for f, part in enumerate(parts):
        moved = pltpu.roll(part, f * BAND, 1) if f else part
        packed = jnp.where((lane >= f * BAND) & (lane < (f + 1) * BAND), moved, packed)
    return packed.T


def near_parcels_body(count_ref, q_ref, parcel_ref, cells_ref, tiles_out, near_out, gas_ref, hot_ref, spread_ref):
    for p in range(PAIRS):
        tiles_out[:, p * 2 * CAZ : (p + 1) * 2 * CAZ] = turned(
            [q_ref[f, 2 * p : 2 * p + 2].reshape(2 * CAZ, CR) for f in range(FIELDS)]
        )
    start = 16
    table = jnp.concatenate(halves(tiles_out[start : 4 * BAND]), axis=0)
    depth = 4 * BAND - start
    spans = [((f + 1) * BAND - start, (f + 1) * BAND - start + CYCLES) for f in range(3)]
    for first in range(0, BLK_DEV, 4):
        hot, lanes = one_hot_rows(cells_ref, first, 4)
        hot_ref[:, first * BLK : (first + 4) * BLK] = hot
        rows = jnp.dot(table, hot, preferred_element_type=F32)
        rows = rows[:depth] + rows[depth:]
        pick(rows, first, spans, iota((CYCLES, 4 * BLK), 0) == lanes, gas_ref)
    _, sources = step(count_ref, parcel_ref, gas_ref)
    rows = [s.astype(BF16).astype(F32) for s in sources]
    rows = rows + [s - r for s, r in zip(sources, rows)]
    for block in range(BLK_DEV):
        mask = iota((CYCLES, BLK), 0) == (cells_ref[block : block + 1, :] & (CR - 1))
        for i, row in enumerate(rows):
            spread_ref[i * CYCLES : (i + 1) * CYCLES, block * BLK : (block + 1) * BLK] = jnp.where(
                mask, row[block : block + 1, :], 0.0
            ).astype(BF16)
    total = lax.dot_general(spread_ref[...], hot_ref[...], NT, preferred_element_type=F32)
    near_out[...] = total[: 4 * CYCLES] + total[4 * CYCLES :]


def near_body(
    odd_ref, coef_ref, q_ref, first_ref, second_ref, tiles_ref, near_ref, send_hbm, az_ref, send_out, sems
):
    for f in range(FIELDS):
        az_ref[f * CAX : (f + 1) * CAX] = q_ref[f, :, 0, :]
        az_ref[(FIELDS + f) * CAX : (FIELDS + f + 1) * CAX] = q_ref[f, :, CAZ - 1, :]
    for owner in range(N_AZ):
        send_out[owner, LINES + 4 :, :] = az_ref[owner * SHARE : (owner + 1) * SHARE]
    copies = []
    lane = iota((CR, 2 * CAZ), 1)
    z = lane % CAZ
    tiles = [tiles_ref[:, p * 2 * CAZ : (p + 1) * 2 * CAZ] for p in range(PAIRS)]
    odd = odd_ref[0] == 1
    first, second = first_ref[...], second_ref[...]
    before, after = jnp.where(odd, first, second), jnp.where(odd, second, first)
    halo = turned([jnp.concatenate([before[f], after[f]], axis=0) for f in range(FIELDS)])

    column = iota((CR, 1), 0)
    radius = column
    c = [jnp.zeros((CR, 1), F32) for _ in range(6)]
    for f in range(FIELDS):
        here = (column >= f * BAND) & (column < (f + 1) * BAND)
        radius = jnp.where(here, column - f * BAND, radius)
        c = [jnp.where(here, coef_ref[f, i], c[i]) for i in range(6)]
    metric = 4.0 / (radius.astype(F32) + 4.0)
    mid = (1.0 - c[1] - c[5]) - c[3] * metric
    az_up, az_down = (0.5 * (c[2] + c[3])) * metric, (0.5 * (c[3] - c[2])) * metric
    ax_up, ax_down = 0.5 * (c[0] + c[1]), 0.5 * (c[1] - c[0])
    rad_up = 0.5 * (c[4] + c[5])
    rad_down = jnp.where(radius == 0, 0.0, 0.5 * (c[5] - c[4]))
    low = lane < CAZ
    swapped = [pltpu.roll(t, CAZ, 1) for t in tiles]
    for p in range(PAIRS):
        q = tiles[p]
        ahead = jnp.where(low, swapped[p], swapped[p + 1] if p + 1 < PAIRS else halo)
        behind = jnp.where(low, swapped[p - 1] if p else halo, swapped[p])
        az_a = jnp.where(z == CAZ - 1, 0.0, pltpu.roll(q, 2 * CAZ - 1, 1))
        az_b = jnp.where(z == 0, 0.0, pltpu.roll(q, 1, 1))
        r_a = pltpu.roll(q, CR - 1, 0)
        r_b = pltpu.roll(q, 1, 0)
        out = (
            mid * q + ax_up * ahead + ax_down * behind + az_up * az_a + az_down * az_b
            + rad_up * r_a + rad_down * r_b
        )
        ends = jnp.where(z == 0, az_up * q, jnp.where(z == CAZ - 1, az_down * q, 0.0))
        ends = sum(
            pltpu.roll(ends[f * BAND : f * BAND + CYCLES], 2 * f, 1) if f else ends[:CYCLES]
            for f in range(FIELDS)
        )
        for f in range(FIELDS):
            s = SOURCE_OF[f] * CYCLES
            block = out[f * BAND : f * BAND + CYCLES] + near_ref[
                s : s + CYCLES, p * 2 * CAZ : (p + 1) * 2 * CAZ
            ]
            for quad in range(QUADS):
                send_out[p * QUADS + quad, f * 4 : f * 4 + 4, :] = block[quad * 4 : quad * 4 + 4]
        for quad in range(QUADS):
            send_out[p * QUADS + quad, LINES : LINES + 4, :] = ends[quad * 4 : quad * 4 + 4]
        span = pl.ds(p * QUADS, QUADS)
        copies.append(pltpu.make_async_copy(send_out.at[span], send_hbm.at[span], sems.at[p]))
        copies[p].start()
    for copy in copies:
        copy.wait()


def rad_edges(rad, q_ref, rad_out):
    extra = jnp.where(rad == 0, 1, 0)
    lane = iota((32, CR), 1)
    packed = jnp.zeros((32, CR), F32)
    for f in range(FIELDS):
        for g in range(16):
            part = q_ref[f, g // 2, (g % 2) * 32 : (g % 2) * 32 + 32, :]
            spot = g * 8 + f
            packed = jnp.where(lane == spot, pltpu.roll(part, spot + extra, 1), packed)
    rad_out[...] = packed


def gas_body(
    rad_ref, odd_ref, coef_ref, q_ref, first_ref, second_ref, rad_in, src_ref, cells_ref, _, sect_out, acc_ref
):
    width = 8
    for first in range(0, BLK_DEV, width):
        hot, lanes = one_hot_rows(cells_ref, first, width)
        mask = iota((CR, width * BLK), 0) == lanes
        spread = [[], []]
        for i in range(4):
            row = jnp.concatenate([src_ref[i, first + j : first + j + 1, :] for j in range(width)], axis=1)
            high = row.astype(BF16).astype(F32)
            spread[0].append(jnp.where(mask, high, 0.0).astype(BF16))
            spread[1].append(jnp.where(mask, row - high, 0.0).astype(BF16))
        total = sum(
            lax.dot_general(hot, jnp.concatenate(part, axis=0), NT, preferred_element_type=F32)
            for part in spread
        )
        if first == 0:
            acc_ref[...] = total
        else:
            acc_ref[...] += total
    rad = rad_ref[0]
    odd = odd_ref[0] == 1
    row = iota((CAZ, CR), 0)
    lane = iota((1, CR), 1)
    metric = 4.0 / ((rad * CR + lane).astype(F32) + 4.0)
    target = jnp.where(rad == 0, CR - 1, 0)
    for f in range(FIELDS):
        c = [coef_ref[f, i] for i in range(6)]
        mid = (1.0 - c[1] - c[5]) - c[3] * metric
        az_up = jnp.where(row == CAZ - 1, 0.0, (0.5 * (c[2] + c[3])) * metric)
        az_down = jnp.where(row == 0, 0.0, (0.5 * (c[3] - c[2])) * metric)
        ax_up, ax_down = 0.5 * (c[0] + c[1]), 0.5 * (c[1] - c[0])
        rad_up = jnp.where(lane == CR - 1, 0.0, 0.5 * (c[4] + c[5]))
        rad_down = jnp.where(lane == 0, 0.0, 0.5 * (c[5] - c[4]))
        across = 0.5 * jnp.where(rad == 0, c[4] + c[5], c[5] - c[4])
        across = jnp.where(lane == target, across, 0.0)
        s = SOURCE_OF[f] * CR
        for a in range(CAX):
            q = q_ref[f, a]
            ahead = q_ref[f, a + 1] if a + 1 < CAX else jnp.where(odd, second_ref[f], first_ref[f])
            behind = q_ref[f, a - 1] if a else jnp.where(odd, first_ref[f], second_ref[f])
            edge = jnp.concatenate(
                [pltpu.roll(rad_in[...], (target + (2 * CR - ((2 * a + h) * 8 + f))) % CR, 1) for h in range(2)],
                axis=0,
            )
            sect_out[f, a] = (
                mid * q + ax_up * ahead + ax_down * behind
                + az_up * pltpu.roll(q, CAZ - 1, 0) + az_down * pltpu.roll(q, 1, 0)
                + rad_up * pltpu.roll(q, CR - 1, 1) + rad_down * pltpu.roll(q, 1, 1)
                + across * edge
                + acc_ref[a * CAZ : (a + 1) * CAZ, s : s + CR]
            )


def lined(pieces, line_ref):
    low = iota((LINES, 2 * CAZ), 1) < CAZ
    for i in range(N_AZ // 2):
        t0, t1 = pieces(2 * i), pieces(2 * i + 1)
        cols = slice(i * 2 * CAZ, (i + 1) * 2 * CAZ)
        line_ref[0:LINES, cols] = jnp.where(low, t0, pltpu.roll(t1, CAZ, 1))
        line_ref[BAND : BAND + LINES, cols] = jnp.where(low, pltpu.roll(t0, CAZ, 1), t1)


def filter_body(
    az_ref, width_ref, basis_ref, turned_ref, got_ref, moved_ref,
    send_out, onward_out, line_ref, ends_ref, piece_ref,
):
    onward_out[...] = moved_ref[1]
    for home in range(N_AZ):
        send_out[home, LINES:, :] = jnp.where(
            az_ref[0] < N_AZ // 2,
            got_ref[(home + 1) % N_AZ, LINES + 4 :, :],
            got_ref[(home - 1) % N_AZ, LINES + 4 :, :],
        )
    quad = az_ref[0] % QUADS
    low = iota((LINES, 2 * CAZ), 1) < CAZ
    line_ref[...] = jnp.zeros_like(line_ref)
    ends_ref[...] = jnp.zeros_like(ends_ref)
    for s in range(N_AZ):
        packed = got_ref[s, LINES : LINES + 4, :]
        for f in range(FIELDS):
            piece_ref[s, f * 4 : f * 4 + 4, :] = pltpu.roll(packed, 2 * CAZ - 2 * f, 1) if f else packed
    lined(lambda s: got_ref[s, 0:LINES, :], line_ref)
    lined(lambda s: piece_ref[s], ends_ref)
    z = iota((2 * BAND, NAZ), 1) % CAZ
    ends = ends_ref[...]
    lines = (
        line_ref[...]
        + jnp.where(z == CAZ - 1, pltpu.roll(ends, NAZ - 1, 1), 0.0)
        + jnp.where(z == 0, pltpu.roll(ends, 1, 1), 0.0)
    )
    rows = 2 * BAND
    both = jnp.concatenate(halves(lines), axis=0)
    whole = jnp.dot(both, turned_ref[...], preferred_element_type=F32)
    coefs = whole[:rows, :MODES] + whole[rows:, :MODES] + whole[:rows, MODES:]
    column = iota((rows, MODES), 1)
    cycle = iota((rows, MODES), 0) % 4
    mode = jnp.where(column < HALF, column, column - HALF + 1)
    width = jnp.zeros((rows, MODES), jnp.int32)
    for i in range(4):
        width = jnp.where(cycle == i, width_ref[quad * 4 + i], width)
    weight = jnp.where(mode == 0, 1.0 / NAZ, 2.0 / NAZ)
    coefs = coefs * jnp.where(mode < width, weight, 0.0)
    high, rest = halves(coefs)
    line_ref[...] = jnp.dot(
        jnp.concatenate([high, high], axis=1), basis_ref[...], preferred_element_type=F32
    ) + jnp.dot(rest, basis_ref[:MODES], preferred_element_type=F32)
    for i in range(N_AZ // 2):
        cols = slice(i * 2 * CAZ, (i + 1) * 2 * CAZ)
        t0, t1 = line_ref[0:LINES, cols], line_ref[BAND : BAND + LINES, cols]
        send_out[2 * i, 0:LINES] = jnp.where(low, t0, pltpu.roll(t1, CAZ, 1))
        send_out[2 * i + 1, 0:LINES] = jnp.where(low, pltpu.roll(t0, CAZ, 1), t1)


def merge_body(
    rad_ref, odd_ref, coef_ref, sect_ref, got_ref, stay_ref, moved_ref, onward_ref,
    gas_out, parcels_out, flip_ref, az_ref,
):
    odd = odd_ref[0] == 1
    parcels_out[:, 0:BLK_DEV, :] = stay_ref[...]
    first, second = moved_ref[0], onward_ref[...]
    parcels_out[:, BLK_DEV : BLK_DEV + MOVEB, :] = jnp.where(odd, first, second)
    parcels_out[:, BLK_DEV + MOVEB :, :] = jnp.where(odd, second, first)
    near = (iota((2 * CAZ, CR), 1) < CYCLES) & (rad_ref[0] == 0)
    for owner in range(N_AZ):
        az_ref[owner * SHARE : (owner + 1) * SHARE] = got_ref[owner, LINES:, :]
    tiles = []
    for pair in range(PAIRS):
        flip_ref[pair, FIELDS * CYCLES :, :] = jnp.zeros((CR - FIELDS * CYCLES, CR), F32)
        for f in range(FIELDS):
            for quad in range(QUADS):
                first = f * CYCLES + quad * 4
                flip_ref[pair, first : first + 4, :] = got_ref[pair * QUADS + quad, f * 4 : f * 4 + 4, :]
        tiles.append(flip_ref[pair].T)
    lane = iota((1, CR), 1)
    metric = 4.0 / ((rad_ref[0] * CR + lane).astype(F32) + 4.0)
    metric = jnp.where((lane < CYCLES) & (rad_ref[0] == 0), 0.0, metric)
    for f in range(FIELDS):
        for pair in range(PAIRS):
            moved = pltpu.roll(tiles[pair], CR - f * CYCLES, 1) if f else tiles[pair]
            kept = sect_ref[f, 2 * pair : 2 * pair + 2].reshape(2 * CAZ, CR)
            gas_out[f, 2 * pair : 2 * pair + 2] = jnp.where(near, moved, kept).reshape(2, CAZ, CR)
        az_up = (0.5 * (coef_ref[f, 2] + coef_ref[f, 3])) * metric
        az_down = (0.5 * (coef_ref[f, 3] - coef_ref[f, 2])) * metric
        after = az_up * az_ref[f * CAX : (f + 1) * CAX]
        before = az_down * az_ref[(FIELDS + f) * CAX : (FIELDS + f + 1) * CAX]
        for a in range(CAX):
            gas_out[f, a, 0:1] += before[a : a + 1]
            gas_out[f, a, CAZ - 1 : CAZ] += after[a : a + 1]


def shards(fields, coeffs, parcels, cells, counts, moves, widths):
    rad_index = lax.axis_index("rad").astype(jnp.int32).reshape(1)
    az_index = lax.axis_index("az").astype(jnp.int32).reshape(1)
    odd = (lax.axis_index("ax").astype(jnp.int32) % 2).reshape(1)
    n_ax, n_rad = lax.axis_size("ax"), lax.axis_size("rad")
    parcels = parcels.reshape(4, BLK_DEV, BLK)
    cells = cells.reshape(BLK_DEV, BLK)
    counts = counts.reshape(1)
    moves = moves.reshape(BLK_DEV)
    inner = [(i, i ^ 1) for i in range(n_ax)]
    outer = [(i, ((i + 1) ^ 1) - 1) for i in range(1, n_ax - 1)]
    along = [(i, i + 2) for i in range(0, n_ax - 2, 2)] + [(i, i - 2) for i in range(3, n_ax, 2)]
    across = [(i, i ^ 1) for i in range(n_rad)]
    gas_shape = (FIELDS, CAX, CAZ, CR)

    first, second = call(
        edges_body, [(FIELDS, CAZ, CR)] * 2, [SMEM, VMEM], 10**6, 10**6, mib=4
    )(odd, fields)
    first = lax.ppermute(first, "ax", inner)
    second = lax.ppermute(second, "ax", outer)

    tiles, near = call(
        near_parcels_body,
        [(CR, ROWS), (4 * CYCLES, ROWS)],
        [SMEM] + [VMEM] * 3, 3 * 10**9, 2 * 10**6,
        [
            pltpu.VMEM((3, BLK_DEV, BLK), F32),
            pltpu.VMEM((ROWS, PARCELS), BF16),
            pltpu.VMEM((8 * CYCLES, PARCELS), BF16),
        ],
        mib=16,
    )(counts, fields, parcels, cells)

    (to_owner,) = call(
        near_body,
        [(N_AZ, LINES + 4 + SHARE, 2 * CAZ)],
        [SMEM, SMEM] + [VMEM] * 5, 10**7, 4 * 10**6,
        [
            pltpu.VMEM((2 * FIELDS * CAX, CR), F32),
            pltpu.VMEM((N_AZ, LINES + 4 + SHARE, 2 * CAZ), F32),
            pltpu.SemaphoreType.DMA((PAIRS,)),
        ],
        mib=8,
        hbm_first=True,
    )(odd, coeffs, fields, first, second, tiles, near)
    lines = lax.all_to_all(to_owner, "az", 0, 0, tiled=True)

    src, stay, leaving, rad_edge = call(
        parcels_body,
        [(4, BLK_DEV, BLK), (4, BLK_DEV, BLK), (2, 4, MOVEB, BLK), (32, CR)],
        [SMEM] * 4 + [VMEM] * 3, 6 * 10**9, 2 * 10**6,
        [
            pltpu.VMEM((3, BLK_DEV, BLK), F32),
            pltpu.VMEM((4, BLK_DEV, BLK), F32),
            pltpu.VMEM((2, 4, MOVEB, BLK), F32),
        ],
        mib=16,
    )(rad_index, odd, counts, moves, fields, parcels, cells)
    rad_got = lax.ppermute(rad_edge, "rad", across)
    moved = lax.ppermute(leaving, "ax", inner)

    basis, basis_turned = basis_parts()
    to_home, onward = call(
        filter_body,
        [(N_AZ, LINES + SHARE, 2 * CAZ), (4, MOVEB, BLK)],
        [SMEM, SMEM] + [VMEM] * 4, 10**8, 10**6,
        [
            pltpu.VMEM((2 * BAND, NAZ), F32),
            pltpu.VMEM((2 * BAND, NAZ), F32),
            pltpu.VMEM((N_AZ, LINES, 2 * CAZ), F32),
        ],
        mib=6,
    )(az_index, widths, basis, basis_turned, lines, moved)
    filtered = lax.all_to_all(to_home, "az", 0, 0, tiled=True)
    onward = lax.ppermute(onward, "ax", along)

    (sect,) = call(
        gas_body, [gas_shape], [SMEM, SMEM, SMEM] + [VMEM] * 6 + [ANY], 8 * 10**9, 4 * 10**6,
        [pltpu.VMEM((ROWS, 4 * CR), F32)],
        mib=16,
    )(rad_index, odd, coeffs, fields, first, second, rad_got, src, cells, to_home)

    gas_out, parcels_out = call(
        merge_body,
        [gas_shape, (4, BLK_DEV + 2 * MOVEB, BLK)],
        [SMEM, SMEM, SMEM] + [VMEM] * 5, 10**6, 4 * 10**6,
        [
            pltpu.VMEM((PAIRS, CR, CR), F32),
            pltpu.VMEM((2 * FIELDS * CAX, CR), F32),
        ],
        mib=8,
    )(rad_index, odd, coeffs, sect, filtered, stay, moved, onward)
    return gas_out, parcels_out.reshape(4, BLK_DEV + 2 * MOVEB, 1, BLK)


def solution(mesh):
    block = P(None, "ax", "az", "rad")
    flat = P("ax", "az", "rad")
    return jax.shard_map(
        shards,
        mesh=mesh,
        in_specs=(block, P(), block, flat, flat, flat, P()),
        out_specs=(block, block),
        check_vma=False,
    )
```

```python
import math

import jax
import jax.numpy as jnp
import ml_dtypes
import numpy as np
from jax import lax
from jax.experimental import pallas as pl
from jax.experimental.pallas import tpu as pltpu
from jax.sharding import PartitionSpec as P

FIELDS = 5
CYCLES = 16
MODES = 128
HALF = MODES // 2
BLK = 128
BLK_DEV = 32
MOVEB = 4
CAX, CAZ, CR = 8, 64, 128
ROWS = CAX * CAZ
PARCELS = BLK * BLK_DEV
NAZ = 1024
N_AZ = 16
PAIRS = CAX // 2
QUADS = CYCLES // 4
LINES = FIELDS * 4

STEP_SIZE = 0.5
EVAP_RATE = 0.5
COUPLING = 0.5

F32 = jnp.float32
BF16 = jnp.bfloat16
HIGHEST = lax.Precision.HIGHEST
VMEM = pl.BlockSpec(memory_space=pltpu.VMEM)
SMEM = pl.BlockSpec(memory_space=pltpu.SMEM)
ANY = pl.BlockSpec(memory_space=pl.ANY)
HBM = pl.BlockSpec(memory_space=pltpu.HBM)
NT = (((1,), (1,)), ((), ()))


def basis_parts():
    column = np.arange(MODES)
    mode = np.where(column < HALF, column, column - HALF + 1)
    phases = (mode[:, None] * np.arange(NAZ)[None, :]) % NAZ
    angles = phases.astype(np.float32) * np.float32(2.0 * math.pi / NAZ)
    table = np.where(column[:, None] < HALF, np.cos(angles), np.sin(angles)).astype(np.float32)
    high = table.astype(ml_dtypes.bfloat16)
    low = (table - high.astype(np.float32)).astype(ml_dtypes.bfloat16)
    parts = np.concatenate([high, low])
    return jnp.asarray(parts), jnp.asarray(np.ascontiguousarray(parts.T))


def iota(shape, axis):
    return lax.broadcasted_iota(jnp.int32, shape, axis)


def halves(value):
    high = value.astype(BF16)
    return high, (value - high.astype(F32)).astype(BF16)


def call(body, out_shape, in_specs, flops, nbytes, scratch=(), mib=24, hbm_first=False):
    return pl.pallas_call(
        body,
        out_shape=[jax.ShapeDtypeStruct(shape, F32) for shape in out_shape],
        in_specs=in_specs,
        out_specs=[HBM if hbm_first and i == 0 else VMEM for i in range(len(out_shape))],
        scratch_shapes=list(scratch),
        compiler_params=pltpu.CompilerParams(vmem_limit_bytes=mib * 2**20),
        cost_estimate=pl.CostEstimate(flops=flops, bytes_accessed=nbytes, transcendentals=0),
    )


def edges_body(odd_ref, q_ref, first_out, second_out, az_lo, az_hi):
    odd = odd_ref[0] == 1
    low, high = q_ref[:, 0], q_ref[:, CAX - 1]
    first_out[...] = jnp.where(odd, low, high)
    second_out[...] = jnp.where(odd, high, low)
    az_lo[...] = q_ref[:, :, 0, :]
    az_hi[...] = q_ref[:, :, CAZ - 1, :]


def lane_row(cells_ref, first, blocks):
    return jnp.concatenate([cells_ref[first + i : first + i + 1, :] for i in range(blocks)], axis=1)


def equals(count, row):
    numbers = iota((count, row.shape[1]), 0).astype(F32).astype(BF16)
    return numbers == row.astype(F32).astype(BF16)


def one_hot_rows(cells_ref, first, blocks):
    cells = lane_row(cells_ref, first, blocks)
    one, zero = jnp.ones((), BF16), jnp.zeros((), BF16)
    half = ROWS // 2
    parts = [jnp.where(equals(half, (cells >> 7) - half * i), one, zero) for i in range(2)]
    return jnp.concatenate(parts, axis=0), cells & (CR - 1)


def step(count_ref, parcel_ref, gas_ref):
    slot = iota((BLK_DEV, BLK), 0) * BLK + iota((BLK_DEV, BLK), 1)
    alive = slot < count_ref[0]
    diam = parcel_ref[3]
    vel = [parcel_ref[i] for i in range(3)]
    gas = [gas_ref[i] for i in range(3)]
    slip = [g - u for g, u in zip(gas, vel)]
    slip_sq = slip[0] * slip[0] + slip[1] * slip[1] + slip[2] * slip[2]
    new_vel = [(u * diam + STEP_SIZE * g) / (diam + STEP_SIZE) for u, g in zip(vel, gas)]
    new_diam = diam / (1.0 + STEP_SIZE * EVAP_RATE * (1.0 + slip_sq))
    sources = [(diam - new_diam) * COUPLING] + [
        -(diam * (v - u)) * COUPLING for v, u in zip(new_vel, vel)
    ]
    state = [jnp.where(alive, s, 0.0) for s in new_vel + [new_diam]]
    return state, [jnp.where(alive, s, 0.0) for s in sources]


def pick(rows, first, spans, mask, gas_ref):
    for f, (start, stop) in enumerate(spans):
        found = jnp.sum(jnp.where(mask, rows[start:stop], 0.0), axis=0, keepdims=True)
        for i in range(4):
            gas_ref[f, first + i : first + i + 1, :] = found[:, i * BLK : (i + 1) * BLK]


def parcels_body(
    rad_ref, odd_ref, count_ref, move_ref, q_ref, parcel_ref, cells_ref,
    src_out, stay_out, leave_out, rad_out, gas_ref, state_ref, leave_ref,
):
    rad_edges(rad_ref[0], q_ref, rad_out)
    table = jnp.concatenate(
        [jnp.concatenate(halves(q_ref[f + 1].reshape(ROWS, CR).T), axis=1) for f in range(3)], axis=0
    )
    spans = [(f * CR, (f + 1) * CR) for f in range(3)]
    for first in range(0, BLK_DEV, 4):
        hot, lanes = one_hot_rows(cells_ref, first, 4)
        rows = jnp.dot(table, jnp.concatenate([hot, hot], axis=0), preferred_element_type=F32)
        pick(rows, first, spans, iota((CR, 4 * BLK), 0) == lanes, gas_ref)
    state, sources = step(count_ref, parcel_ref, gas_ref)
    for i in range(4):
        src_out[i] = sources[i]
        state_ref[i] = state[i]
    leave_ref[...] = jnp.zeros_like(leave_ref)

    def place(block, ranks):
        up, down = ranks
        move = move_ref[block]
        row = state_ref[:, pl.ds(block, 1), :]
        stay_out[:, pl.ds(block, 1), :] = jnp.where(move == 0, row, 0.0)

        @pl.when(move == 1)
        def _():
            leave_ref[0, :, pl.ds(jnp.minimum(up, MOVEB - 1), 1), :] = row

        @pl.when(move == -1)
        def _():
            leave_ref[1, :, pl.ds(jnp.minimum(down, MOVEB - 1), 1), :] = row

        return up + (move == 1).astype(jnp.int32), down + (move == -1).astype(jnp.int32)

    lax.fori_loop(0, BLK_DEV, place, (jnp.int32(0), jnp.int32(0)))
    odd = odd_ref[0] == 1
    up, down = leave_ref[0], leave_ref[1]
    leave_out[0] = jnp.where(odd, down, up)
    leave_out[1] = jnp.where(odd, up, down)


SOURCE_OF = (0, 1, 2, 3, 0)


BAND = 24


def turned(parts):
    lane = iota((2 * CAZ, CR), 1)
    packed = jnp.zeros((2 * CAZ, CR), F32)
    for f, part in enumerate(parts):
        moved = pltpu.roll(part, f * BAND, 1) if f else part
        packed = jnp.where((lane >= f * BAND) & (lane < (f + 1) * BAND), moved, packed)
    return packed.T


def near_parcels_body(count_ref, q_ref, parcel_ref, cells_ref, tiles_out, near_out, gas_ref, hot_ref, spread_ref):
    for p in range(PAIRS):
        tiles_out[:, p * 2 * CAZ : (p + 1) * 2 * CAZ] = turned(
            [q_ref[f, 2 * p : 2 * p + 2].reshape(2 * CAZ, CR) for f in range(FIELDS)]
        )
    start = 16
    table = jnp.concatenate(halves(tiles_out[start : 4 * BAND]), axis=0)
    depth = 4 * BAND - start
    spans = [((f + 1) * BAND - start, (f + 1) * BAND - start + CYCLES) for f in range(3)]
    for first in range(0, BLK_DEV, 4):
        hot, lanes = one_hot_rows(cells_ref, first, 4)
        hot_ref[:, first * BLK : (first + 4) * BLK] = hot
        rows = jnp.dot(table, hot, preferred_element_type=F32)
        rows = rows[:depth] + rows[depth:]
        pick(rows, first, spans, iota((CYCLES, 4 * BLK), 0) == lanes, gas_ref)
    _, sources = step(count_ref, parcel_ref, gas_ref)
    rows = [s.astype(BF16) for s in sources]
    rows = [r.astype(F32) for r in rows] + [s - r.astype(F32) for s, r in zip(sources, rows)]
    zero = jnp.zeros((), BF16)
    for first in range(0, BLK_DEV, 4):
        mask = equals(CYCLES, lane_row(cells_ref, first, 4) & (CR - 1))
        for i, row in enumerate(rows):
            row = jnp.concatenate([row[first + j : first + j + 1] for j in range(4)], axis=1).astype(BF16)
            spread_ref[i * CYCLES : (i + 1) * CYCLES, first * BLK : (first + 4) * BLK] = jnp.where(mask, row, zero)
    total = lax.dot_general(spread_ref[...], hot_ref[...], NT, preferred_element_type=F32)
    near_out[...] = total[: 4 * CYCLES] + total[4 * CYCLES :]


def near_body(
    odd_ref, coef_ref, first_ref, second_ref, tiles_ref, near_ref, _, __, send_hbm, send_out, sems
):
    copies = []
    lane = iota((CR, 2 * CAZ), 1)
    z = lane % CAZ
    tiles = [tiles_ref[:, p * 2 * CAZ : (p + 1) * 2 * CAZ] for p in range(PAIRS)]
    odd = odd_ref[0] == 1
    first, second = first_ref[...], second_ref[...]
    before, after = jnp.where(odd, first, second), jnp.where(odd, second, first)
    halo = turned([jnp.concatenate([before[f], after[f]], axis=0) for f in range(FIELDS)])

    column = iota((CR, 1), 0)
    radius = column
    c = [jnp.zeros((CR, 1), F32) for _ in range(6)]
    for f in range(FIELDS):
        here = (column >= f * BAND) & (column < (f + 1) * BAND)
        radius = jnp.where(here, column - f * BAND, radius)
        c = [jnp.where(here, coef_ref[f, i], c[i]) for i in range(6)]
    metric = 4.0 / (radius.astype(F32) + 4.0)
    mid = (1.0 - c[1] - c[5]) - c[3] * metric
    az_up, az_down = (0.5 * (c[2] + c[3])) * metric, (0.5 * (c[3] - c[2])) * metric
    ax_up, ax_down = 0.5 * (c[0] + c[1]), 0.5 * (c[1] - c[0])
    rad_up = 0.5 * (c[4] + c[5])
    rad_down = jnp.where(radius == 0, 0.0, 0.5 * (c[5] - c[4]))
    low = lane < CAZ
    swapped = [pltpu.roll(t, CAZ, 1) for t in tiles]
    for p in range(PAIRS):
        q = tiles[p]
        ahead = jnp.where(low, swapped[p], swapped[p + 1] if p + 1 < PAIRS else halo)
        behind = jnp.where(low, swapped[p - 1] if p else halo, swapped[p])
        az_a = jnp.where(z == CAZ - 1, 0.0, pltpu.roll(q, 2 * CAZ - 1, 1))
        az_b = jnp.where(z == 0, 0.0, pltpu.roll(q, 1, 1))
        r_a = pltpu.roll(q, CR - 1, 0)
        r_b = pltpu.roll(q, 1, 0)
        out = (
            mid * q + ax_up * ahead + ax_down * behind + az_up * az_a + az_down * az_b
            + rad_up * r_a + rad_down * r_b
        )
        ends = jnp.where(z == 0, az_up * q, jnp.where(z == CAZ - 1, az_down * q, 0.0))
        ends = sum(
            pltpu.roll(ends[f * BAND : f * BAND + CYCLES], 2 * f, 1) if f else ends[:CYCLES]
            for f in range(FIELDS)
        )
        for f in range(FIELDS):
            s = SOURCE_OF[f] * CYCLES
            block = out[f * BAND : f * BAND + CYCLES] + near_ref[
                s : s + CYCLES, p * 2 * CAZ : (p + 1) * 2 * CAZ
            ]
            for quad in range(QUADS):
                send_out[p * QUADS + quad, f * 4 : f * 4 + 4, :] = block[quad * 4 : quad * 4 + 4]
        for quad in range(QUADS):
            send_out[p * QUADS + quad, LINES : LINES + 4, :] = ends[quad * 4 : quad * 4 + 4]
        span = pl.ds(p * QUADS, QUADS)
        copies.append(pltpu.make_async_copy(send_out.at[span], send_hbm.at[span], sems.at[p]))
        copies[p].start()
    for copy in copies:
        copy.wait()


def rad_edges(rad, q_ref, rad_out):
    extra = jnp.where(rad == 0, 1, 0)
    lane = iota((32, CR), 1)
    packed = jnp.zeros((32, CR), F32)
    for f in range(FIELDS):
        for g in range(16):
            part = q_ref[f, g // 2, (g % 2) * 32 : (g % 2) * 32 + 32, :]
            spot = g * 8 + f
            packed = jnp.where(lane == spot, pltpu.roll(part, spot + extra, 1), packed)
    rad_out[...] = packed


def gas_body(
    rad_ref, odd_ref, coef_ref, q_ref, first_ref, second_ref, az_prev, az_next, rad_in, src_ref, cells_ref, _,
    sect_out, hot_ref, spread_ref,
):
    width = 4
    zero = jnp.zeros((), BF16)
    for first in range(0, BLK_DEV, width):
        cols = slice(first * BLK, (first + width) * BLK)
        hot, lanes = one_hot_rows(cells_ref, first, width)
        hot_ref[:, cols] = hot
        mask = equals(CR, lanes)
        for i in range(4):
            row = jnp.concatenate([src_ref[i, first + j : first + j + 1, :] for j in range(width)], axis=1)
            high = row.astype(BF16)
            low = (row - high.astype(F32)).astype(BF16)
            spread_ref[i, 0:CR, cols] = jnp.where(mask, high, zero)
            spread_ref[i, CR:, cols] = jnp.where(mask, low, zero)
    added = []
    for i in range(4):
        total = lax.dot_general(hot_ref[...], spread_ref[i], NT, preferred_element_type=F32)
        added.append(total[:, :CR] + total[:, CR:])
    rad = rad_ref[0]
    odd = odd_ref[0] == 1
    row = iota((CAZ, CR), 0)
    lane = iota((1, CR), 1)
    metric = 4.0 / ((rad * CR + lane).astype(F32) + 4.0)
    target = jnp.where(rad == 0, CR - 1, 0)
    for f in range(FIELDS):
        c = [coef_ref[f, i] for i in range(6)]
        mid = (1.0 - c[1] - c[5]) - c[3] * metric
        az_up_edge, az_down_edge = (0.5 * (c[2] + c[3])) * metric, (0.5 * (c[3] - c[2])) * metric
        az_up = jnp.where(row == CAZ - 1, 0.0, az_up_edge)
        az_down = jnp.where(row == 0, 0.0, az_down_edge)
        ax_up, ax_down = 0.5 * (c[0] + c[1]), 0.5 * (c[1] - c[0])
        rad_up = jnp.where(lane == CR - 1, 0.0, 0.5 * (c[4] + c[5]))
        rad_down = jnp.where(lane == 0, 0.0, 0.5 * (c[5] - c[4]))
        across = 0.5 * jnp.where(rad == 0, c[4] + c[5], c[5] - c[4])
        across = jnp.where(lane == target, across, 0.0)
        for a in range(CAX):
            q = q_ref[f, a]
            ahead = q_ref[f, a + 1] if a + 1 < CAX else jnp.where(odd, second_ref[f], first_ref[f])
            behind = q_ref[f, a - 1] if a else jnp.where(odd, first_ref[f], second_ref[f])
            edge = jnp.concatenate(
                [pltpu.roll(rad_in[...], (target + (2 * CR - ((2 * a + h) * 8 + f))) % CR, 1) for h in range(2)],
                axis=0,
            )
            sect_out[f, a] = (
                mid * q + ax_up * ahead + ax_down * behind
                + az_up * pltpu.roll(q, CAZ - 1, 0) + az_down * pltpu.roll(q, 1, 0)
                + rad_up * pltpu.roll(q, CR - 1, 1) + rad_down * pltpu.roll(q, 1, 1)
                + across * edge
                + added[SOURCE_OF[f]][a * CAZ : (a + 1) * CAZ]
            )
            sect_out[f, a, 0:1] += az_down_edge * az_prev[f, a : a + 1]
            sect_out[f, a, CAZ - 1 : CAZ] += az_up_edge * az_next[f, a : a + 1]


def lined(pieces, line_ref):
    low = iota((LINES, 2 * CAZ), 1) < CAZ
    for i in range(N_AZ // 2):
        t0, t1 = pieces(2 * i), pieces(2 * i + 1)
        cols = slice(i * 2 * CAZ, (i + 1) * 2 * CAZ)
        line_ref[0:LINES, cols] = jnp.where(low, t0, pltpu.roll(t1, CAZ, 1))
        line_ref[BAND : BAND + LINES, cols] = jnp.where(low, pltpu.roll(t0, CAZ, 1), t1)


def filter_body(
    az_ref, width_ref, basis_ref, turned_ref, got_ref, moved_ref,
    send_out, onward_out, line_ref, ends_ref, piece_ref,
):
    onward_out[...] = moved_ref[1]
    quad = az_ref[0] % QUADS
    low = iota((LINES, 2 * CAZ), 1) < CAZ
    line_ref[...] = jnp.zeros_like(line_ref)
    ends_ref[...] = jnp.zeros_like(ends_ref)
    for s in range(N_AZ):
        packed = got_ref[s, LINES : LINES + 4, :]
        for f in range(FIELDS):
            piece_ref[s, f * 4 : f * 4 + 4, :] = pltpu.roll(packed, 2 * CAZ - 2 * f, 1) if f else packed
    lined(lambda s: got_ref[s, 0:LINES, :], line_ref)
    lined(lambda s: piece_ref[s], ends_ref)
    z = iota((2 * BAND, NAZ), 1) % CAZ
    ends = ends_ref[...]
    lines = (
        line_ref[...]
        + jnp.where(z == CAZ - 1, pltpu.roll(ends, NAZ - 1, 1), 0.0)
        + jnp.where(z == 0, pltpu.roll(ends, 1, 1), 0.0)
    )
    rows = 2 * BAND
    both = jnp.concatenate(halves(lines), axis=0)
    whole = jnp.dot(both, turned_ref[...], preferred_element_type=F32)
    coefs = whole[:rows, :MODES] + whole[rows:, :MODES] + whole[:rows, MODES:]
    column = iota((rows, MODES), 1)
    cycle = iota((rows, MODES), 0) % 4
    mode = jnp.where(column < HALF, column, column - HALF + 1)
    width = jnp.zeros((rows, MODES), jnp.int32)
    for i in range(4):
        width = jnp.where(cycle == i, width_ref[quad * 4 + i], width)
    weight = jnp.where(mode == 0, 1.0 / NAZ, 2.0 / NAZ)
    coefs = coefs * jnp.where(mode < width, weight, 0.0)
    high, rest = halves(coefs)
    line_ref[...] = jnp.dot(
        jnp.concatenate([high, high], axis=1), basis_ref[...], preferred_element_type=F32
    ) + jnp.dot(rest, basis_ref[:MODES], preferred_element_type=F32)
    for i in range(N_AZ // 2):
        cols = slice(i * 2 * CAZ, (i + 1) * 2 * CAZ)
        t0, t1 = line_ref[0:LINES, cols], line_ref[BAND : BAND + LINES, cols]
        send_out[2 * i, 0:LINES] = jnp.where(low, t0, pltpu.roll(t1, CAZ, 1))
        send_out[2 * i + 1, 0:LINES] = jnp.where(low, pltpu.roll(t0, CAZ, 1), t1)


def merge_body(
    rad_ref, odd_ref, sect_ref, got_ref, stay_ref, moved_ref, onward_ref, gas_out, parcels_out, flip_ref
):
    odd = odd_ref[0] == 1
    parcels_out[:, 0:BLK_DEV, :] = stay_ref[...]
    first, second = moved_ref[0], onward_ref[...]
    parcels_out[:, BLK_DEV : BLK_DEV + MOVEB, :] = jnp.where(odd, first, second)
    parcels_out[:, BLK_DEV + MOVEB :, :] = jnp.where(odd, second, first)
    near = (iota((2 * CAZ, CR), 1) < CYCLES) & (rad_ref[0] == 0)
    tiles = []
    for pair in range(PAIRS):
        flip_ref[pair, FIELDS * CYCLES :, :] = jnp.zeros((CR - FIELDS * CYCLES, CR), F32)
        for f in range(FIELDS):
            for quad in range(QUADS):
                first = f * CYCLES + quad * 4
                flip_ref[pair, first : first + 4, :] = got_ref[pair * QUADS + quad, f * 4 : f * 4 + 4, :]
        tiles.append(flip_ref[pair].T)
    for f in range(FIELDS):
        for pair in range(PAIRS):
            moved = pltpu.roll(tiles[pair], CR - f * CYCLES, 1) if f else tiles[pair]
            kept = sect_ref[f, 2 * pair : 2 * pair + 2].reshape(2 * CAZ, CR)
            gas_out[f, 2 * pair : 2 * pair + 2] = jnp.where(near, moved, kept).reshape(2, CAZ, CR)


def shards(fields, coeffs, parcels, cells, counts, moves, widths):
    rad_index = lax.axis_index("rad").astype(jnp.int32).reshape(1)
    az_index = lax.axis_index("az").astype(jnp.int32).reshape(1)
    odd = (lax.axis_index("ax").astype(jnp.int32) % 2).reshape(1)
    n_ax, n_az, n_rad = (lax.axis_size(axis) for axis in ("ax", "az", "rad"))
    parcels = parcels.reshape(4, BLK_DEV, BLK)
    cells = cells.reshape(BLK_DEV, BLK)
    counts = counts.reshape(1)
    moves = moves.reshape(BLK_DEV)
    inner = [(i, i ^ 1) for i in range(n_ax)]
    outer = [(i, ((i + 1) ^ 1) - 1) for i in range(1, n_ax - 1)]
    along = [(i, i + 2) for i in range(0, n_ax - 2, 2)] + [(i, i - 2) for i in range(3, n_ax, 2)]
    ahead = [(i, (i + 1) % n_az) for i in range(n_az)]
    back = [((i + 1) % n_az, i) for i in range(n_az)]
    across = [(i, i ^ 1) for i in range(n_rad)]
    gas_shape = (FIELDS, CAX, CAZ, CR)

    first, second, az_lo, az_hi = call(
        edges_body, [(FIELDS, CAZ, CR)] * 2 + [(FIELDS, CAX, CR)] * 2, [SMEM, VMEM], 10**6, 10**6, mib=4
    )(odd, fields)
    first = lax.ppermute(first, "ax", inner)
    second = lax.ppermute(second, "ax", outer)
    az_prev = lax.ppermute(az_hi, "az", ahead)
    az_next = lax.ppermute(az_lo, "az", back)

    tiles, near = call(
        near_parcels_body,
        [(CR, ROWS), (4 * CYCLES, ROWS)],
        [SMEM] + [VMEM] * 3, 3 * 10**9, 2 * 10**6,
        [
            pltpu.VMEM((3, BLK_DEV, BLK), F32),
            pltpu.VMEM((ROWS, PARCELS), BF16),
            pltpu.VMEM((8 * CYCLES, PARCELS), BF16),
        ],
        mib=16,
    )(counts, fields, parcels, cells)

    (to_owner,) = call(
        near_body,
        [(N_AZ, LINES + 4, 2 * CAZ)],
        [SMEM, SMEM] + [VMEM] * 4 + [ANY] * 2, 10**7, 4 * 10**6,
        [
            pltpu.VMEM((N_AZ, LINES + 4, 2 * CAZ), F32),
            pltpu.SemaphoreType.DMA((PAIRS,)),
        ],
        mib=8,
        hbm_first=True,
    )(odd, coeffs, first, second, tiles, near, az_prev, az_next)
    lines = lax.all_to_all(to_owner, "az", 0, 0, tiled=True)

    src, stay, leaving, rad_edge = call(
        parcels_body,
        [(4, BLK_DEV, BLK), (4, BLK_DEV, BLK), (2, 4, MOVEB, BLK), (32, CR)],
        [SMEM] * 4 + [VMEM] * 3, 6 * 10**9, 2 * 10**6,
        [
            pltpu.VMEM((3, BLK_DEV, BLK), F32),
            pltpu.VMEM((4, BLK_DEV, BLK), F32),
            pltpu.VMEM((2, 4, MOVEB, BLK), F32),
        ],
        mib=16,
    )(rad_index, odd, counts, moves, fields, parcels, cells)
    rad_got = lax.ppermute(rad_edge, "rad", across)
    moved = lax.ppermute(leaving, "ax", inner)

    basis, basis_turned = basis_parts()
    to_home, onward = call(
        filter_body,
        [(N_AZ, LINES, 2 * CAZ), (4, MOVEB, BLK)],
        [SMEM, SMEM] + [VMEM] * 4, 10**8, 10**6,
        [
            pltpu.VMEM((2 * BAND, NAZ), F32),
            pltpu.VMEM((2 * BAND, NAZ), F32),
            pltpu.VMEM((N_AZ, LINES, 2 * CAZ), F32),
        ],
        mib=6,
    )(az_index, widths, basis, basis_turned, lines, moved)
    filtered = lax.all_to_all(to_home, "az", 0, 0, tiled=True)
    onward = lax.ppermute(onward, "ax", along)

    (sect,) = call(
        gas_body, [gas_shape], [SMEM, SMEM, SMEM] + [VMEM] * 8 + [ANY], 8 * 10**9, 4 * 10**6,
        [pltpu.VMEM((ROWS, PARCELS), BF16), pltpu.VMEM((4, 2 * CR, PARCELS), BF16)],
        mib=24,
    )(rad_index, odd, coeffs, fields, first, second, az_prev, az_next, rad_got, src, cells, to_home)

    gas_out, parcels_out = call(
        merge_body,
        [gas_shape, (4, BLK_DEV + 2 * MOVEB, BLK)],
        [SMEM, SMEM] + [VMEM] * 5, 10**6, 4 * 10**6,
        [pltpu.VMEM((PAIRS, CR, CR), F32)],
        mib=8,
    )(rad_index, odd, sect, filtered, stay, moved, onward)
    return gas_out, parcels_out.reshape(4, BLK_DEV + 2 * MOVEB, 1, BLK)


def solution(mesh):
    block = P(None, "ax", "az", "rad")
    flat = P("ax", "az", "rad")
    return jax.shard_map(
        shards,
        mesh=mesh,
        in_specs=(block, P(), block, flat, flat, flat, P()),
        out_specs=(block, block),
        check_vma=False,
    )
```

```python
import math

import jax
import jax.numpy as jnp
import ml_dtypes
import numpy as np
from jax import lax
from jax.experimental import pallas as pl
from jax.experimental.pallas import tpu as pltpu
from jax.sharding import PartitionSpec as P

FIELDS = 5
CYCLES = 16
MODES = 128
HALF = MODES // 2
BLK = 128
BLK_DEV = 32
MOVEB = 4
CAX, CAZ, CR = 8, 64, 128
ROWS = CAX * CAZ
PARCELS = BLK * BLK_DEV
NAZ = 1024
N_AZ = 16
PAIRS = CAX // 2
QUADS = CYCLES // 4
LINES = FIELDS * 4

STEP_SIZE = 0.5
EVAP_RATE = 0.5
COUPLING = 0.5

F32 = jnp.float32
BF16 = jnp.bfloat16
HIGHEST = lax.Precision.HIGHEST
VMEM = pl.BlockSpec(memory_space=pltpu.VMEM)
SMEM = pl.BlockSpec(memory_space=pltpu.SMEM)
ANY = pl.BlockSpec(memory_space=pl.ANY)
HBM = pl.BlockSpec(memory_space=pltpu.HBM)
NT = (((1,), (1,)), ((), ()))


def basis_parts():
    column = np.arange(MODES)
    mode = np.where(column < HALF, column, column - HALF + 1)
    phases = (mode[:, None] * np.arange(NAZ)[None, :]) % NAZ
    angles = phases.astype(np.float32) * np.float32(2.0 * math.pi / NAZ)
    table = np.where(column[:, None] < HALF, np.cos(angles), np.sin(angles)).astype(np.float32)
    high = table.astype(ml_dtypes.bfloat16)
    low = (table - high.astype(np.float32)).astype(ml_dtypes.bfloat16)
    parts = np.concatenate([high, low])
    return jnp.asarray(parts), jnp.asarray(np.ascontiguousarray(parts.T))


def iota(shape, axis):
    return lax.broadcasted_iota(jnp.int32, shape, axis)


def halves(value):
    high = value.astype(BF16)
    return high, (value - high.astype(F32)).astype(BF16)


def call(body, out_shape, in_specs, flops, nbytes, scratch=(), mib=24, hbm_first=False):
    return pl.pallas_call(
        body,
        out_shape=[jax.ShapeDtypeStruct(shape, F32) for shape in out_shape],
        in_specs=in_specs,
        out_specs=[HBM if hbm_first and i == 0 else VMEM for i in range(len(out_shape))],
        scratch_shapes=list(scratch),
        compiler_params=pltpu.CompilerParams(vmem_limit_bytes=mib * 2**20),
        cost_estimate=pl.CostEstimate(flops=flops, bytes_accessed=nbytes, transcendentals=0),
    )


def edges_body(odd_ref, q_ref, first_out, second_out, az_lo, az_hi):
    odd = odd_ref[0] == 1
    low, high = q_ref[:, 0], q_ref[:, CAX - 1]
    first_out[...] = jnp.where(odd, low, high)
    second_out[...] = jnp.where(odd, high, low)
    az_lo[...] = q_ref[:, :, 0, :]
    az_hi[...] = q_ref[:, :, CAZ - 1, :]


def lane_row(cells_ref, first, blocks):
    return jnp.concatenate([cells_ref[first + i : first + i + 1, :] for i in range(blocks)], axis=1)


def equals(count, row):
    numbers = iota((count, row.shape[1]), 0).astype(F32).astype(BF16)
    return numbers == row.astype(F32).astype(BF16)


def one_hot_rows(cells_ref, first, blocks):
    cells = lane_row(cells_ref, first, blocks)
    one, zero = jnp.ones((), BF16), jnp.zeros((), BF16)
    half = ROWS // 2
    parts = [jnp.where(equals(half, (cells >> 7) - half * i), one, zero) for i in range(2)]
    return jnp.concatenate(parts, axis=0), cells & (CR - 1)


def step(count_ref, parcel_ref, gas_ref):
    slot = iota((BLK_DEV, BLK), 0) * BLK + iota((BLK_DEV, BLK), 1)
    alive = slot < count_ref[0]
    diam = parcel_ref[3]
    vel = [parcel_ref[i] for i in range(3)]
    gas = [gas_ref[i] for i in range(3)]
    slip = [g - u for g, u in zip(gas, vel)]
    slip_sq = slip[0] * slip[0] + slip[1] * slip[1] + slip[2] * slip[2]
    new_vel = [(u * diam + STEP_SIZE * g) / (diam + STEP_SIZE) for u, g in zip(vel, gas)]
    new_diam = diam / (1.0 + STEP_SIZE * EVAP_RATE * (1.0 + slip_sq))
    sources = [(diam - new_diam) * COUPLING] + [
        -(diam * (v - u)) * COUPLING for v, u in zip(new_vel, vel)
    ]
    state = [jnp.where(alive, s, 0.0) for s in new_vel + [new_diam]]
    return state, [jnp.where(alive, s, 0.0) for s in sources]


def pick(rows, first, spans, mask, gas_ref):
    for f, (start, stop) in enumerate(spans):
        found = jnp.sum(jnp.where(mask, rows[start:stop], 0.0), axis=0, keepdims=True)
        for i in range(4):
            gas_ref[f, first + i : first + i + 1, :] = found[:, i * BLK : (i + 1) * BLK]


def parcels_body(
    rad_ref, odd_ref, count_ref, move_ref, q_ref, parcel_ref, cells_ref,
    src_out, stay_out, leave_out, rad_out, gas_ref, state_ref, leave_ref,
):
    rad_edges(rad_ref[0], q_ref, rad_out)
    table = jnp.concatenate(
        [jnp.concatenate(halves(q_ref[f + 1].reshape(ROWS, CR).T), axis=1) for f in range(3)], axis=0
    )
    spans = [(f * CR, (f + 1) * CR) for f in range(3)]
    for first in range(0, BLK_DEV, 4):
        hot, lanes = one_hot_rows(cells_ref, first, 4)
        rows = jnp.dot(table, jnp.concatenate([hot, hot], axis=0), preferred_element_type=F32)
        pick(rows, first, spans, iota((CR, 4 * BLK), 0) == lanes, gas_ref)
    state, sources = step(count_ref, parcel_ref, gas_ref)
    for i in range(4):
        src_out[i] = sources[i]
        state_ref[i] = state[i]
    leave_ref[...] = jnp.zeros_like(leave_ref)

    def place(block, ranks):
        up, down = ranks
        move = move_ref[block]
        row = state_ref[:, pl.ds(block, 1), :]
        stay_out[:, pl.ds(block, 1), :] = jnp.where(move == 0, row, 0.0)

        @pl.when(move == 1)
        def _():
            leave_ref[0, :, pl.ds(jnp.minimum(up, MOVEB - 1), 1), :] = row

        @pl.when(move == -1)
        def _():
            leave_ref[1, :, pl.ds(jnp.minimum(down, MOVEB - 1), 1), :] = row

        return up + (move == 1).astype(jnp.int32), down + (move == -1).astype(jnp.int32)

    lax.fori_loop(0, BLK_DEV, place, (jnp.int32(0), jnp.int32(0)))
    odd = odd_ref[0] == 1
    up, down = leave_ref[0], leave_ref[1]
    leave_out[0] = jnp.where(odd, down, up)
    leave_out[1] = jnp.where(odd, up, down)


SOURCE_OF = (0, 1, 2, 3, 0)


BAND = 24


def turned(parts):
    lane = iota((2 * CAZ, CR), 1)
    packed = jnp.zeros((2 * CAZ, CR), F32)
    for f, part in enumerate(parts):
        moved = pltpu.roll(part, f * BAND, 1) if f else part
        packed = jnp.where((lane >= f * BAND) & (lane < (f + 1) * BAND), moved, packed)
    return packed.T


def near_parcels_body(count_ref, q_ref, parcel_ref, cells_ref, tiles_out, near_out, gas_ref, hot_ref, spread_ref):
    for p in range(PAIRS):
        tiles_out[:, p * 2 * CAZ : (p + 1) * 2 * CAZ] = turned(
            [q_ref[f, 2 * p : 2 * p + 2].reshape(2 * CAZ, CR) for f in range(FIELDS)]
        )
    start = 16
    table = jnp.concatenate(halves(tiles_out[start : 4 * BAND]), axis=0)
    depth = 4 * BAND - start
    spans = [((f + 1) * BAND - start, (f + 1) * BAND - start + CYCLES) for f in range(3)]
    for first in range(0, BLK_DEV, 4):
        hot, lanes = one_hot_rows(cells_ref, first, 4)
        hot_ref[:, first * BLK : (first + 4) * BLK] = hot
        rows = jnp.dot(table, hot, preferred_element_type=F32)
        rows = rows[:depth] + rows[depth:]
        pick(rows, first, spans, iota((CYCLES, 4 * BLK), 0) == lanes, gas_ref)
    _, sources = step(count_ref, parcel_ref, gas_ref)
    rows = [s.astype(BF16) for s in sources]
    rows = [r.astype(F32) for r in rows] + [s - r.astype(F32) for s, r in zip(sources, rows)]
    zero = jnp.zeros((), BF16)
    for first in range(0, BLK_DEV, 4):
        mask = equals(CYCLES, lane_row(cells_ref, first, 4) & (CR - 1))
        for i, row in enumerate(rows):
            row = jnp.concatenate([row[first + j : first + j + 1] for j in range(4)], axis=1).astype(BF16)
            spread_ref[i * CYCLES : (i + 1) * CYCLES, first * BLK : (first + 4) * BLK] = jnp.where(mask, row, zero)
    total = lax.dot_general(spread_ref[...], hot_ref[...], NT, preferred_element_type=F32)
    near_out[...] = total[: 4 * CYCLES] + total[4 * CYCLES :]


def near_body(
    odd_ref, coef_ref, first_ref, second_ref, tiles_ref, near_ref, send_hbm, send_out, sems
):
    copies = []
    lane = iota((CR, 2 * CAZ), 1)
    z = lane % CAZ
    tiles = [tiles_ref[:, p * 2 * CAZ : (p + 1) * 2 * CAZ] for p in range(PAIRS)]
    odd = odd_ref[0] == 1
    first, second = first_ref[...], second_ref[...]
    before, after = jnp.where(odd, first, second), jnp.where(odd, second, first)
    halo = turned([jnp.concatenate([before[f], after[f]], axis=0) for f in range(FIELDS)])

    column = iota((CR, 1), 0)
    radius = column
    c = [jnp.zeros((CR, 1), F32) for _ in range(6)]
    for f in range(FIELDS):
        here = (column >= f * BAND) & (column < (f + 1) * BAND)
        radius = jnp.where(here, column - f * BAND, radius)
        c = [jnp.where(here, coef_ref[f, i], c[i]) for i in range(6)]
    metric = 4.0 / (radius.astype(F32) + 4.0)
    mid = (1.0 - c[1] - c[5]) - c[3] * metric
    az_up, az_down = (0.5 * (c[2] + c[3])) * metric, (0.5 * (c[3] - c[2])) * metric
    ax_up, ax_down = 0.5 * (c[0] + c[1]), 0.5 * (c[1] - c[0])
    rad_up = 0.5 * (c[4] + c[5])
    rad_down = jnp.where(radius == 0, 0.0, 0.5 * (c[5] - c[4]))
    low = lane < CAZ
    swapped = [pltpu.roll(t, CAZ, 1) for t in tiles]
    for p in range(PAIRS):
        q = tiles[p]
        ahead = jnp.where(low, swapped[p], swapped[p + 1] if p + 1 < PAIRS else halo)
        behind = jnp.where(low, swapped[p - 1] if p else halo, swapped[p])
        az_a = jnp.where(z == CAZ - 1, 0.0, pltpu.roll(q, 2 * CAZ - 1, 1))
        az_b = jnp.where(z == 0, 0.0, pltpu.roll(q, 1, 1))
        r_a = pltpu.roll(q, CR - 1, 0)
        r_b = pltpu.roll(q, 1, 0)
        out = (
            mid * q + ax_up * ahead + ax_down * behind + az_up * az_a + az_down * az_b
            + rad_up * r_a + rad_down * r_b
        )
        ends = jnp.where(z == 0, az_up * q, jnp.where(z == CAZ - 1, az_down * q, 0.0))
        ends = sum(
            pltpu.roll(ends[f * BAND : f * BAND + CYCLES], 2 * f, 1) if f else ends[:CYCLES]
            for f in range(FIELDS)
        )
        for f in range(FIELDS):
            s = SOURCE_OF[f] * CYCLES
            block = out[f * BAND : f * BAND + CYCLES] + near_ref[
                s : s + CYCLES, p * 2 * CAZ : (p + 1) * 2 * CAZ
            ]
            for quad in range(QUADS):
                send_out[p * QUADS + quad, f * 4 : f * 4 + 4, :] = block[quad * 4 : quad * 4 + 4]
        for quad in range(QUADS):
            send_out[p * QUADS + quad, LINES : LINES + 4, :] = ends[quad * 4 : quad * 4 + 4]
        span = pl.ds(p * QUADS, QUADS)
        copies.append(pltpu.make_async_copy(send_out.at[span], send_hbm.at[span], sems.at[p]))
        copies[p].start()
    for copy in copies:
        copy.wait()


def rad_edges(rad, q_ref, rad_out):
    extra = jnp.where(rad == 0, 1, 0)
    lane = iota((32, CR), 1)
    packed = jnp.zeros((32, CR), F32)
    for f in range(FIELDS):
        for g in range(16):
            part = q_ref[f, g // 2, (g % 2) * 32 : (g % 2) * 32 + 32, :]
            spot = g * 8 + f
            packed = jnp.where(lane == spot, pltpu.roll(part, spot + extra, 1), packed)
    rad_out[...] = packed


def gas_body(
    rad_ref, odd_ref, coef_ref, q_ref, first_ref, second_ref, az_prev, az_next, rad_in, src_ref, cells_ref, _,
    sect_out, hot_ref, spread_ref,
):
    width = 4
    zero = jnp.zeros((), BF16)

    def scattered(i):
        for first in range(0, BLK_DEV, width):
            cols = slice(first * BLK, (first + width) * BLK)
            if i == 0:
                hot_ref[:, cols] = one_hot_rows(cells_ref, first, width)[0]
            mask = equals(CR, lane_row(cells_ref, first, width) & (CR - 1))
            row = jnp.concatenate([src_ref[i, first + j : first + j + 1, :] for j in range(width)], axis=1)
            high = row.astype(BF16)
            low = (row - high.astype(F32)).astype(BF16)
            spread_ref[i, 0:CR, cols] = jnp.where(mask, high, zero)
            spread_ref[i, CR:, cols] = jnp.where(mask, low, zero)
        total = lax.dot_general(hot_ref[...], spread_ref[i], NT, preferred_element_type=F32)
        return total[:, :CR] + total[:, CR:]

    rad = rad_ref[0]
    odd = odd_ref[0] == 1
    row = iota((CAZ, CR), 0)
    lane = iota((1, CR), 1)
    metric = 4.0 / ((rad * CR + lane).astype(F32) + 4.0)
    target = jnp.where(rad == 0, CR - 1, 0)
    added = {0: scattered(0)}
    for f in (0, 4, 1, 2, 3):
        if f in (0, 1, 2):
            added[f + 1] = scattered(f + 1)
        c = [coef_ref[f, i] for i in range(6)]
        mid = (1.0 - c[1] - c[5]) - c[3] * metric
        az_up_edge, az_down_edge = (0.5 * (c[2] + c[3])) * metric, (0.5 * (c[3] - c[2])) * metric
        az_up = jnp.where(row == CAZ - 1, 0.0, az_up_edge)
        az_down = jnp.where(row == 0, 0.0, az_down_edge)
        ax_up, ax_down = 0.5 * (c[0] + c[1]), 0.5 * (c[1] - c[0])
        rad_up = jnp.where(lane == CR - 1, 0.0, 0.5 * (c[4] + c[5]))
        rad_down = jnp.where(lane == 0, 0.0, 0.5 * (c[5] - c[4]))
        across = 0.5 * jnp.where(rad == 0, c[4] + c[5], c[5] - c[4])
        across = jnp.where(lane == target, across, 0.0)
        for a in range(CAX):
            q = q_ref[f, a]
            ahead = q_ref[f, a + 1] if a + 1 < CAX else jnp.where(odd, second_ref[f], first_ref[f])
            behind = q_ref[f, a - 1] if a else jnp.where(odd, first_ref[f], second_ref[f])
            edge = jnp.concatenate(
                [pltpu.roll(rad_in[...], (target + (2 * CR - ((2 * a + h) * 8 + f))) % CR, 1) for h in range(2)],
                axis=0,
            )
            sect_out[f, a] = (
                mid * q + ax_up * ahead + ax_down * behind
                + az_up * pltpu.roll(q, CAZ - 1, 0) + az_down * pltpu.roll(q, 1, 0)
                + rad_up * pltpu.roll(q, CR - 1, 1) + rad_down * pltpu.roll(q, 1, 1)
                + across * edge
                + added[SOURCE_OF[f]][a * CAZ : (a + 1) * CAZ]
            )
            sect_out[f, a, 0:1] += az_down_edge * az_prev[f, a : a + 1]
            sect_out[f, a, CAZ - 1 : CAZ] += az_up_edge * az_next[f, a : a + 1]


def lined(pieces, line_ref):
    low = iota((LINES, 2 * CAZ), 1) < CAZ
    for i in range(N_AZ // 2):
        t0, t1 = pieces(2 * i), pieces(2 * i + 1)
        cols = slice(i * 2 * CAZ, (i + 1) * 2 * CAZ)
        line_ref[0:LINES, cols] = jnp.where(low, t0, pltpu.roll(t1, CAZ, 1))
        line_ref[BAND : BAND + LINES, cols] = jnp.where(low, pltpu.roll(t0, CAZ, 1), t1)


def filter_body(
    az_ref, width_ref, basis_ref, turned_ref, got_ref, moved_ref,
    send_out, onward_out, line_ref, ends_ref, piece_ref,
):
    onward_out[...] = moved_ref[1]
    quad = az_ref[0] % QUADS
    low = iota((LINES, 2 * CAZ), 1) < CAZ
    line_ref[...] = jnp.zeros_like(line_ref)
    ends_ref[...] = jnp.zeros_like(ends_ref)
    for s in range(N_AZ):
        packed = got_ref[s, LINES : LINES + 4, :]
        for f in range(FIELDS):
            piece_ref[s, f * 4 : f * 4 + 4, :] = pltpu.roll(packed, 2 * CAZ - 2 * f, 1) if f else packed
    lined(lambda s: got_ref[s, 0:LINES, :], line_ref)
    lined(lambda s: piece_ref[s], ends_ref)
    z = iota((2 * BAND, NAZ), 1) % CAZ
    ends = ends_ref[...]
    lines = (
        line_ref[...]
        + jnp.where(z == CAZ - 1, pltpu.roll(ends, NAZ - 1, 1), 0.0)
        + jnp.where(z == 0, pltpu.roll(ends, 1, 1), 0.0)
    )
    rows = 2 * BAND
    both = jnp.concatenate(halves(lines), axis=0)
    whole = jnp.dot(both, turned_ref[...], preferred_element_type=F32)
    coefs = whole[:rows, :MODES] + whole[rows:, :MODES] + whole[:rows, MODES:]
    column = iota((rows, MODES), 1)
    cycle = iota((rows, MODES), 0) % 4
    mode = jnp.where(column < HALF, column, column - HALF + 1)
    width = jnp.zeros((rows, MODES), jnp.int32)
    for i in range(4):
        width = jnp.where(cycle == i, width_ref[quad * 4 + i], width)
    weight = jnp.where(mode == 0, 1.0 / NAZ, 2.0 / NAZ)
    coefs = coefs * jnp.where(mode < width, weight, 0.0)
    high, rest = halves(coefs)
    line_ref[...] = jnp.dot(
        jnp.concatenate([high, high], axis=1), basis_ref[...], preferred_element_type=F32
    ) + jnp.dot(rest, basis_ref[:MODES], preferred_element_type=F32)
    for i in range(N_AZ // 2):
        cols = slice(i * 2 * CAZ, (i + 1) * 2 * CAZ)
        t0, t1 = line_ref[0:LINES, cols], line_ref[BAND : BAND + LINES, cols]
        send_out[2 * i, 0:LINES] = jnp.where(low, t0, pltpu.roll(t1, CAZ, 1))
        send_out[2 * i + 1, 0:LINES] = jnp.where(low, pltpu.roll(t0, CAZ, 1), t1)


def merge_body(
    rad_ref, odd_ref, sect_ref, got_ref, stay_ref, moved_ref, onward_ref, gas_out, parcels_out, flip_ref
):
    odd = odd_ref[0] == 1
    parcels_out[:, 0:BLK_DEV, :] = stay_ref[...]
    first, second = moved_ref[0], onward_ref[...]
    parcels_out[:, BLK_DEV : BLK_DEV + MOVEB, :] = jnp.where(odd, first, second)
    parcels_out[:, BLK_DEV + MOVEB :, :] = jnp.where(odd, second, first)
    near = (iota((2 * CAZ, CR), 1) < CYCLES) & (rad_ref[0] == 0)
    tiles = []
    for pair in range(PAIRS):
        flip_ref[pair, FIELDS * CYCLES :, :] = jnp.zeros((CR - FIELDS * CYCLES, CR), F32)
        for f in range(FIELDS):
            for quad in range(QUADS):
                first = f * CYCLES + quad * 4
                flip_ref[pair, first : first + 4, :] = got_ref[pair * QUADS + quad, f * 4 : f * 4 + 4, :]
        tiles.append(flip_ref[pair].T)
    for f in range(FIELDS):
        for pair in range(PAIRS):
            moved = pltpu.roll(tiles[pair], CR - f * CYCLES, 1) if f else tiles[pair]
            kept = sect_ref[f, 2 * pair : 2 * pair + 2].reshape(2 * CAZ, CR)
            gas_out[f, 2 * pair : 2 * pair + 2] = jnp.where(near, moved, kept).reshape(2, CAZ, CR)


def shards(fields, coeffs, parcels, cells, counts, moves, widths):
    rad_index = lax.axis_index("rad").astype(jnp.int32).reshape(1)
    az_index = lax.axis_index("az").astype(jnp.int32).reshape(1)
    odd = (lax.axis_index("ax").astype(jnp.int32) % 2).reshape(1)
    n_ax, n_az, n_rad = (lax.axis_size(axis) for axis in ("ax", "az", "rad"))
    parcels = parcels.reshape(4, BLK_DEV, BLK)
    cells = cells.reshape(BLK_DEV, BLK)
    counts = counts.reshape(1)
    moves = moves.reshape(BLK_DEV)
    inner = [(i, i ^ 1) for i in range(n_ax)]
    outer = [(i, ((i + 1) ^ 1) - 1) for i in range(1, n_ax - 1)]
    along = [(i, i + 2) for i in range(0, n_ax - 2, 2)] + [(i, i - 2) for i in range(3, n_ax, 2)]
    ahead = [(i, (i + 1) % n_az) for i in range(n_az)]
    back = [((i + 1) % n_az, i) for i in range(n_az)]
    across = [(i, i ^ 1) for i in range(n_rad)]
    gas_shape = (FIELDS, CAX, CAZ, CR)

    first, second, az_lo, az_hi = call(
        edges_body, [(FIELDS, CAZ, CR)] * 2 + [(FIELDS, CAX, CR)] * 2, [SMEM, VMEM], 10**6, 10**6, mib=4
    )(odd, fields)
    first = lax.ppermute(first, "ax", inner)
    second = lax.ppermute(second, "ax", outer)
    az_prev = lax.ppermute(az_hi, "az", ahead)
    az_next = lax.ppermute(az_lo, "az", back)

    tiles, near = call(
        near_parcels_body,
        [(CR, ROWS), (4 * CYCLES, ROWS)],
        [SMEM] + [VMEM] * 3, 3 * 10**9, 2 * 10**6,
        [
            pltpu.VMEM((3, BLK_DEV, BLK), F32),
            pltpu.VMEM((ROWS, PARCELS), BF16),
            pltpu.VMEM((8 * CYCLES, PARCELS), BF16),
        ],
        mib=16,
    )(counts, fields, parcels, cells)

    (to_owner,) = call(
        near_body,
        [(N_AZ, LINES + 4, 2 * CAZ)],
        [SMEM, SMEM] + [VMEM] * 4, 10**7, 4 * 10**6,
        [
            pltpu.VMEM((N_AZ, LINES + 4, 2 * CAZ), F32),
            pltpu.SemaphoreType.DMA((PAIRS,)),
        ],
        mib=8,
        hbm_first=True,
    )(odd, coeffs, first, second, tiles, near)
    lines = lax.all_to_all(to_owner, "az", 0, 0, tiled=True)

    src, stay, leaving, rad_edge = call(
        parcels_body,
        [(4, BLK_DEV, BLK), (4, BLK_DEV, BLK), (2, 4, MOVEB, BLK), (32, CR)],
        [SMEM] * 4 + [VMEM] * 3, 6 * 10**9, 2 * 10**6,
        [
            pltpu.VMEM((3, BLK_DEV, BLK), F32),
            pltpu.VMEM((4, BLK_DEV, BLK), F32),
            pltpu.VMEM((2, 4, MOVEB, BLK), F32),
        ],
        mib=16,
    )(rad_index, odd, counts, moves, fields, parcels, cells)
    rad_got = lax.ppermute(rad_edge, "rad", across)
    moved = lax.ppermute(leaving, "ax", inner)

    basis, basis_turned = basis_parts()
    to_home, onward = call(
        filter_body,
        [(N_AZ, LINES, 2 * CAZ), (4, MOVEB, BLK)],
        [SMEM, SMEM] + [VMEM] * 4, 10**8, 10**6,
        [
            pltpu.VMEM((2 * BAND, NAZ), F32),
            pltpu.VMEM((2 * BAND, NAZ), F32),
            pltpu.VMEM((N_AZ, LINES, 2 * CAZ), F32),
        ],
        mib=6,
    )(az_index, widths, basis, basis_turned, lines, moved)
    filtered = lax.all_to_all(to_home, "az", 0, 0, tiled=True)
    onward = lax.ppermute(onward, "ax", along)

    (sect,) = call(
        gas_body, [gas_shape], [SMEM, SMEM, SMEM] + [VMEM] * 8 + [ANY], 8 * 10**9, 4 * 10**6,
        [pltpu.VMEM((ROWS, PARCELS), BF16), pltpu.VMEM((4, 2 * CR, PARCELS), BF16)],
        mib=24,
    )(rad_index, odd, coeffs, fields, first, second, az_prev, az_next, rad_got, src, cells, to_home)

    gas_out, parcels_out = call(
        merge_body,
        [gas_shape, (4, BLK_DEV + 2 * MOVEB, BLK)],
        [SMEM, SMEM] + [VMEM] * 5, 10**6, 4 * 10**6,
        [pltpu.VMEM((PAIRS, CR, CR), F32)],
        mib=8,
    )(rad_index, odd, sect, filtered, stay, moved, onward)
    return gas_out, parcels_out.reshape(4, BLK_DEV + 2 * MOVEB, 1, BLK)


def solution(mesh):
    block = P(None, "ax", "az", "rad")
    flat = P("ax", "az", "rad")
    return jax.shard_map(
        shards,
        mesh=mesh,
        in_specs=(block, P(), block, flat, flat, flat, P()),
        out_specs=(block, block),
        check_vma=False,
    )
```

```python
import math

import jax
import jax.numpy as jnp
import ml_dtypes
import numpy as np
from jax import lax
from jax.experimental import pallas as pl
from jax.experimental.pallas import tpu as pltpu
from jax.sharding import PartitionSpec as P

FIELDS = 5
CYCLES = 16
MODES = 128
HALF = MODES // 2
BLK = 128
BLK_DEV = 32
MOVEB = 4
CAX, CAZ, CR = 8, 64, 128
ROWS = CAX * CAZ
PARCELS = BLK * BLK_DEV
NAZ = 1024
N_AZ = 16
PAIRS = CAX // 2
QUADS = CYCLES // 4
LINES = FIELDS * 4

STEP_SIZE = 0.5
EVAP_RATE = 0.5
COUPLING = 0.5

F32 = jnp.float32
BF16 = jnp.bfloat16
HIGHEST = lax.Precision.HIGHEST
VMEM = pl.BlockSpec(memory_space=pltpu.VMEM)
SMEM = pl.BlockSpec(memory_space=pltpu.SMEM)
ANY = pl.BlockSpec(memory_space=pl.ANY)
HBM = pl.BlockSpec(memory_space=pltpu.HBM)
NT = (((1,), (1,)), ((), ()))


def basis_parts():
    column = np.arange(MODES)
    mode = np.where(column < HALF, column, column - HALF + 1)
    phases = (mode[:, None] * np.arange(NAZ)[None, :]) % NAZ
    angles = phases.astype(np.float32) * np.float32(2.0 * math.pi / NAZ)
    table = np.where(column[:, None] < HALF, np.cos(angles), np.sin(angles)).astype(np.float32)
    high = table.astype(ml_dtypes.bfloat16)
    low = (table - high.astype(np.float32)).astype(ml_dtypes.bfloat16)
    parts = np.concatenate([high, low])
    return jnp.asarray(parts), jnp.asarray(np.ascontiguousarray(parts.T))


def iota(shape, axis):
    return lax.broadcasted_iota(jnp.int32, shape, axis)


def halves(value):
    high = value.astype(BF16)
    return high, (value - high.astype(F32)).astype(BF16)


def call(body, out_shape, in_specs, flops, nbytes, scratch=(), mib=24, hbm_first=False):
    return pl.pallas_call(
        body,
        out_shape=[jax.ShapeDtypeStruct(shape, F32) for shape in out_shape],
        in_specs=in_specs,
        out_specs=[HBM if hbm_first and i == 0 else VMEM for i in range(len(out_shape))],
        scratch_shapes=list(scratch),
        compiler_params=pltpu.CompilerParams(vmem_limit_bytes=mib * 2**20),
        cost_estimate=pl.CostEstimate(flops=flops, bytes_accessed=nbytes, transcendentals=0),
    )


def edges_body(odd_ref, az_ref, q_ref, first_out, second_out, az_first, az_second):
    odd, odd_az = odd_ref[0] == 1, az_ref[0] % 2 == 1
    low, high = q_ref[:, 0], q_ref[:, CAX - 1]
    first_out[...] = jnp.where(odd, low, high)
    second_out[...] = jnp.where(odd, high, low)
    low, high = q_ref[:, :, 0, :], q_ref[:, :, CAZ - 1, :]
    az_first[...] = jnp.where(odd_az, low, high)
    az_second[...] = jnp.where(odd_az, high, low)


def lane_row(cells_ref, first, blocks):
    return jnp.concatenate([cells_ref[first + i : first + i + 1, :] for i in range(blocks)], axis=1)


def equals(count, row):
    numbers = iota((count, row.shape[1]), 0).astype(F32).astype(BF16)
    return numbers == row.astype(F32).astype(BF16)


def one_hot_rows(cells_ref, first, blocks):
    cells = lane_row(cells_ref, first, blocks)
    one, zero = jnp.ones((), BF16), jnp.zeros((), BF16)
    half = ROWS // 2
    parts = [jnp.where(equals(half, (cells >> 7) - half * i), one, zero) for i in range(2)]
    return jnp.concatenate(parts, axis=0), cells & (CR - 1)


def step(count_ref, parcel_ref, gas_ref):
    slot = iota((BLK_DEV, BLK), 0) * BLK + iota((BLK_DEV, BLK), 1)
    alive = slot < count_ref[0]
    diam = parcel_ref[3]
    vel = [parcel_ref[i] for i in range(3)]
    gas = [gas_ref[i] for i in range(3)]
    slip = [g - u for g, u in zip(gas, vel)]
    slip_sq = slip[0] * slip[0] + slip[1] * slip[1] + slip[2] * slip[2]
    new_vel = [(u * diam + STEP_SIZE * g) / (diam + STEP_SIZE) for u, g in zip(vel, gas)]
    new_diam = diam / (1.0 + STEP_SIZE * EVAP_RATE * (1.0 + slip_sq))
    sources = [(diam - new_diam) * COUPLING] + [
        -(diam * (v - u)) * COUPLING for v, u in zip(new_vel, vel)
    ]
    state = [jnp.where(alive, s, 0.0) for s in new_vel + [new_diam]]
    return state, [jnp.where(alive, s, 0.0) for s in sources]


def pick(rows, first, spans, mask, gas_ref):
    for f, (start, stop) in enumerate(spans):
        found = jnp.sum(jnp.where(mask, rows[start:stop], 0.0), axis=0, keepdims=True)
        for i in range(4):
            gas_ref[f, first + i : first + i + 1, :] = found[:, i * BLK : (i + 1) * BLK]


def parcels_body(
    rad_ref, odd_ref, count_ref, move_ref, q_ref, parcel_ref, cells_ref,
    src_out, stay_out, leave_out, rad_out, gas_ref, state_ref, leave_ref,
):
    rad_edges(rad_ref[0], q_ref, rad_out)
    table = jnp.concatenate(
        [jnp.concatenate(halves(q_ref[f + 1].reshape(ROWS, CR).T), axis=1) for f in range(3)], axis=0
    )
    spans = [(f * CR, (f + 1) * CR) for f in range(3)]
    ready = one_hot_rows(cells_ref, 0, 4)
    for first in range(0, BLK_DEV, 4):
        hot, lanes = ready
        rows = jnp.dot(table, jnp.concatenate([hot, hot], axis=0), preferred_element_type=F32)
        if first + 4 < BLK_DEV:
            ready = one_hot_rows(cells_ref, first + 4, 4)
        pick(rows, first, spans, iota((CR, 4 * BLK), 0) == lanes, gas_ref)
    state, sources = step(count_ref, parcel_ref, gas_ref)
    for i in range(4):
        src_out[i] = sources[i]
        state_ref[i] = state[i]
    leave_ref[...] = jnp.zeros_like(leave_ref)
    up, down, spare = jnp.int32(0), jnp.int32(0), 2 * MOVEB - 1
    for block in range(BLK_DEV):
        move = move_ref[block]
        row = state_ref[:, block : block + 1, :]
        stay_out[:, block : block + 1, :] = jnp.where(move == 0, row, 0.0)
        to_up = jnp.where(move == 1, jnp.minimum(up, MOVEB - 1), spare)
        to_down = jnp.where(move == -1, jnp.minimum(down, MOVEB - 1), spare)
        leave_ref[0, :, pl.ds(to_up, 1), :] = row
        leave_ref[1, :, pl.ds(to_down, 1), :] = row
        up = up + jnp.where(move == 1, 1, 0)
        down = down + jnp.where(move == -1, 1, 0)
    odd = odd_ref[0] == 1
    up, down = leave_ref[0, :, :MOVEB], leave_ref[1, :, :MOVEB]
    leave_out[0] = jnp.where(odd, down, up)
    leave_out[1] = jnp.where(odd, up, down)


SOURCE_OF = (0, 1, 2, 3, 0)


BAND = 24


def turned(parts):
    lane = iota((2 * CAZ, CR), 1)
    packed = jnp.zeros((2 * CAZ, CR), F32)
    for f, part in enumerate(parts):
        moved = pltpu.roll(part, f * BAND, 1) if f else part
        packed = jnp.where((lane >= f * BAND) & (lane < (f + 1) * BAND), moved, packed)
    return packed.T


def near_parcels_body(count_ref, q_ref, parcel_ref, cells_ref, tiles_out, near_out, gas_ref, hot_ref, spread_ref):
    for p in range(PAIRS):
        tiles_out[:, p * 2 * CAZ : (p + 1) * 2 * CAZ] = turned(
            [q_ref[f, 2 * p : 2 * p + 2].reshape(2 * CAZ, CR) for f in range(FIELDS)]
        )
    start = 16
    table = jnp.concatenate(halves(tiles_out[start : 4 * BAND]), axis=0)
    depth = 4 * BAND - start
    spans = [((f + 1) * BAND - start, (f + 1) * BAND - start + CYCLES) for f in range(3)]
    for first in range(0, BLK_DEV, 4):
        hot, lanes = one_hot_rows(cells_ref, first, 4)
        hot_ref[:, first * BLK : (first + 4) * BLK] = hot
        rows = jnp.dot(table, hot, preferred_element_type=F32)
        rows = rows[:depth] + rows[depth:]
        pick(rows, first, spans, iota((CYCLES, 4 * BLK), 0) == lanes, gas_ref)
    _, sources = step(count_ref, parcel_ref, gas_ref)
    rows = [s.astype(BF16) for s in sources]
    rows = [r.astype(F32) for r in rows] + [s - r.astype(F32) for s, r in zip(sources, rows)]
    zero = jnp.zeros((), BF16)
    for first in range(0, BLK_DEV, 4):
        mask = equals(CYCLES, lane_row(cells_ref, first, 4) & (CR - 1))
        for i, row in enumerate(rows):
            row = jnp.concatenate([row[first + j : first + j + 1] for j in range(4)], axis=1).astype(BF16)
            spread_ref[i * CYCLES : (i + 1) * CYCLES, first * BLK : (first + 4) * BLK] = jnp.where(mask, row, zero)
    total = lax.dot_general(spread_ref[...], hot_ref[...], NT, preferred_element_type=F32)
    near_out[...] = total[: 4 * CYCLES] + total[4 * CYCLES :]


def near_body(
    odd_ref, coef_ref, first_ref, second_ref, tiles_ref, near_ref, send_hbm, send_out, sems
):
    copies = []
    lane = iota((CR, 2 * CAZ), 1)
    z = lane % CAZ
    tiles = [tiles_ref[:, p * 2 * CAZ : (p + 1) * 2 * CAZ] for p in range(PAIRS)]
    odd = odd_ref[0] == 1
    first, second = first_ref[...], second_ref[...]
    before, after = jnp.where(odd, first, second), jnp.where(odd, second, first)
    halo = turned([jnp.concatenate([before[f], after[f]], axis=0) for f in range(FIELDS)])

    column = iota((CR, 1), 0)
    radius = column
    c = [jnp.zeros((CR, 1), F32) for _ in range(6)]
    for f in range(FIELDS):
        here = (column >= f * BAND) & (column < (f + 1) * BAND)
        radius = jnp.where(here, column - f * BAND, radius)
        c = [jnp.where(here, coef_ref[f, i], c[i]) for i in range(6)]
    metric = 4.0 / (radius.astype(F32) + 4.0)
    mid = (1.0 - c[1] - c[5]) - c[3] * metric
    az_up, az_down = (0.5 * (c[2] + c[3])) * metric, (0.5 * (c[3] - c[2])) * metric
    ax_up, ax_down = 0.5 * (c[0] + c[1]), 0.5 * (c[1] - c[0])
    rad_up = 0.5 * (c[4] + c[5])
    rad_down = jnp.where(radius == 0, 0.0, 0.5 * (c[5] - c[4]))
    low = lane < CAZ
    swapped = [pltpu.roll(t, CAZ, 1) for t in tiles]
    for p in range(PAIRS):
        q = tiles[p]
        ahead = jnp.where(low, swapped[p], swapped[p + 1] if p + 1 < PAIRS else halo)
        behind = jnp.where(low, swapped[p - 1] if p else halo, swapped[p])
        az_a = jnp.where(z == CAZ - 1, 0.0, pltpu.roll(q, 2 * CAZ - 1, 1))
        az_b = jnp.where(z == 0, 0.0, pltpu.roll(q, 1, 1))
        r_a = pltpu.roll(q, CR - 1, 0)
        r_b = pltpu.roll(q, 1, 0)
        out = (
            mid * q + ax_up * ahead + ax_down * behind + az_up * az_a + az_down * az_b
            + rad_up * r_a + rad_down * r_b
        )
        ends = jnp.where(z == 0, az_up * q, jnp.where(z == CAZ - 1, az_down * q, 0.0))
        ends = sum(
            pltpu.roll(ends[f * BAND : f * BAND + CYCLES], 2 * f, 1) if f else ends[:CYCLES]
            for f in range(FIELDS)
        )
        for f in range(FIELDS):
            s = SOURCE_OF[f] * CYCLES
            block = out[f * BAND : f * BAND + CYCLES] + near_ref[
                s : s + CYCLES, p * 2 * CAZ : (p + 1) * 2 * CAZ
            ]
            for quad in range(QUADS):
                send_out[p * QUADS + quad, f * 4 : f * 4 + 4, :] = block[quad * 4 : quad * 4 + 4]
        for quad in range(QUADS):
            send_out[p * QUADS + quad, LINES : LINES + 4, :] = ends[quad * 4 : quad * 4 + 4]
        span = pl.ds(p * QUADS, QUADS)
        copies.append(pltpu.make_async_copy(send_out.at[span], send_hbm.at[span], sems.at[p]))
        copies[p].start()
    for copy in copies:
        copy.wait()


def rad_edges(rad, q_ref, rad_out):
    extra = jnp.where(rad == 0, 1, 0)
    lane = iota((32, CR), 1)
    packed = jnp.zeros((32, CR), F32)
    for f in range(FIELDS):
        for g in range(16):
            part = q_ref[f, g // 2, (g % 2) * 32 : (g % 2) * 32 + 32, :]
            spot = g * 8 + f
            packed = jnp.where(lane == spot, pltpu.roll(part, spot + extra, 1), packed)
    rad_out[...] = packed


def gas_body(
    rad_ref, odd_ref, az_ref, coef_ref, q_ref, first_ref, second_ref, az_first, az_second, rad_in, src_ref,
    cells_ref, _,
    sect_out, hot_ref, spread_ref,
):
    width = 4
    zero = jnp.zeros((), BF16)

    def scattered(i):
        for first in range(0, BLK_DEV, width):
            cols = slice(first * BLK, (first + width) * BLK)
            if i == 0:
                hot_ref[:, cols] = one_hot_rows(cells_ref, first, width)[0]
            mask = equals(CR, lane_row(cells_ref, first, width) & (CR - 1))
            row = jnp.concatenate([src_ref[i, first + j : first + j + 1, :] for j in range(width)], axis=1)
            high = row.astype(BF16)
            low = (row - high.astype(F32)).astype(BF16)
            spread_ref[i, 0:CR, cols] = jnp.where(mask, high, zero)
            spread_ref[i, CR:, cols] = jnp.where(mask, low, zero)
        total = lax.dot_general(hot_ref[...], spread_ref[i], NT, preferred_element_type=F32)
        return total[:, :CR] + total[:, CR:]

    rad = rad_ref[0]
    odd = odd_ref[0] == 1
    row = iota((CAZ, CR), 0)
    lane = iota((1, CR), 1)
    metric = 4.0 / ((rad * CR + lane).astype(F32) + 4.0)
    target = jnp.where(rad == 0, CR - 1, 0)
    odd_az = az_ref[0] % 2 == 1
    az_prev = jnp.where(odd_az, az_first[...], az_second[...])
    az_next = jnp.where(odd_az, az_second[...], az_first[...])
    added = {0: scattered(0)}
    for f in (0, 4, 1, 2, 3):
        if f in (0, 1, 2):
            added[f + 1] = scattered(f + 1)
        c = [coef_ref[f, i] for i in range(6)]
        mid = (1.0 - c[1] - c[5]) - c[3] * metric
        az_up_edge, az_down_edge = (0.5 * (c[2] + c[3])) * metric, (0.5 * (c[3] - c[2])) * metric
        az_up = jnp.where(row == CAZ - 1, 0.0, az_up_edge)
        az_down = jnp.where(row == 0, 0.0, az_down_edge)
        ax_up, ax_down = 0.5 * (c[0] + c[1]), 0.5 * (c[1] - c[0])
        rad_up = jnp.where(lane == CR - 1, 0.0, 0.5 * (c[4] + c[5]))
        rad_down = jnp.where(lane == 0, 0.0, 0.5 * (c[5] - c[4]))
        across = 0.5 * jnp.where(rad == 0, c[4] + c[5], c[5] - c[4])
        across = jnp.where(lane == target, across, 0.0)
        for a in range(CAX):
            q = q_ref[f, a]
            ahead = q_ref[f, a + 1] if a + 1 < CAX else jnp.where(odd, second_ref[f], first_ref[f])
            behind = q_ref[f, a - 1] if a else jnp.where(odd, first_ref[f], second_ref[f])
            edge = jnp.concatenate(
                [pltpu.roll(rad_in[...], (target + (2 * CR - ((2 * a + h) * 8 + f))) % CR, 1) for h in range(2)],
                axis=0,
            )
            sect_out[f, a] = (
                mid * q + ax_up * ahead + ax_down * behind
                + az_up * pltpu.roll(q, CAZ - 1, 0) + az_down * pltpu.roll(q, 1, 0)
                + rad_up * pltpu.roll(q, CR - 1, 1) + rad_down * pltpu.roll(q, 1, 1)
                + across * edge
                + added[SOURCE_OF[f]][a * CAZ : (a + 1) * CAZ]
            )
            sect_out[f, a, 0:1] += az_down_edge * az_prev[f, a : a + 1]
            sect_out[f, a, CAZ - 1 : CAZ] += az_up_edge * az_next[f, a : a + 1]


def lined(pieces, line_ref):
    low = iota((LINES, 2 * CAZ), 1) < CAZ
    for i in range(N_AZ // 2):
        t0, t1 = pieces(2 * i), pieces(2 * i + 1)
        cols = slice(i * 2 * CAZ, (i + 1) * 2 * CAZ)
        line_ref[0:LINES, cols] = jnp.where(low, t0, pltpu.roll(t1, CAZ, 1))
        line_ref[BAND : BAND + LINES, cols] = jnp.where(low, pltpu.roll(t0, CAZ, 1), t1)


def filter_body(
    az_ref, width_ref, basis_ref, turned_ref, got_ref, moved_ref,
    send_out, onward_out, line_ref, ends_ref, piece_ref,
):
    onward_out[...] = moved_ref[1]
    quad = az_ref[0] % QUADS
    low = iota((LINES, 2 * CAZ), 1) < CAZ
    line_ref[...] = jnp.zeros_like(line_ref)
    ends_ref[...] = jnp.zeros_like(ends_ref)
    for s in range(N_AZ):
        packed = got_ref[s, LINES : LINES + 4, :]
        for f in range(FIELDS):
            piece_ref[s, f * 4 : f * 4 + 4, :] = pltpu.roll(packed, 2 * CAZ - 2 * f, 1) if f else packed
    lined(lambda s: got_ref[s, 0:LINES, :], line_ref)
    lined(lambda s: piece_ref[s], ends_ref)
    z = iota((2 * BAND, NAZ), 1) % CAZ
    ends = ends_ref[...]
    lines = (
        line_ref[...]
        + jnp.where(z == CAZ - 1, pltpu.roll(ends, NAZ - 1, 1), 0.0)
        + jnp.where(z == 0, pltpu.roll(ends, 1, 1), 0.0)
    )
    rows = 2 * BAND
    both = jnp.concatenate(halves(lines), axis=0)
    whole = jnp.dot(both, turned_ref[...], preferred_element_type=F32)
    coefs = whole[:rows, :MODES] + whole[rows:, :MODES] + whole[:rows, MODES:]
    column = iota((rows, MODES), 1)
    cycle = iota((rows, MODES), 0) % 4
    mode = jnp.where(column < HALF, column, column - HALF + 1)
    width = jnp.zeros((rows, MODES), jnp.int32)
    for i in range(4):
        width = jnp.where(cycle == i, width_ref[quad * 4 + i], width)
    weight = jnp.where(mode == 0, 1.0 / NAZ, 2.0 / NAZ)
    coefs = coefs * jnp.where(mode < width, weight, 0.0)
    high, rest = halves(coefs)
    line_ref[...] = jnp.dot(
        jnp.concatenate([high, high], axis=1), basis_ref[...], preferred_element_type=F32
    ) + jnp.dot(rest, basis_ref[:MODES], preferred_element_type=F32)
    for i in range(N_AZ // 2):
        cols = slice(i * 2 * CAZ, (i + 1) * 2 * CAZ)
        t0, t1 = line_ref[0:LINES, cols], line_ref[BAND : BAND + LINES, cols]
        send_out[2 * i, 0:LINES] = jnp.where(low, t0, pltpu.roll(t1, CAZ, 1))
        send_out[2 * i + 1, 0:LINES] = jnp.where(low, pltpu.roll(t0, CAZ, 1), t1)


def merge_body(
    rad_ref, odd_ref, sect_ref, got_ref, stay_ref, moved_ref, onward_ref, gas_out, parcels_out, flip_ref
):
    odd = odd_ref[0] == 1
    parcels_out[:, 0:BLK_DEV, :] = stay_ref[...]
    first, second = moved_ref[0], onward_ref[...]
    parcels_out[:, BLK_DEV : BLK_DEV + MOVEB, :] = jnp.where(odd, first, second)
    parcels_out[:, BLK_DEV + MOVEB :, :] = jnp.where(odd, second, first)
    near = (iota((2 * CAZ, CR), 1) < CYCLES) & (rad_ref[0] == 0)
    tiles = []
    for pair in range(PAIRS):
        flip_ref[pair, FIELDS * CYCLES :, :] = jnp.zeros((CR - FIELDS * CYCLES, CR), F32)
        for f in range(FIELDS):
            for quad in range(QUADS):
                first = f * CYCLES + quad * 4
                flip_ref[pair, first : first + 4, :] = got_ref[pair * QUADS + quad, f * 4 : f * 4 + 4, :]
        tiles.append(flip_ref[pair].T)
    for f in range(FIELDS):
        for pair in range(PAIRS):
            moved = pltpu.roll(tiles[pair], CR - f * CYCLES, 1) if f else tiles[pair]
            kept = sect_ref[f, 2 * pair : 2 * pair + 2].reshape(2 * CAZ, CR)
            gas_out[f, 2 * pair : 2 * pair + 2] = jnp.where(near, moved, kept).reshape(2, CAZ, CR)


def shards(fields, coeffs, parcels, cells, counts, moves, widths):
    rad_index = lax.axis_index("rad").astype(jnp.int32).reshape(1)
    az_index = lax.axis_index("az").astype(jnp.int32).reshape(1)
    odd = (lax.axis_index("ax").astype(jnp.int32) % 2).reshape(1)
    n_ax, n_az, n_rad = (lax.axis_size(axis) for axis in ("ax", "az", "rad"))
    parcels = parcels.reshape(4, BLK_DEV, BLK)
    cells = cells.reshape(BLK_DEV, BLK)
    counts = counts.reshape(1)
    moves = moves.reshape(BLK_DEV)
    inner = [(i, i ^ 1) for i in range(n_ax)]
    outer = [(i, ((i + 1) ^ 1) - 1) for i in range(1, n_ax - 1)]
    along = [(i, i + 2) for i in range(0, n_ax - 2, 2)] + [(i, i - 2) for i in range(3, n_ax, 2)]
    inner_az = [(i, i ^ 1) for i in range(n_az)]
    outer_az = [(i, (((i + 1) ^ 1) - 1) % n_az) for i in range(n_az)]
    across = [(i, i ^ 1) for i in range(n_rad)]
    gas_shape = (FIELDS, CAX, CAZ, CR)

    first, second, az_first, az_second = call(
        edges_body, [(FIELDS, CAZ, CR)] * 2 + [(FIELDS, CAX, CR)] * 2, [SMEM, SMEM, VMEM], 10**6, 10**6, mib=4
    )(odd, az_index, fields)
    first = lax.ppermute(first, "ax", inner)
    second = lax.ppermute(second, "ax", outer)
    az_first = lax.ppermute(az_first, "az", inner_az)
    az_second = lax.ppermute(az_second, "az", outer_az)

    tiles, near = call(
        near_parcels_body,
        [(CR, ROWS), (4 * CYCLES, ROWS)],
        [SMEM] + [VMEM] * 3, 3 * 10**9, 2 * 10**6,
        [
            pltpu.VMEM((3, BLK_DEV, BLK), F32),
            pltpu.VMEM((ROWS, PARCELS), BF16),
            pltpu.VMEM((8 * CYCLES, PARCELS), BF16),
        ],
        mib=16,
    )(counts, fields, parcels, cells)

    (to_owner,) = call(
        near_body,
        [(N_AZ, LINES + 4, 2 * CAZ)],
        [SMEM, SMEM] + [VMEM] * 4, 10**7, 4 * 10**6,
        [
            pltpu.VMEM((N_AZ, LINES + 4, 2 * CAZ), F32),
            pltpu.SemaphoreType.DMA((PAIRS,)),
        ],
        mib=8,
        hbm_first=True,
    )(odd, coeffs, first, second, tiles, near)
    lines = lax.all_to_all(to_owner, "az", 0, 0, tiled=True)

    src, stay, leaving, rad_edge = call(
        parcels_body,
        [(4, BLK_DEV, BLK), (4, BLK_DEV, BLK), (2, 4, MOVEB, BLK), (32, CR)],
        [SMEM] * 4 + [VMEM] * 3, 6 * 10**9, 2 * 10**6,
        [
            pltpu.VMEM((3, BLK_DEV, BLK), F32),
            pltpu.VMEM((4, BLK_DEV, BLK), F32),
            pltpu.VMEM((2, 4, 2 * MOVEB, BLK), F32),
        ],
        mib=16,
    )(rad_index, odd, counts, moves, fields, parcels, cells)
    rad_got = lax.ppermute(rad_edge, "rad", across)
    moved = lax.ppermute(leaving, "ax", inner)

    basis, basis_turned = basis_parts()
    to_home, onward = call(
        filter_body,
        [(N_AZ, LINES, 2 * CAZ), (4, MOVEB, BLK)],
        [SMEM, SMEM] + [VMEM] * 4, 10**8, 10**6,
        [
            pltpu.VMEM((2 * BAND, NAZ), F32),
            pltpu.VMEM((2 * BAND, NAZ), F32),
            pltpu.VMEM((N_AZ, LINES, 2 * CAZ), F32),
        ],
        mib=6,
    )(az_index, widths, basis, basis_turned, lines, moved)
    filtered = lax.all_to_all(to_home, "az", 0, 0, tiled=True)
    onward = lax.ppermute(onward, "ax", along)

    (sect,) = call(
        gas_body, [gas_shape], [SMEM] * 4 + [VMEM] * 8 + [ANY], 8 * 10**9, 4 * 10**6,
        [pltpu.VMEM((ROWS, PARCELS), BF16), pltpu.VMEM((4, 2 * CR, PARCELS), BF16)],
        mib=24,
    )(rad_index, odd, az_index, coeffs, fields, first, second, az_first, az_second, rad_got, src, cells, to_home)

    gas_out, parcels_out = call(
        merge_body,
        [gas_shape, (4, BLK_DEV + 2 * MOVEB, BLK)],
        [SMEM, SMEM] + [VMEM] * 5, 10**6, 4 * 10**6,
        [pltpu.VMEM((PAIRS, CR, CR), F32)],
        mib=8,
    )(rad_index, odd, sect, filtered, stay, moved, onward)
    return gas_out, parcels_out.reshape(4, BLK_DEV + 2 * MOVEB, 1, BLK)


def solution(mesh):
    block = P(None, "ax", "az", "rad")
    flat = P("ax", "az", "rad")
    return jax.shard_map(
        shards,
        mesh=mesh,
        in_specs=(block, P(), block, flat, flat, flat, P()),
        out_specs=(block, block),
        check_vma=False,
    )
```

```python
import math

import jax
import jax.numpy as jnp
import ml_dtypes
import numpy as np
from jax import lax
from jax.experimental import pallas as pl
from jax.experimental.pallas import tpu as pltpu
from jax.sharding import PartitionSpec as P

FIELDS = 5
CYCLES = 16
MODES = 128
HALF = MODES // 2
BLK = 128
BLK_DEV = 32
MOVEB = 4
CAX, CAZ, CR = 8, 64, 128
ROWS = CAX * CAZ
PARCELS = BLK * BLK_DEV
NAZ = 1024
N_AZ = 16
PAIRS = CAX // 2
QUADS = CYCLES // 4
LINES = FIELDS * 4
BAND = 24

STEP_SIZE = 0.5
EVAP_RATE = 0.5
COUPLING = 0.5

F32 = jnp.float32
BF16 = jnp.bfloat16
HIGHEST = lax.Precision.HIGHEST
VMEM = pl.BlockSpec(memory_space=pltpu.VMEM)
SMEM = pl.BlockSpec(memory_space=pltpu.SMEM)
ANY = pl.BlockSpec(memory_space=pl.ANY)
HBM = pl.BlockSpec(memory_space=pltpu.HBM)
NT = (((1,), (1,)), ((), ()))


def basis_parts():
    column = np.arange(MODES)
    mode = np.where(column < HALF, column, column - HALF + 1)
    phases = (mode[:, None] * np.arange(NAZ)[None, :]) % NAZ
    angles = phases.astype(np.float32) * np.float32(2.0 * math.pi / NAZ)
    table = np.where(column[:, None] < HALF, np.cos(angles), np.sin(angles)).astype(np.float32)
    high = table.astype(ml_dtypes.bfloat16)
    low = (table - high.astype(np.float32)).astype(ml_dtypes.bfloat16)
    parts = np.concatenate([high, low])
    return jnp.asarray(parts), jnp.asarray(np.ascontiguousarray(parts.T))


def iota(shape, axis):
    return lax.broadcasted_iota(jnp.int32, shape, axis)


def halves(value):
    high = value.astype(BF16)
    return high, (value - high.astype(F32)).astype(BF16)


def call(body, out_shape, in_specs, flops, nbytes, scratch=(), mib=24, hbm_first=False):
    return pl.pallas_call(
        body,
        out_shape=[jax.ShapeDtypeStruct(shape, F32) for shape in out_shape],
        in_specs=in_specs,
        out_specs=[HBM if hbm_first and i == 0 else VMEM for i in range(len(out_shape))],
        scratch_shapes=list(scratch),
        compiler_params=pltpu.CompilerParams(vmem_limit_bytes=mib * 2**20),
        cost_estimate=pl.CostEstimate(flops=flops, bytes_accessed=nbytes, transcendentals=0),
    )


def turned(parts):
    lane = iota((2 * CAZ, CR), 1)
    packed = jnp.zeros((2 * CAZ, CR), F32)
    for f, part in enumerate(parts):
        moved = pltpu.roll(part, f * BAND, 1) if f else part
        packed = jnp.where((lane >= f * BAND) & (lane < (f + 1) * BAND), moved, packed)
    return packed.T


def edges_body(odd_ref, az_ref, q_ref, first_out, second_out, az_first, az_second, tiles_out):
    odd, odd_az = odd_ref[0] == 1, az_ref[0] % 2 == 1
    low, high = q_ref[:, 0], q_ref[:, CAX - 1]
    first_out[...] = jnp.where(odd, low, high)
    second_out[...] = jnp.where(odd, high, low)
    low, high = q_ref[:, :, 0, :], q_ref[:, :, CAZ - 1, :]
    az_first[...] = jnp.where(odd_az, low, high)
    az_second[...] = jnp.where(odd_az, high, low)
    for p in range(PAIRS):
        tiles_out[:, p * 2 * CAZ : (p + 1) * 2 * CAZ] = turned(
            [q_ref[f, 2 * p : 2 * p + 2].reshape(2 * CAZ, CR) for f in range(FIELDS)]
        )


def lane_row(cells_ref, first, blocks):
    return jnp.concatenate([cells_ref[first + i : first + i + 1, :] for i in range(blocks)], axis=1)


def equals(count, row):
    numbers = iota((count, row.shape[1]), 0).astype(F32).astype(BF16)
    return numbers == row.astype(F32).astype(BF16)


def one_hot_rows(cells_ref, first, blocks):
    cells = lane_row(cells_ref, first, blocks)
    one, zero = jnp.ones((), BF16), jnp.zeros((), BF16)
    half = ROWS // 2
    parts = [jnp.where(equals(half, (cells >> 7) - half * i), one, zero) for i in range(2)]
    return jnp.concatenate(parts, axis=0), cells & (CR - 1)


def step(count_ref, parcel_ref, gas_ref):
    slot = iota((BLK_DEV, BLK), 0) * BLK + iota((BLK_DEV, BLK), 1)
    alive = slot < count_ref[0]
    diam = parcel_ref[3]
    vel = [parcel_ref[i] for i in range(3)]
    gas = [gas_ref[i] for i in range(3)]
    slip = [g - u for g, u in zip(gas, vel)]
    slip_sq = slip[0] * slip[0] + slip[1] * slip[1] + slip[2] * slip[2]
    new_vel = [(u * diam + STEP_SIZE * g) / (diam + STEP_SIZE) for u, g in zip(vel, gas)]
    new_diam = diam / (1.0 + STEP_SIZE * EVAP_RATE * (1.0 + slip_sq))
    sources = [(diam - new_diam) * COUPLING] + [
        -(diam * (v - u)) * COUPLING for v, u in zip(new_vel, vel)
    ]
    state = [jnp.where(alive, s, 0.0) for s in new_vel + [new_diam]]
    return state, [jnp.where(alive, s, 0.0) for s in sources]


def pick(rows, first, spans, mask, gas_ref):
    for f, (start, stop) in enumerate(spans):
        found = jnp.sum(jnp.where(mask, rows[start:stop], 0.0), axis=0, keepdims=True)
        for i in range(4):
            gas_ref[f, first + i : first + i + 1, :] = found[:, i * BLK : (i + 1) * BLK]


def parcels_body(
    rad_ref, odd_ref, count_ref, move_ref, q_ref, parcel_ref, cells_ref,
    src_out, stay_out, leave_out, rad_out, gas_ref, state_ref, leave_ref,
):
    rad_edges(rad_ref[0], q_ref, rad_out)
    table = jnp.concatenate(
        [jnp.concatenate(halves(q_ref[f + 1].reshape(ROWS, CR).T), axis=1) for f in range(3)], axis=0
    )
    spans = [(f * CR, (f + 1) * CR) for f in range(3)]
    ready = one_hot_rows(cells_ref, 0, 4)
    for first in range(0, BLK_DEV, 4):
        hot, lanes = ready
        rows = jnp.dot(table, jnp.concatenate([hot, hot], axis=0), preferred_element_type=F32)
        if first + 4 < BLK_DEV:
            ready = one_hot_rows(cells_ref, first + 4, 4)
        pick(rows, first, spans, iota((CR, 4 * BLK), 0) == lanes, gas_ref)
    state, sources = step(count_ref, parcel_ref, gas_ref)
    for i in range(4):
        src_out[i] = sources[i]
        state_ref[i] = state[i]
    leave_ref[...] = jnp.zeros_like(leave_ref)
    up, down, spare = jnp.int32(0), jnp.int32(0), 2 * MOVEB - 1
    for block in range(BLK_DEV):
        move = move_ref[block]
        row = state_ref[:, block : block + 1, :]
        stay_out[:, block : block + 1, :] = jnp.where(move == 0, row, 0.0)
        to_up = jnp.where(move == 1, jnp.minimum(up, MOVEB - 1), spare)
        to_down = jnp.where(move == -1, jnp.minimum(down, MOVEB - 1), spare)
        leave_ref[0, :, pl.ds(to_up, 1), :] = row
        leave_ref[1, :, pl.ds(to_down, 1), :] = row
        up = up + jnp.where(move == 1, 1, 0)
        down = down + jnp.where(move == -1, 1, 0)
    odd = odd_ref[0] == 1
    up, down = leave_ref[0, :, :MOVEB], leave_ref[1, :, :MOVEB]
    leave_out[0] = jnp.where(odd, down, up)
    leave_out[1] = jnp.where(odd, up, down)


SOURCE_OF = (0, 1, 2, 3, 0)


def near_parcels_body(count_ref, tiles_ref, parcel_ref, cells_ref, near_out, gas_ref, hot_ref, spread_ref):
    start = 16
    table = jnp.concatenate(halves(tiles_ref[start : 4 * BAND]), axis=0)
    depth = 4 * BAND - start
    spans = [((f + 1) * BAND - start, (f + 1) * BAND - start + CYCLES) for f in range(3)]
    for first in range(0, BLK_DEV, 4):
        hot, lanes = one_hot_rows(cells_ref, first, 4)
        hot_ref[:, first * BLK : (first + 4) * BLK] = hot
        rows = jnp.dot(table, hot, preferred_element_type=F32)
        rows = rows[:depth] + rows[depth:]
        pick(rows, first, spans, iota((CYCLES, 4 * BLK), 0) == lanes, gas_ref)
    _, sources = step(count_ref, parcel_ref, gas_ref)
    rows = [s.astype(BF16) for s in sources]
    rows = [r.astype(F32) for r in rows] + [s - r.astype(F32) for s, r in zip(sources, rows)]
    zero = jnp.zeros((), BF16)
    for first in range(0, BLK_DEV, 4):
        mask = equals(CYCLES, lane_row(cells_ref, first, 4) & (CR - 1))
        for i, row in enumerate(rows):
            row = jnp.concatenate([row[first + j : first + j + 1] for j in range(4)], axis=1).astype(BF16)
            spread_ref[i * CYCLES : (i + 1) * CYCLES, first * BLK : (first + 4) * BLK] = jnp.where(mask, row, zero)
    total = lax.dot_general(spread_ref[...], hot_ref[...], NT, preferred_element_type=F32)
    near_out[...] = total[: 4 * CYCLES] + total[4 * CYCLES :]


def near_body(
    odd_ref, coef_ref, first_ref, second_ref, tiles_ref, near_ref, send_hbm, send_out, sems
):
    copies = []
    lane = iota((CR, 2 * CAZ), 1)
    z = lane % CAZ
    tiles = [tiles_ref[:, p * 2 * CAZ : (p + 1) * 2 * CAZ] for p in range(PAIRS)]
    odd = odd_ref[0] == 1
    first, second = first_ref[...], second_ref[...]
    before, after = jnp.where(odd, first, second), jnp.where(odd, second, first)
    halo = turned([jnp.concatenate([before[f], after[f]], axis=0) for f in range(FIELDS)])

    column = iota((CR, 1), 0)
    radius = column
    c = [jnp.zeros((CR, 1), F32) for _ in range(6)]
    for f in range(FIELDS):
        here = (column >= f * BAND) & (column < (f + 1) * BAND)
        radius = jnp.where(here, column - f * BAND, radius)
        c = [jnp.where(here, coef_ref[f, i], c[i]) for i in range(6)]
    metric = 4.0 / (radius.astype(F32) + 4.0)
    mid = (1.0 - c[1] - c[5]) - c[3] * metric
    az_up, az_down = (0.5 * (c[2] + c[3])) * metric, (0.5 * (c[3] - c[2])) * metric
    ax_up, ax_down = 0.5 * (c[0] + c[1]), 0.5 * (c[1] - c[0])
    rad_up = 0.5 * (c[4] + c[5])
    rad_down = jnp.where(radius == 0, 0.0, 0.5 * (c[5] - c[4]))
    low = lane < CAZ
    swapped = [pltpu.roll(t, CAZ, 1) for t in tiles]
    for p in range(PAIRS):
        q = tiles[p]
        ahead = jnp.where(low, swapped[p], swapped[p + 1] if p + 1 < PAIRS else halo)
        behind = jnp.where(low, swapped[p - 1] if p else halo, swapped[p])
        az_a = jnp.where(z == CAZ - 1, 0.0, pltpu.roll(q, 2 * CAZ - 1, 1))
        az_b = jnp.where(z == 0, 0.0, pltpu.roll(q, 1, 1))
        r_a = pltpu.roll(q, CR - 1, 0)
        r_b = pltpu.roll(q, 1, 0)
        out = (
            mid * q + ax_up * ahead + ax_down * behind + az_up * az_a + az_down * az_b
            + rad_up * r_a + rad_down * r_b
        )
        ends = jnp.where(z == 0, az_up * q, jnp.where(z == CAZ - 1, az_down * q, 0.0))
        ends = sum(
            pltpu.roll(ends[f * BAND : f * BAND + CYCLES], 2 * f, 1) if f else ends[:CYCLES]
            for f in range(FIELDS)
        )
        for f in range(FIELDS):
            s = SOURCE_OF[f] * CYCLES
            block = out[f * BAND : f * BAND + CYCLES] + near_ref[
                s : s + CYCLES, p * 2 * CAZ : (p + 1) * 2 * CAZ
            ]
            for quad in range(QUADS):
                send_out[p * QUADS + quad, f * 4 : f * 4 + 4, :] = block[quad * 4 : quad * 4 + 4]
        for quad in range(QUADS):
            send_out[p * QUADS + quad, LINES : LINES + 4, :] = ends[quad * 4 : quad * 4 + 4]
        span = pl.ds(p * QUADS, QUADS)
        copies.append(pltpu.make_async_copy(send_out.at[span], send_hbm.at[span], sems.at[p]))
        copies[p].start()
    for copy in copies:
        copy.wait()


def rad_edges(rad, q_ref, rad_out):
    extra = jnp.where(rad == 0, 1, 0)
    lane = iota((32, CR), 1)
    packed = jnp.zeros((32, CR), F32)
    for f in range(FIELDS):
        for g in range(16):
            part = q_ref[f, g // 2, (g % 2) * 32 : (g % 2) * 32 + 32, :]
            spot = g * 8 + f
            packed = jnp.where(lane == spot, pltpu.roll(part, spot + extra, 1), packed)
    rad_out[...] = packed


def gas_body(
    rad_ref, odd_ref, az_ref, coef_ref, q_ref, first_ref, second_ref, az_first, az_second, rad_in, src_ref,
    cells_ref, _,
    sect_out, hot_ref, spread_ref,
):
    width = 4
    zero = jnp.zeros((), BF16)

    def scattered(i):
        for first in range(0, BLK_DEV, width):
            cols = slice(first * BLK, (first + width) * BLK)
            if i == 0:
                hot_ref[:, cols] = one_hot_rows(cells_ref, first, width)[0]
            mask = equals(CR, lane_row(cells_ref, first, width) & (CR - 1))
            row = jnp.concatenate([src_ref[i, first + j : first + j + 1, :] for j in range(width)], axis=1)
            high = row.astype(BF16)
            low = (row - high.astype(F32)).astype(BF16)
            spread_ref[i, 0:CR, cols] = jnp.where(mask, high, zero)
            spread_ref[i, CR:, cols] = jnp.where(mask, low, zero)
        total = lax.dot_general(hot_ref[...], spread_ref[i], NT, preferred_element_type=F32)
        return total[:, :CR] + total[:, CR:]

    rad = rad_ref[0]
    odd = odd_ref[0] == 1
    row = iota((CAZ, CR), 0)
    lane = iota((1, CR), 1)
    metric = 4.0 / ((rad * CR + lane).astype(F32) + 4.0)
    target = jnp.where(rad == 0, CR - 1, 0)
    odd_az = az_ref[0] % 2 == 1
    az_prev = jnp.where(odd_az, az_first[...], az_second[...])
    az_next = jnp.where(odd_az, az_second[...], az_first[...])
    added = {0: scattered(0)}
    for f in (0, 4, 1, 2, 3):
        if f in (0, 1, 2):
            added[f + 1] = scattered(f + 1)
        c = [coef_ref[f, i] for i in range(6)]
        mid = (1.0 - c[1] - c[5]) - c[3] * metric
        az_up_edge, az_down_edge = (0.5 * (c[2] + c[3])) * metric, (0.5 * (c[3] - c[2])) * metric
        az_up = jnp.where(row == CAZ - 1, 0.0, az_up_edge)
        az_down = jnp.where(row == 0, 0.0, az_down_edge)
        ax_up, ax_down = 0.5 * (c[0] + c[1]), 0.5 * (c[1] - c[0])
        rad_up = jnp.where(lane == CR - 1, 0.0, 0.5 * (c[4] + c[5]))
        rad_down = jnp.where(lane == 0, 0.0, 0.5 * (c[5] - c[4]))
        across = 0.5 * jnp.where(rad == 0, c[4] + c[5], c[5] - c[4])
        across = jnp.where(lane == target, across, 0.0)
        for a in range(CAX):
            q = q_ref[f, a]
            ahead = q_ref[f, a + 1] if a + 1 < CAX else jnp.where(odd, second_ref[f], first_ref[f])
            behind = q_ref[f, a - 1] if a else jnp.where(odd, first_ref[f], second_ref[f])
            edge = jnp.concatenate(
                [pltpu.roll(rad_in[...], (target + (2 * CR - ((2 * a + h) * 8 + f))) % CR, 1) for h in range(2)],
                axis=0,
            )
            sect_out[f, a] = (
                mid * q + ax_up * ahead + ax_down * behind
                + az_up * pltpu.roll(q, CAZ - 1, 0) + az_down * pltpu.roll(q, 1, 0)
                + rad_up * pltpu.roll(q, CR - 1, 1) + rad_down * pltpu.roll(q, 1, 1)
                + across * edge
                + added[SOURCE_OF[f]][a * CAZ : (a + 1) * CAZ]
            )
            sect_out[f, a, 0:1] += az_down_edge * az_prev[f, a : a + 1]
            sect_out[f, a, CAZ - 1 : CAZ] += az_up_edge * az_next[f, a : a + 1]


def lined(pieces, line_ref):
    low = iota((LINES, 2 * CAZ), 1) < CAZ
    for i in range(N_AZ // 2):
        t0, t1 = pieces(2 * i), pieces(2 * i + 1)
        cols = slice(i * 2 * CAZ, (i + 1) * 2 * CAZ)
        line_ref[0:LINES, cols] = jnp.where(low, t0, pltpu.roll(t1, CAZ, 1))
        line_ref[BAND : BAND + LINES, cols] = jnp.where(low, pltpu.roll(t0, CAZ, 1), t1)


def filter_body(
    az_ref, width_ref, basis_ref, turned_ref, got_ref, moved_ref,
    send_out, onward_out, line_ref, ends_ref, piece_ref,
):
    onward_out[...] = moved_ref[1]
    quad = az_ref[0] % QUADS
    low = iota((LINES, 2 * CAZ), 1) < CAZ
    line_ref[...] = jnp.zeros_like(line_ref)
    ends_ref[...] = jnp.zeros_like(ends_ref)
    for s in range(N_AZ):
        packed = got_ref[s, LINES : LINES + 4, :]
        for f in range(FIELDS):
            piece_ref[s, f * 4 : f * 4 + 4, :] = pltpu.roll(packed, 2 * CAZ - 2 * f, 1) if f else packed
    lined(lambda s: got_ref[s, 0:LINES, :], line_ref)
    lined(lambda s: piece_ref[s], ends_ref)
    z = iota((2 * BAND, NAZ), 1) % CAZ
    ends = ends_ref[...]
    lines = (
        line_ref[...]
        + jnp.where(z == CAZ - 1, pltpu.roll(ends, NAZ - 1, 1), 0.0)
        + jnp.where(z == 0, pltpu.roll(ends, 1, 1), 0.0)
    )
    rows = 2 * BAND
    both = jnp.concatenate(halves(lines), axis=0)
    whole = jnp.dot(both, turned_ref[...], preferred_element_type=F32)
    coefs = whole[:rows, :MODES] + whole[rows:, :MODES] + whole[:rows, MODES:]
    column = iota((rows, MODES), 1)
    cycle = iota((rows, MODES), 0) % 4
    mode = jnp.where(column < HALF, column, column - HALF + 1)
    width = jnp.zeros((rows, MODES), jnp.int32)
    for i in range(4):
        width = jnp.where(cycle == i, width_ref[quad * 4 + i], width)
    weight = jnp.where(mode == 0, 1.0 / NAZ, 2.0 / NAZ)
    coefs = coefs * jnp.where(mode < width, weight, 0.0)
    high, rest = halves(coefs)
    line_ref[...] = jnp.dot(
        jnp.concatenate([high, high], axis=1), basis_ref[...], preferred_element_type=F32
    ) + jnp.dot(rest, basis_ref[:MODES], preferred_element_type=F32)
    for i in range(N_AZ // 2):
        cols = slice(i * 2 * CAZ, (i + 1) * 2 * CAZ)
        t0, t1 = line_ref[0:LINES, cols], line_ref[BAND : BAND + LINES, cols]
        send_out[2 * i, 0:LINES] = jnp.where(low, t0, pltpu.roll(t1, CAZ, 1))
        send_out[2 * i + 1, 0:LINES] = jnp.where(low, pltpu.roll(t0, CAZ, 1), t1)


def merge_body(
    rad_ref, odd_ref, sect_ref, got_ref, stay_ref, moved_ref, onward_ref, gas_out, parcels_out, flip_ref
):
    odd = odd_ref[0] == 1
    parcels_out[:, 0:BLK_DEV, :] = stay_ref[...]
    first, second = moved_ref[0], onward_ref[...]
    parcels_out[:, BLK_DEV : BLK_DEV + MOVEB, :] = jnp.where(odd, first, second)
    parcels_out[:, BLK_DEV + MOVEB :, :] = jnp.where(odd, second, first)
    near = (iota((2 * CAZ, CR), 1) < CYCLES) & (rad_ref[0] == 0)
    tiles = []
    for pair in range(PAIRS):
        flip_ref[pair, FIELDS * CYCLES :, :] = jnp.zeros((CR - FIELDS * CYCLES, CR), F32)
        for f in range(FIELDS):
            for quad in range(QUADS):
                first = f * CYCLES + quad * 4
                flip_ref[pair, first : first + 4, :] = got_ref[pair * QUADS + quad, f * 4 : f * 4 + 4, :]
        tiles.append(flip_ref[pair].T)
    for f in range(FIELDS):
        for pair in range(PAIRS):
            moved = pltpu.roll(tiles[pair], CR - f * CYCLES, 1) if f else tiles[pair]
            kept = sect_ref[f, 2 * pair : 2 * pair + 2].reshape(2 * CAZ, CR)
            gas_out[f, 2 * pair : 2 * pair + 2] = jnp.where(near, moved, kept).reshape(2, CAZ, CR)


def shards(fields, coeffs, parcels, cells, counts, moves, widths):
    rad_index = lax.axis_index("rad").astype(jnp.int32).reshape(1)
    az_index = lax.axis_index("az").astype(jnp.int32).reshape(1)
    odd = (lax.axis_index("ax").astype(jnp.int32) % 2).reshape(1)
    n_ax, n_az, n_rad = (lax.axis_size(axis) for axis in ("ax", "az", "rad"))
    parcels = parcels.reshape(4, BLK_DEV, BLK)
    cells = cells.reshape(BLK_DEV, BLK)
    counts = counts.reshape(1)
    moves = moves.reshape(BLK_DEV)
    inner = [(i, i ^ 1) for i in range(n_ax)]
    outer = [(i, ((i + 1) ^ 1) - 1) for i in range(1, n_ax - 1)]
    along = [(i, i + 2) for i in range(0, n_ax - 2, 2)] + [(i, i - 2) for i in range(3, n_ax, 2)]
    inner_az = [(i, i ^ 1) for i in range(n_az)]
    outer_az = [(i, (((i + 1) ^ 1) - 1) % n_az) for i in range(n_az)]
    across = [(i, i ^ 1) for i in range(n_rad)]
    gas_shape = (FIELDS, CAX, CAZ, CR)

    first, second, az_first, az_second, tiles = call(
        edges_body, [(FIELDS, CAZ, CR)] * 2 + [(FIELDS, CAX, CR)] * 2 + [(CR, ROWS)], [SMEM, SMEM, VMEM], 10**6, 10**6, mib=4
    )(odd, az_index, fields)
    first = lax.ppermute(first, "ax", inner)
    second = lax.ppermute(second, "ax", outer)
    az_first = lax.ppermute(az_first, "az", inner_az)
    az_second = lax.ppermute(az_second, "az", outer_az)

    (near,) = call(
        near_parcels_body,
        [(4 * CYCLES, ROWS)],
        [SMEM] + [VMEM] * 3, 3 * 10**9, 2 * 10**6,
        [
            pltpu.VMEM((3, BLK_DEV, BLK), F32),
            pltpu.VMEM((ROWS, PARCELS), BF16),
            pltpu.VMEM((8 * CYCLES, PARCELS), BF16),
        ],
        mib=16,
    )(counts, tiles, parcels, cells)

    (to_owner,) = call(
        near_body,
        [(N_AZ, LINES + 4, 2 * CAZ)],
        [SMEM, SMEM] + [VMEM] * 4, 10**7, 4 * 10**6,
        [
            pltpu.VMEM((N_AZ, LINES + 4, 2 * CAZ), F32),
            pltpu.SemaphoreType.DMA((PAIRS,)),
        ],
        mib=8,
        hbm_first=True,
    )(odd, coeffs, first, second, tiles, near)
    lines = lax.all_to_all(to_owner, "az", 0, 0, tiled=True)

    src, stay, leaving, rad_edge = call(
        parcels_body,
        [(4, BLK_DEV, BLK), (4, BLK_DEV, BLK), (2, 4, MOVEB, BLK), (32, CR)],
        [SMEM] * 4 + [VMEM] * 3, 6 * 10**9, 2 * 10**6,
        [
            pltpu.VMEM((3, BLK_DEV, BLK), F32),
            pltpu.VMEM((4, BLK_DEV, BLK), F32),
            pltpu.VMEM((2, 4, 2 * MOVEB, BLK), F32),
        ],
        mib=16,
    )(rad_index, odd, counts, moves, fields, parcels, cells)
    rad_got = lax.ppermute(rad_edge, "rad", across)
    moved = lax.ppermute(leaving, "ax", inner)

    basis, basis_turned = basis_parts()
    to_home, onward = call(
        filter_body,
        [(N_AZ, LINES, 2 * CAZ), (4, MOVEB, BLK)],
        [SMEM, SMEM] + [VMEM] * 4, 10**8, 10**6,
        [
            pltpu.VMEM((2 * BAND, NAZ), F32),
            pltpu.VMEM((2 * BAND, NAZ), F32),
            pltpu.VMEM((N_AZ, LINES, 2 * CAZ), F32),
        ],
        mib=6,
    )(az_index, widths, basis, basis_turned, lines, moved)
    filtered = lax.all_to_all(to_home, "az", 0, 0, tiled=True)
    onward = lax.ppermute(onward, "ax", along)

    (sect,) = call(
        gas_body, [gas_shape], [SMEM] * 4 + [VMEM] * 8 + [ANY], 8 * 10**9, 4 * 10**6,
        [pltpu.VMEM((ROWS, PARCELS), BF16), pltpu.VMEM((4, 2 * CR, PARCELS), BF16)],
        mib=24,
    )(rad_index, odd, az_index, coeffs, fields, first, second, az_first, az_second, rad_got, src, cells, to_home)

    gas_out, parcels_out = call(
        merge_body,
        [gas_shape, (4, BLK_DEV + 2 * MOVEB, BLK)],
        [SMEM, SMEM] + [VMEM] * 5, 10**6, 4 * 10**6,
        [pltpu.VMEM((PAIRS, CR, CR), F32)],
        mib=8,
    )(rad_index, odd, sect, filtered, stay, moved, onward)
    return gas_out, parcels_out.reshape(4, BLK_DEV + 2 * MOVEB, 1, BLK)


def solution(mesh):
    block = P(None, "ax", "az", "rad")
    flat = P("ax", "az", "rad")
    return jax.shard_map(
        shards,
        mesh=mesh,
        in_specs=(block, P(), block, flat, flat, flat, P()),
        out_specs=(block, block),
        check_vma=False,
    )
```

```python
import math

import jax
import jax.numpy as jnp
import ml_dtypes
import numpy as np
from jax import lax
from jax.experimental import pallas as pl
from jax.experimental.pallas import tpu as pltpu
from jax.sharding import PartitionSpec as P

FIELDS = 5
CYCLES = 16
MODES = 128
HALF = MODES // 2
BLK = 128
BLK_DEV = 32
MOVEB = 4
CAX, CAZ, CR = 8, 64, 128
ROWS = CAX * CAZ
PARCELS = BLK * BLK_DEV
NAZ = 1024
N_AZ = 16
PAIRS = CAX // 2
QUADS = CYCLES // 4
LINES = FIELDS * 4
BAND = 24

STEP_SIZE = 0.5
EVAP_RATE = 0.5
COUPLING = 0.5

F32 = jnp.float32
BF16 = jnp.bfloat16
HIGHEST = lax.Precision.HIGHEST
VMEM = pl.BlockSpec(memory_space=pltpu.VMEM)
SMEM = pl.BlockSpec(memory_space=pltpu.SMEM)
ANY = pl.BlockSpec(memory_space=pl.ANY)
HBM = pl.BlockSpec(memory_space=pltpu.HBM)
NT = (((1,), (1,)), ((), ()))


def basis_parts():
    column = np.arange(MODES)
    mode = np.where(column < HALF, column, column - HALF + 1)
    phases = (mode[:, None] * np.arange(NAZ)[None, :]) % NAZ
    angles = phases.astype(np.float32) * np.float32(2.0 * math.pi / NAZ)
    table = np.where(column[:, None] < HALF, np.cos(angles), np.sin(angles)).astype(np.float32)
    high = table.astype(ml_dtypes.bfloat16)
    low = (table - high.astype(np.float32)).astype(ml_dtypes.bfloat16)
    parts = np.concatenate([high, low])
    return jnp.asarray(parts), jnp.asarray(np.ascontiguousarray(parts.T))


def iota(shape, axis):
    return lax.broadcasted_iota(jnp.int32, shape, axis)


def halves(value):
    high = value.astype(BF16)
    return high, (value - high.astype(F32)).astype(BF16)


def call(body, out_shape, in_specs, flops, nbytes, scratch=(), mib=24, hbm_first=False):
    return pl.pallas_call(
        body,
        out_shape=[jax.ShapeDtypeStruct(shape, F32) for shape in out_shape],
        in_specs=in_specs,
        out_specs=[HBM if hbm_first and i == 0 else VMEM for i in range(len(out_shape))],
        scratch_shapes=list(scratch),
        compiler_params=pltpu.CompilerParams(vmem_limit_bytes=mib * 2**20),
        cost_estimate=pl.CostEstimate(flops=flops, bytes_accessed=nbytes, transcendentals=0),
    )


def turned(parts):
    lane = iota((2 * CAZ, CR), 1)
    packed = jnp.zeros((2 * CAZ, CR), F32)
    for f, part in enumerate(parts):
        moved = pltpu.roll(part, f * BAND, 1) if f else part
        packed = jnp.where((lane >= f * BAND) & (lane < (f + 1) * BAND), moved, packed)
    return packed.T


def rad_edges(rad, q_ref, rad_out):
    extra = jnp.where(rad == 0, 1, 0)
    lane = iota((32, CR), 1)
    packed = jnp.zeros((32, CR), F32)
    for f in range(FIELDS):
        for g in range(16):
            part = q_ref[f, g // 2, (g % 2) * 32 : (g % 2) * 32 + 32, :]
            spot = g * 8 + f
            packed = jnp.where(lane == spot, pltpu.roll(part, spot + extra, 1), packed)
    rad_out[...] = packed


def edges_body(
    rad_ref, odd_ref, az_ref, q_ref, first_out, second_out, az_first, az_second, tiles_out, rad_out
):
    rad_edges(rad_ref[0], q_ref, rad_out)
    odd, odd_az = odd_ref[0] == 1, az_ref[0] % 2 == 1
    low, high = q_ref[:, 0], q_ref[:, CAX - 1]
    first_out[...] = jnp.where(odd, low, high)
    second_out[...] = jnp.where(odd, high, low)
    low, high = q_ref[:, :, 0, :], q_ref[:, :, CAZ - 1, :]
    az_first[...] = jnp.where(odd_az, low, high)
    az_second[...] = jnp.where(odd_az, high, low)
    for p in range(PAIRS):
        tiles_out[:, p * 2 * CAZ : (p + 1) * 2 * CAZ] = turned(
            [q_ref[f, 2 * p : 2 * p + 2].reshape(2 * CAZ, CR) for f in range(FIELDS)]
        )


def lane_row(cells_ref, first, blocks):
    return jnp.concatenate([cells_ref[first + i : first + i + 1, :] for i in range(blocks)], axis=1)


def equals(count, row):
    numbers = iota((count, row.shape[1]), 0).astype(F32).astype(BF16)
    return numbers == row.astype(F32).astype(BF16)


def one_hot_rows(cells_ref, first, blocks):
    cells = lane_row(cells_ref, first, blocks)
    one, zero = jnp.ones((), BF16), jnp.zeros((), BF16)
    half = ROWS // 2
    parts = [jnp.where(equals(half, (cells >> 7) - half * i), one, zero) for i in range(2)]
    return jnp.concatenate(parts, axis=0), cells & (CR - 1)


def step(count_ref, parcel_ref, gas_ref):
    slot = iota((BLK_DEV, BLK), 0) * BLK + iota((BLK_DEV, BLK), 1)
    alive = slot < count_ref[0, 0, 0]
    diam = parcel_ref[3]
    vel = [parcel_ref[i] for i in range(3)]
    gas = [gas_ref[i] for i in range(3)]
    slip = [g - u for g, u in zip(gas, vel)]
    slip_sq = slip[0] * slip[0] + slip[1] * slip[1] + slip[2] * slip[2]
    new_vel = [(u * diam + STEP_SIZE * g) / (diam + STEP_SIZE) for u, g in zip(vel, gas)]
    new_diam = diam / (1.0 + STEP_SIZE * EVAP_RATE * (1.0 + slip_sq))
    sources = [(diam - new_diam) * COUPLING] + [
        -(diam * (v - u)) * COUPLING for v, u in zip(new_vel, vel)
    ]
    state = [jnp.where(alive, s, 0.0) for s in new_vel + [new_diam]]
    return state, [jnp.where(alive, s, 0.0) for s in sources]


def pick(rows, first, spans, mask, gas_ref):
    for f, (start, stop) in enumerate(spans):
        found = jnp.sum(jnp.where(mask, rows[start:stop], 0.0), axis=0, keepdims=True)
        for i in range(4):
            gas_ref[f, first + i : first + i + 1, :] = found[:, i * BLK : (i + 1) * BLK]


def parcels_body(
    odd_ref, count_ref, move_ref, q_ref, parcel_ref, cells_ref,
    src_out, stay_out, leave_out, gas_ref, state_ref, leave_ref,
):
    table = jnp.concatenate(
        [jnp.concatenate(halves(q_ref[f + 1].reshape(ROWS, CR).T), axis=1) for f in range(3)], axis=0
    )
    spans = [(f * CR, (f + 1) * CR) for f in range(3)]
    ready = one_hot_rows(cells_ref, 0, 4)
    for first in range(0, BLK_DEV, 4):
        hot, lanes = ready
        rows = jnp.dot(table, jnp.concatenate([hot, hot], axis=0), preferred_element_type=F32)
        if first + 4 < BLK_DEV:
            ready = one_hot_rows(cells_ref, first + 4, 4)
        pick(rows, first, spans, iota((CR, 4 * BLK), 0) == lanes, gas_ref)
    state, sources = step(count_ref, parcel_ref, gas_ref)
    for i in range(4):
        src_out[i] = sources[i]
        state_ref[i] = state[i]
    leave_ref[...] = jnp.zeros_like(leave_ref)
    up, down, spare = jnp.int32(0), jnp.int32(0), 2 * MOVEB - 1
    for block in range(BLK_DEV):
        move = move_ref[block]
        row = state_ref[:, block : block + 1, :]
        stay_out[:, block : block + 1, :] = jnp.where(move == 0, row, 0.0)
        to_up = jnp.where(move == 1, jnp.minimum(up, MOVEB - 1), spare)
        to_down = jnp.where(move == -1, jnp.minimum(down, MOVEB - 1), spare)
        leave_ref[0, :, pl.ds(to_up, 1), :] = row
        leave_ref[1, :, pl.ds(to_down, 1), :] = row
        up = up + jnp.where(move == 1, 1, 0)
        down = down + jnp.where(move == -1, 1, 0)
    odd = odd_ref[0] == 1
    up, down = leave_ref[0, :, :MOVEB], leave_ref[1, :, :MOVEB]
    leave_out[0] = jnp.where(odd, down, up)
    leave_out[1] = jnp.where(odd, up, down)


SOURCE_OF = (0, 1, 2, 3, 0)


def near_parcels_body(
    count_ref, tiles_ref, parcel_ref, cells_ref, rad_ref, near_out, rad_out, gas_ref, hot_ref, spread_ref
):
    rad_out[...] = rad_ref[...]
    start = 16
    table = jnp.concatenate(halves(tiles_ref[start : 4 * BAND]), axis=0)
    depth = 4 * BAND - start
    spans = [((f + 1) * BAND - start, (f + 1) * BAND - start + CYCLES) for f in range(3)]
    for first in range(0, BLK_DEV, 4):
        hot, lanes = one_hot_rows(cells_ref, first, 4)
        hot_ref[:, first * BLK : (first + 4) * BLK] = hot
        rows = jnp.dot(table, hot, preferred_element_type=F32)
        rows = rows[:depth] + rows[depth:]
        pick(rows, first, spans, iota((CYCLES, 4 * BLK), 0) == lanes, gas_ref)
    _, sources = step(count_ref, parcel_ref, gas_ref)
    rows = [s.astype(BF16) for s in sources]
    rows = [r.astype(F32) for r in rows] + [s - r.astype(F32) for s, r in zip(sources, rows)]
    zero = jnp.zeros((), BF16)
    for first in range(0, BLK_DEV, 4):
        mask = equals(CYCLES, lane_row(cells_ref, first, 4) & (CR - 1))
        for i, row in enumerate(rows):
            row = jnp.concatenate([row[first + j : first + j + 1] for j in range(4)], axis=1).astype(BF16)
            spread_ref[i * CYCLES : (i + 1) * CYCLES, first * BLK : (first + 4) * BLK] = jnp.where(mask, row, zero)
    total = lax.dot_general(spread_ref[...], hot_ref[...], NT, preferred_element_type=F32)
    near_out[...] = total[: 4 * CYCLES] + total[4 * CYCLES :]


def near_body(
    odd_ref, coef_ref, first_ref, second_ref, tiles_ref, near_ref, _, send_hbm, send_out, sems
):
    copies = []
    lane = iota((CR, 2 * CAZ), 1)
    z = lane % CAZ
    tiles = [tiles_ref[:, p * 2 * CAZ : (p + 1) * 2 * CAZ] for p in range(PAIRS)]
    odd = odd_ref[0] == 1
    first, second = first_ref[...], second_ref[...]
    before, after = jnp.where(odd, first, second), jnp.where(odd, second, first)
    halo = turned([jnp.concatenate([before[f], after[f]], axis=0) for f in range(FIELDS)])

    column = iota((CR, 1), 0)
    radius = column
    c = [jnp.zeros((CR, 1), F32) for _ in range(6)]
    for f in range(FIELDS):
        here = (column >= f * BAND) & (column < (f + 1) * BAND)
        radius = jnp.where(here, column - f * BAND, radius)
        c = [jnp.where(here, coef_ref[f, i], c[i]) for i in range(6)]
    metric = 4.0 / (radius.astype(F32) + 4.0)
    mid = (1.0 - c[1] - c[5]) - c[3] * metric
    az_up, az_down = (0.5 * (c[2] + c[3])) * metric, (0.5 * (c[3] - c[2])) * metric
    ax_up, ax_down = 0.5 * (c[0] + c[1]), 0.5 * (c[1] - c[0])
    rad_up = 0.5 * (c[4] + c[5])
    rad_down = jnp.where(radius == 0, 0.0, 0.5 * (c[5] - c[4]))
    low = lane < CAZ
    swapped = [pltpu.roll(t, CAZ, 1) for t in tiles]
    for p in range(PAIRS):
        q = tiles[p]
        ahead = jnp.where(low, swapped[p], swapped[p + 1] if p + 1 < PAIRS else halo)
        behind = jnp.where(low, swapped[p - 1] if p else halo, swapped[p])
        az_a = jnp.where(z == CAZ - 1, 0.0, pltpu.roll(q, 2 * CAZ - 1, 1))
        az_b = jnp.where(z == 0, 0.0, pltpu.roll(q, 1, 1))
        r_a = pltpu.roll(q, CR - 1, 0)
        r_b = pltpu.roll(q, 1, 0)
        out = (
            mid * q + ax_up * ahead + ax_down * behind + az_up * az_a + az_down * az_b
            + rad_up * r_a + rad_down * r_b
        )
        ends = jnp.where(z == 0, az_up * q, jnp.where(z == CAZ - 1, az_down * q, 0.0))
        ends = sum(
            pltpu.roll(ends[f * BAND : f * BAND + CYCLES], 2 * f, 1) if f else ends[:CYCLES]
            for f in range(FIELDS)
        )
        for f in range(FIELDS):
            s = SOURCE_OF[f] * CYCLES
            block = out[f * BAND : f * BAND + CYCLES] + near_ref[
                s : s + CYCLES, p * 2 * CAZ : (p + 1) * 2 * CAZ
            ]
            for quad in range(QUADS):
                send_out[p * QUADS + quad, f * 4 : f * 4 + 4, :] = block[quad * 4 : quad * 4 + 4]
        for quad in range(QUADS):
            send_out[p * QUADS + quad, LINES : LINES + 4, :] = ends[quad * 4 : quad * 4 + 4]
        span = pl.ds(p * QUADS, QUADS)
        copies.append(pltpu.make_async_copy(send_out.at[span], send_hbm.at[span], sems.at[p]))
        copies[p].start()
    for copy in copies:
        copy.wait()


def gas_body(
    rad_ref, odd_ref, az_ref, coef_ref, q_ref, first_ref, second_ref, az_first, az_second, rad_in, src_ref,
    cells_ref, _,
    sect_out, hot_ref, spread_ref,
):
    width = 4
    zero = jnp.zeros((), BF16)

    def scattered(i):
        for first in range(0, BLK_DEV, width):
            cols = slice(first * BLK, (first + width) * BLK)
            if i == 0:
                hot_ref[:, cols] = one_hot_rows(cells_ref, first, width)[0]
            mask = equals(CR, lane_row(cells_ref, first, width) & (CR - 1))
            row = jnp.concatenate([src_ref[i, first + j : first + j + 1, :] for j in range(width)], axis=1)
            high = row.astype(BF16)
            low = (row - high.astype(F32)).astype(BF16)
            spread_ref[i, 0:CR, cols] = jnp.where(mask, high, zero)
            spread_ref[i, CR:, cols] = jnp.where(mask, low, zero)
        total = lax.dot_general(hot_ref[...], spread_ref[i], NT, preferred_element_type=F32)
        return total[:, :CR] + total[:, CR:]

    rad = rad_ref[0]
    odd = odd_ref[0] == 1
    row = iota((CAZ, CR), 0)
    lane = iota((1, CR), 1)
    metric = 4.0 / ((rad * CR + lane).astype(F32) + 4.0)
    target = jnp.where(rad == 0, CR - 1, 0)
    odd_az = az_ref[0] % 2 == 1
    az_prev = jnp.where(odd_az, az_first[...], az_second[...])
    az_next = jnp.where(odd_az, az_second[...], az_first[...])
    added = {0: scattered(0)}
    for f in (0, 4, 1, 2, 3):
        if f in (0, 1, 2):
            added[f + 1] = scattered(f + 1)
        c = [coef_ref[f, i] for i in range(6)]
        mid = (1.0 - c[1] - c[5]) - c[3] * metric
        az_up_edge, az_down_edge = (0.5 * (c[2] + c[3])) * metric, (0.5 * (c[3] - c[2])) * metric
        az_up = jnp.where(row == CAZ - 1, 0.0, az_up_edge)
        az_down = jnp.where(row == 0, 0.0, az_down_edge)
        ax_up, ax_down = 0.5 * (c[0] + c[1]), 0.5 * (c[1] - c[0])
        rad_up = jnp.where(lane == CR - 1, 0.0, 0.5 * (c[4] + c[5]))
        rad_down = jnp.where(lane == 0, 0.0, 0.5 * (c[5] - c[4]))
        across = 0.5 * jnp.where(rad == 0, c[4] + c[5], c[5] - c[4])
        across = jnp.where(lane == target, across, 0.0)
        for a in range(CAX):
            q = q_ref[f, a]
            ahead = q_ref[f, a + 1] if a + 1 < CAX else jnp.where(odd, second_ref[f], first_ref[f])
            behind = q_ref[f, a - 1] if a else jnp.where(odd, first_ref[f], second_ref[f])
            edge = jnp.concatenate(
                [pltpu.roll(rad_in[...], (target + (2 * CR - ((2 * a + h) * 8 + f))) % CR, 1) for h in range(2)],
                axis=0,
            )
            sect_out[f, a] = (
                mid * q + ax_up * ahead + ax_down * behind
                + az_up * pltpu.roll(q, CAZ - 1, 0) + az_down * pltpu.roll(q, 1, 0)
                + rad_up * pltpu.roll(q, CR - 1, 1) + rad_down * pltpu.roll(q, 1, 1)
                + across * edge
                + added[SOURCE_OF[f]][a * CAZ : (a + 1) * CAZ]
            )
            sect_out[f, a, 0:1] += az_down_edge * az_prev[f, a : a + 1]
            sect_out[f, a, CAZ - 1 : CAZ] += az_up_edge * az_next[f, a : a + 1]


def lined(pieces, line_ref):
    low = iota((LINES, 2 * CAZ), 1) < CAZ
    for i in range(N_AZ // 2):
        t0, t1 = pieces(2 * i), pieces(2 * i + 1)
        cols = slice(i * 2 * CAZ, (i + 1) * 2 * CAZ)
        line_ref[0:LINES, cols] = jnp.where(low, t0, pltpu.roll(t1, CAZ, 1))
        line_ref[BAND : BAND + LINES, cols] = jnp.where(low, pltpu.roll(t0, CAZ, 1), t1)


def filter_body(
    az_ref, width_ref, basis_ref, turned_ref, got_ref, moved_ref,
    send_out, onward_out, line_ref, ends_ref, piece_ref,
):
    onward_out[...] = moved_ref[1]
    quad = az_ref[0] % QUADS
    low = iota((LINES, 2 * CAZ), 1) < CAZ
    line_ref[...] = jnp.zeros_like(line_ref)
    ends_ref[...] = jnp.zeros_like(ends_ref)
    for s in range(N_AZ):
        packed = got_ref[s, LINES : LINES + 4, :]
        for f in range(FIELDS):
            piece_ref[s, f * 4 : f * 4 + 4, :] = pltpu.roll(packed, 2 * CAZ - 2 * f, 1) if f else packed
    lined(lambda s: got_ref[s, 0:LINES, :], line_ref)
    lined(lambda s: piece_ref[s], ends_ref)
    z = iota((2 * BAND, NAZ), 1) % CAZ
    ends = ends_ref[...]
    lines = (
        line_ref[...]
        + jnp.where(z == CAZ - 1, pltpu.roll(ends, NAZ - 1, 1), 0.0)
        + jnp.where(z == 0, pltpu.roll(ends, 1, 1), 0.0)
    )
    rows = 2 * BAND
    both = jnp.concatenate(halves(lines), axis=0)
    whole = jnp.dot(both, turned_ref[...], preferred_element_type=F32)
    coefs = whole[:rows, :MODES] + whole[rows:, :MODES] + whole[:rows, MODES:]
    column = iota((rows, MODES), 1)
    cycle = iota((rows, MODES), 0) % 4
    mode = jnp.where(column < HALF, column, column - HALF + 1)
    width = jnp.zeros((rows, MODES), jnp.int32)
    for i in range(4):
        width = jnp.where(cycle == i, width_ref[quad * 4 + i], width)
    weight = jnp.where(mode == 0, 1.0 / NAZ, 2.0 / NAZ)
    coefs = coefs * jnp.where(mode < width, weight, 0.0)
    high, rest = halves(coefs)
    line_ref[...] = jnp.dot(
        jnp.concatenate([high, high], axis=1), basis_ref[...], preferred_element_type=F32
    ) + jnp.dot(rest, basis_ref[:MODES], preferred_element_type=F32)
    for i in range(N_AZ // 2):
        cols = slice(i * 2 * CAZ, (i + 1) * 2 * CAZ)
        t0, t1 = line_ref[0:LINES, cols], line_ref[BAND : BAND + LINES, cols]
        send_out[2 * i, 0:LINES] = jnp.where(low, t0, pltpu.roll(t1, CAZ, 1))
        send_out[2 * i + 1, 0:LINES] = jnp.where(low, pltpu.roll(t0, CAZ, 1), t1)


def merge_body(
    rad_ref, odd_ref, sect_ref, got_ref, stay_ref, moved_ref, onward_ref, gas_out, parcels_out, flip_ref
):
    odd = odd_ref[0] == 1
    parcels_out[:, 0:BLK_DEV, :] = stay_ref[...]
    first, second = moved_ref[0], onward_ref[...]
    parcels_out[:, BLK_DEV : BLK_DEV + MOVEB, :] = jnp.where(odd, first, second)
    parcels_out[:, BLK_DEV + MOVEB :, :] = jnp.where(odd, second, first)
    near = (iota((2 * CAZ, CR), 1) < CYCLES) & (rad_ref[0] == 0)
    tiles = []
    for pair in range(PAIRS):
        flip_ref[pair, FIELDS * CYCLES :, :] = jnp.zeros((CR - FIELDS * CYCLES, CR), F32)
        for f in range(FIELDS):
            for quad in range(QUADS):
                first = f * CYCLES + quad * 4
                flip_ref[pair, first : first + 4, :] = got_ref[pair * QUADS + quad, f * 4 : f * 4 + 4, :]
        tiles.append(flip_ref[pair].T)
    for f in range(FIELDS):
        for pair in range(PAIRS):
            moved = pltpu.roll(tiles[pair], CR - f * CYCLES, 1) if f else tiles[pair]
            kept = sect_ref[f, 2 * pair : 2 * pair + 2].reshape(2 * CAZ, CR)
            gas_out[f, 2 * pair : 2 * pair + 2] = jnp.where(near, moved, kept).reshape(2, CAZ, CR)


def shards(fields, coeffs, parcels, cells, counts, moves, widths):
    rad_index = lax.axis_index("rad").astype(jnp.int32).reshape(1)
    az_index = lax.axis_index("az").astype(jnp.int32).reshape(1)
    odd = (lax.axis_index("ax").astype(jnp.int32) % 2).reshape(1)
    n_ax, n_az, n_rad = (lax.axis_size(axis) for axis in ("ax", "az", "rad"))
    parcels = parcels.reshape(4, BLK_DEV, BLK)
    cells = cells.reshape(BLK_DEV, BLK)
    moves = moves.reshape(BLK_DEV)
    inner = [(i, i ^ 1) for i in range(n_ax)]
    outer = [(i, ((i + 1) ^ 1) - 1) for i in range(1, n_ax - 1)]
    along = [(i, i + 2) for i in range(0, n_ax - 2, 2)] + [(i, i - 2) for i in range(3, n_ax, 2)]
    inner_az = [(i, i ^ 1) for i in range(n_az)]
    outer_az = [(i, (((i + 1) ^ 1) - 1) % n_az) for i in range(n_az)]
    across = [(i, i ^ 1) for i in range(n_rad)]
    gas_shape = (FIELDS, CAX, CAZ, CR)

    first, second, az_first, az_second, tiles, rad_edge = call(
        edges_body,
        [(FIELDS, CAZ, CR)] * 2 + [(FIELDS, CAX, CR)] * 2 + [(CR, ROWS), (32, CR)],
        [SMEM, SMEM, SMEM, VMEM], 10**6, 10**6,
        mib=4,
    )(rad_index, odd, az_index, fields)
    second = lax.ppermute(second, "ax", outer)
    first = lax.ppermute(first, "ax", inner)
    az_first = lax.ppermute(az_first, "az", inner_az)
    az_second = lax.ppermute(az_second, "az", outer_az)

    near, rad_edge = call(
        near_parcels_body,
        [(4 * CYCLES, ROWS), (32, CR)],
        [SMEM] + [VMEM] * 4, 3 * 10**9, 2 * 10**6,
        [
            pltpu.VMEM((3, BLK_DEV, BLK), F32),
            pltpu.VMEM((ROWS, PARCELS), BF16),
            pltpu.VMEM((8 * CYCLES, PARCELS), BF16),
        ],
        mib=16,
    )(counts, tiles, parcels, cells, rad_edge)
    rad_got = lax.ppermute(rad_edge, "rad", across)

    (to_owner,) = call(
        near_body,
        [(N_AZ, LINES + 4, 2 * CAZ)],
        [SMEM, SMEM] + [VMEM] * 4 + [ANY], 10**7, 4 * 10**6,
        [
            pltpu.VMEM((N_AZ, LINES + 4, 2 * CAZ), F32),
            pltpu.SemaphoreType.DMA((PAIRS,)),
        ],
        mib=8,
        hbm_first=True,
    )(odd, coeffs, first, second, tiles, near, rad_got)
    lines = lax.all_to_all(to_owner, "az", 0, 0, tiled=True)

    src, stay, leaving = call(
        parcels_body,
        [(4, BLK_DEV, BLK), (4, BLK_DEV, BLK), (2, 4, MOVEB, BLK)],
        [SMEM] * 3 + [VMEM] * 3, 6 * 10**9, 2 * 10**6,
        [
            pltpu.VMEM((3, BLK_DEV, BLK), F32),
            pltpu.VMEM((4, BLK_DEV, BLK), F32),
            pltpu.VMEM((2, 4, 2 * MOVEB, BLK), F32),
        ],
        mib=16,
    )(odd, counts, moves, fields, parcels, cells)
    moved = lax.ppermute(leaving, "ax", inner)

    basis, basis_turned = basis_parts()
    to_home, onward = call(
        filter_body,
        [(N_AZ, LINES, 2 * CAZ), (4, MOVEB, BLK)],
        [SMEM, SMEM] + [VMEM] * 4, 10**8, 10**6,
        [
            pltpu.VMEM((2 * BAND, NAZ), F32),
            pltpu.VMEM((2 * BAND, NAZ), F32),
            pltpu.VMEM((N_AZ, LINES, 2 * CAZ), F32),
        ],
        mib=6,
    )(az_index, widths, basis, basis_turned, lines, moved)
    filtered = lax.all_to_all(to_home, "az", 0, 0, tiled=True)
    onward = lax.ppermute(onward, "ax", along)

    (sect,) = call(
        gas_body, [gas_shape], [SMEM] * 4 + [VMEM] * 8 + [ANY], 8 * 10**9, 4 * 10**6,
        [pltpu.VMEM((ROWS, PARCELS), BF16), pltpu.VMEM((4, 2 * CR, PARCELS), BF16)],
        mib=24,
    )(rad_index, odd, az_index, coeffs, fields, first, second, az_first, az_second, rad_got, src, cells, to_home)

    gas_out, parcels_out = call(
        merge_body,
        [gas_shape, (4, BLK_DEV + 2 * MOVEB, BLK)],
        [SMEM, SMEM] + [VMEM] * 5, 10**6, 4 * 10**6,
        [pltpu.VMEM((PAIRS, CR, CR), F32)],
        mib=8,
    )(rad_index, odd, sect, filtered, stay, moved, onward)
    return gas_out, parcels_out.reshape(4, BLK_DEV + 2 * MOVEB, 1, BLK)


def solution(mesh):
    block = P(None, "ax", "az", "rad")
    flat = P("ax", "az", "rad")
    return jax.shard_map(
        shards,
        mesh=mesh,
        in_specs=(block, P(), block, flat, flat, flat, P()),
        out_specs=(block, block),
        check_vma=False,
    )
```

```python
import math

import jax
import jax.numpy as jnp
import ml_dtypes
import numpy as np
from jax import lax
from jax.experimental import pallas as pl
from jax.experimental.pallas import tpu as pltpu
from jax.sharding import PartitionSpec as P

FIELDS = 5
CYCLES = 16
MODES = 128
HALF = MODES // 2
BLK = 128
BLK_DEV = 32
MOVEB = 4
CAX, CAZ, CR = 8, 64, 128
ROWS = CAX * CAZ
PARCELS = BLK * BLK_DEV
NAZ = 1024
N_AZ = 16
PAIRS = CAX // 2
QUADS = CYCLES // 4
LINES = FIELDS * 4

STEP_SIZE = 0.5
EVAP_RATE = 0.5
COUPLING = 0.5

F32 = jnp.float32
BF16 = jnp.bfloat16
HIGHEST = lax.Precision.HIGHEST
VMEM = pl.BlockSpec(memory_space=pltpu.VMEM)
SMEM = pl.BlockSpec(memory_space=pltpu.SMEM)
ANY = pl.BlockSpec(memory_space=pl.ANY)
HBM = pl.BlockSpec(memory_space=pltpu.HBM)
NT = (((1,), (1,)), ((), ()))


def basis_parts():
    column = np.arange(MODES)
    mode = np.where(column < HALF, column, column - HALF + 1)
    phases = (mode[:, None] * np.arange(NAZ)[None, :]) % NAZ
    angles = phases.astype(np.float32) * np.float32(2.0 * math.pi / NAZ)
    table = np.where(column[:, None] < HALF, np.cos(angles), np.sin(angles)).astype(np.float32)
    high = table.astype(ml_dtypes.bfloat16)
    low = (table - high.astype(np.float32)).astype(ml_dtypes.bfloat16)
    parts = np.concatenate([high, low])
    return jnp.asarray(parts), jnp.asarray(np.ascontiguousarray(parts.T))


def iota(shape, axis):
    return lax.broadcasted_iota(jnp.int32, shape, axis)


def halves(value):
    high = value.astype(BF16)
    return high, (value - high.astype(F32)).astype(BF16)


def call(body, out_shape, in_specs, flops, nbytes, scratch=(), mib=24, hbm_first=False):
    return pl.pallas_call(
        body,
        out_shape=[jax.ShapeDtypeStruct(shape, F32) for shape in out_shape],
        in_specs=in_specs,
        out_specs=[HBM if hbm_first and i == 0 else VMEM for i in range(len(out_shape))],
        scratch_shapes=list(scratch),
        compiler_params=pltpu.CompilerParams(vmem_limit_bytes=mib * 2**20),
        cost_estimate=pl.CostEstimate(flops=flops, bytes_accessed=nbytes, transcendentals=0),
    )


def edges_body(odd_ref, az_ref, q_ref, first_out, second_out, az_first, az_second):
    odd, odd_az = odd_ref[0] == 1, az_ref[0] % 2 == 1
    low, high = q_ref[:, 0], q_ref[:, CAX - 1]
    first_out[...] = jnp.where(odd, low, high)
    second_out[...] = jnp.where(odd, high, low)
    low, high = q_ref[:, :, 0, :], q_ref[:, :, CAZ - 1, :]
    az_first[...] = jnp.where(odd_az, low, high)
    az_second[...] = jnp.where(odd_az, high, low)


def lane_row(cells_ref, first, blocks):
    return jnp.concatenate([cells_ref[first + i : first + i + 1, :] for i in range(blocks)], axis=1)


def equals(count, row):
    numbers = iota((count, row.shape[1]), 0).astype(F32).astype(BF16)
    return numbers == row.astype(F32).astype(BF16)


def one_hot_rows(cells_ref, first, blocks):
    cells = lane_row(cells_ref, first, blocks)
    one, zero = jnp.ones((), BF16), jnp.zeros((), BF16)
    half = ROWS // 2
    parts = [jnp.where(equals(half, (cells >> 7) - half * i), one, zero) for i in range(2)]
    return jnp.concatenate(parts, axis=0), cells & (CR - 1)


def step(count_ref, parcel_ref, gas_ref):
    slot = iota((BLK_DEV, BLK), 0) * BLK + iota((BLK_DEV, BLK), 1)
    alive = slot < count_ref[0]
    diam = parcel_ref[3]
    vel = [parcel_ref[i] for i in range(3)]
    gas = [gas_ref[i] for i in range(3)]
    slip = [g - u for g, u in zip(gas, vel)]
    slip_sq = slip[0] * slip[0] + slip[1] * slip[1] + slip[2] * slip[2]
    new_vel = [(u * diam + STEP_SIZE * g) / (diam + STEP_SIZE) for u, g in zip(vel, gas)]
    new_diam = diam / (1.0 + STEP_SIZE * EVAP_RATE * (1.0 + slip_sq))
    sources = [(diam - new_diam) * COUPLING] + [
        -(diam * (v - u)) * COUPLING for v, u in zip(new_vel, vel)
    ]
    state = [jnp.where(alive, s, 0.0) for s in new_vel + [new_diam]]
    return state, [jnp.where(alive, s, 0.0) for s in sources]


def pick(rows, first, spans, mask, gas_ref):
    for f, (start, stop) in enumerate(spans):
        found = jnp.sum(jnp.where(mask, rows[start:stop], 0.0), axis=0, keepdims=True)
        for i in range(4):
            gas_ref[f, first + i : first + i + 1, :] = found[:, i * BLK : (i + 1) * BLK]


def parcels_body(
    rad_ref, odd_ref, count_ref, move_ref, q_ref, parcel_ref, cells_ref,
    src_out, stay_out, leave_out, rad_out, gas_ref, state_ref, leave_ref,
):
    rad_edges(rad_ref[0], q_ref, rad_out)
    table = jnp.concatenate(
        [jnp.concatenate(halves(q_ref[f + 1].reshape(ROWS, CR).T), axis=1) for f in range(3)], axis=0
    )
    spans = [(f * CR, (f + 1) * CR) for f in range(3)]
    ready = one_hot_rows(cells_ref, 0, 4)
    for first in range(0, BLK_DEV, 4):
        hot, lanes = ready
        rows = jnp.dot(table, jnp.concatenate([hot, hot], axis=0), preferred_element_type=F32)
        if first + 4 < BLK_DEV:
            ready = one_hot_rows(cells_ref, first + 4, 4)
        pick(rows, first, spans, iota((CR, 4 * BLK), 0) == lanes, gas_ref)
    state, sources = step(count_ref, parcel_ref, gas_ref)
    for i in range(4):
        src_out[i] = sources[i]
        state_ref[i] = state[i]
    leave_ref[...] = jnp.zeros_like(leave_ref)
    up, down, spare = jnp.int32(0), jnp.int32(0), 2 * MOVEB - 1
    for block in range(BLK_DEV):
        move = move_ref[block]
        row = state_ref[:, block : block + 1, :]
        stay_out[:, block : block + 1, :] = jnp.where(move == 0, row, 0.0)
        to_up = jnp.where(move == 1, jnp.minimum(up, MOVEB - 1), spare)
        to_down = jnp.where(move == -1, jnp.minimum(down, MOVEB - 1), spare)
        leave_ref[0, :, pl.ds(to_up, 1), :] = row
        leave_ref[1, :, pl.ds(to_down, 1), :] = row
        up = up + jnp.where(move == 1, 1, 0)
        down = down + jnp.where(move == -1, 1, 0)
    odd = odd_ref[0] == 1
    up, down = leave_ref[0, :, :MOVEB], leave_ref[1, :, :MOVEB]
    leave_out[0] = jnp.where(odd, down, up)
    leave_out[1] = jnp.where(odd, up, down)


SOURCE_OF = (0, 1, 2, 3, 0)


BAND = 24


def turned(parts):
    lane = iota((2 * CAZ, CR), 1)
    packed = jnp.zeros((2 * CAZ, CR), F32)
    for f, part in enumerate(parts):
        moved = pltpu.roll(part, f * BAND, 1) if f else part
        packed = jnp.where((lane >= f * BAND) & (lane < (f + 1) * BAND), moved, packed)
    return packed.T


def near_parcels_body(count_ref, q_ref, parcel_ref, cells_ref, tiles_out, near_out, gas_ref, hot_ref, spread_ref):
    for p in range(PAIRS):
        tiles_out[:, p * 2 * CAZ : (p + 1) * 2 * CAZ] = turned(
            [q_ref[f, 2 * p : 2 * p + 2].reshape(2 * CAZ, CR) for f in range(FIELDS)]
        )
    start = 16
    table = jnp.concatenate(halves(tiles_out[start : 4 * BAND]), axis=0)
    depth = 4 * BAND - start
    spans = [((f + 1) * BAND - start, (f + 1) * BAND - start + CYCLES) for f in range(3)]
    for first in range(0, BLK_DEV, 4):
        hot, lanes = one_hot_rows(cells_ref, first, 4)
        hot_ref[:, first * BLK : (first + 4) * BLK] = hot
        rows = jnp.dot(table, hot, preferred_element_type=F32)
        rows = rows[:depth] + rows[depth:]
        pick(rows, first, spans, iota((CYCLES, 4 * BLK), 0) == lanes, gas_ref)
    _, sources = step(count_ref, parcel_ref, gas_ref)
    rows = [s.astype(BF16) for s in sources]
    rows = [r.astype(F32) for r in rows] + [s - r.astype(F32) for s, r in zip(sources, rows)]
    zero = jnp.zeros((), BF16)
    for first in range(0, BLK_DEV, 4):
        mask = equals(CYCLES, lane_row(cells_ref, first, 4) & (CR - 1))
        for i, row in enumerate(rows):
            row = jnp.concatenate([row[first + j : first + j + 1] for j in range(4)], axis=1).astype(BF16)
            spread_ref[i * CYCLES : (i + 1) * CYCLES, first * BLK : (first + 4) * BLK] = jnp.where(mask, row, zero)
    total = lax.dot_general(spread_ref[...], hot_ref[...], NT, preferred_element_type=F32)
    near_out[...] = total[: 4 * CYCLES] + total[4 * CYCLES :]


def near_body(
    odd_ref, coef_ref, first_ref, second_ref, tiles_ref, near_ref, send_hbm, send_out, sems
):
    copies = []
    lane = iota((CR, 2 * CAZ), 1)
    z = lane % CAZ
    tiles = [tiles_ref[:, p * 2 * CAZ : (p + 1) * 2 * CAZ] for p in range(PAIRS)]
    odd = odd_ref[0] == 1
    first, second = first_ref[...], second_ref[...]
    before, after = jnp.where(odd, first, second), jnp.where(odd, second, first)
    halo = turned([jnp.concatenate([before[f], after[f]], axis=0) for f in range(FIELDS)])

    column = iota((CR, 1), 0)
    radius = column
    c = [jnp.zeros((CR, 1), F32) for _ in range(6)]
    for f in range(FIELDS):
        here = (column >= f * BAND) & (column < (f + 1) * BAND)
        radius = jnp.where(here, column - f * BAND, radius)
        c = [jnp.where(here, coef_ref[f, i], c[i]) for i in range(6)]
    metric = 4.0 / (radius.astype(F32) + 4.0)
    mid = (1.0 - c[1] - c[5]) - c[3] * metric
    az_up, az_down = (0.5 * (c[2] + c[3])) * metric, (0.5 * (c[3] - c[2])) * metric
    ax_up, ax_down = 0.5 * (c[0] + c[1]), 0.5 * (c[1] - c[0])
    rad_up = 0.5 * (c[4] + c[5])
    rad_down = jnp.where(radius == 0, 0.0, 0.5 * (c[5] - c[4]))
    low = lane < CAZ
    swapped = [pltpu.roll(t, CAZ, 1) for t in tiles]
    for p in range(PAIRS):
        q = tiles[p]
        ahead = jnp.where(low, swapped[p], swapped[p + 1] if p + 1 < PAIRS else halo)
        behind = jnp.where(low, swapped[p - 1] if p else halo, swapped[p])
        az_a = jnp.where(z == CAZ - 1, 0.0, pltpu.roll(q, 2 * CAZ - 1, 1))
        az_b = jnp.where(z == 0, 0.0, pltpu.roll(q, 1, 1))
        r_a = pltpu.roll(q, CR - 1, 0)
        r_b = pltpu.roll(q, 1, 0)
        out = (
            mid * q + ax_up * ahead + ax_down * behind + az_up * az_a + az_down * az_b
            + rad_up * r_a + rad_down * r_b
        )
        ends = jnp.where(z == 0, az_up * q, jnp.where(z == CAZ - 1, az_down * q, 0.0))
        ends = sum(
            pltpu.roll(ends[f * BAND : f * BAND + CYCLES], 2 * f, 1) if f else ends[:CYCLES]
            for f in range(FIELDS)
        )
        for f in range(FIELDS):
            s = SOURCE_OF[f] * CYCLES
            block = out[f * BAND : f * BAND + CYCLES] + near_ref[
                s : s + CYCLES, p * 2 * CAZ : (p + 1) * 2 * CAZ
            ]
            for quad in range(QUADS):
                send_out[p * QUADS + quad, f * 4 : f * 4 + 4, :] = block[quad * 4 : quad * 4 + 4]
        for quad in range(QUADS):
            send_out[p * QUADS + quad, LINES : LINES + 4, :] = ends[quad * 4 : quad * 4 + 4]
        span = pl.ds(p * QUADS, QUADS)
        copies.append(pltpu.make_async_copy(send_out.at[span], send_hbm.at[span], sems.at[p]))
        copies[p].start()
    for copy in copies:
        copy.wait()


def rad_edges(rad, q_ref, rad_out):
    extra = jnp.where(rad == 0, 1, 0)
    lane = iota((32, CR), 1)
    packed = jnp.zeros((32, CR), F32)
    for f in range(FIELDS):
        for g in range(16):
            part = q_ref[f, g // 2, (g % 2) * 32 : (g % 2) * 32 + 32, :]
            spot = g * 8 + f
            packed = jnp.where(lane == spot, pltpu.roll(part, spot + extra, 1), packed)
    rad_out[...] = packed


def gas_body(
    rad_ref, odd_ref, az_ref, coef_ref, q_ref, first_ref, second_ref, az_first, az_second, rad_in, src_ref,
    cells_ref, _,
    sect_out, hot_ref, spread_ref,
):
    width = 4
    zero = jnp.zeros((), BF16)

    def scattered(i):
        parts = 2 if i == 0 else 1
        blocks = BLK_DEV // parts
        total = None
        for start in range(0, BLK_DEV, blocks):
            for first in range(start, start + blocks, width):
                cols = slice(first * BLK, (first + width) * BLK)
                if i == 0:
                    hot_ref[:, cols] = one_hot_rows(cells_ref, first, width)[0]
                mask = equals(CR, lane_row(cells_ref, first, width) & (CR - 1))
                row = jnp.concatenate([src_ref[i, first + j : first + j + 1, :] for j in range(width)], axis=1)
                high = row.astype(BF16)
                low = (row - high.astype(F32)).astype(BF16)
                spread_ref[i, 0:CR, cols] = jnp.where(mask, high, zero)
                spread_ref[i, CR:, cols] = jnp.where(mask, low, zero)
            cols = slice(start * BLK, (start + blocks) * BLK)
            part = lax.dot_general(hot_ref[:, cols], spread_ref[i, :, cols], NT, preferred_element_type=F32)
            total = part if total is None else total + part
        return total[:, :CR] + total[:, CR:]

    rad = rad_ref[0]
    odd = odd_ref[0] == 1
    row = iota((CAZ, CR), 0)
    lane = iota((1, CR), 1)
    metric = 4.0 / ((rad * CR + lane).astype(F32) + 4.0)
    target = jnp.where(rad == 0, CR - 1, 0)
    odd_az = az_ref[0] % 2 == 1
    az_prev = jnp.where(odd_az, az_first[...], az_second[...])
    az_next = jnp.where(odd_az, az_second[...], az_first[...])
    added = {0: scattered(0)}
    for f in (0, 4, 1, 2, 3):
        if f in (0, 1, 2):
            added[f + 1] = scattered(f + 1)
        c = [coef_ref[f, i] for i in range(6)]
        mid = (1.0 - c[1] - c[5]) - c[3] * metric
        az_up_edge, az_down_edge = (0.5 * (c[2] + c[3])) * metric, (0.5 * (c[3] - c[2])) * metric
        az_up = jnp.where(row == CAZ - 1, 0.0, az_up_edge)
        az_down = jnp.where(row == 0, 0.0, az_down_edge)
        ax_up, ax_down = 0.5 * (c[0] + c[1]), 0.5 * (c[1] - c[0])
        rad_up = jnp.where(lane == CR - 1, 0.0, 0.5 * (c[4] + c[5]))
        rad_down = jnp.where(lane == 0, 0.0, 0.5 * (c[5] - c[4]))
        across = 0.5 * jnp.where(rad == 0, c[4] + c[5], c[5] - c[4])
        across = jnp.where(lane == target, across, 0.0)
        for a in range(CAX):
            q = q_ref[f, a]
            ahead = q_ref[f, a + 1] if a + 1 < CAX else jnp.where(odd, second_ref[f], first_ref[f])
            behind = q_ref[f, a - 1] if a else jnp.where(odd, first_ref[f], second_ref[f])
            edge = jnp.concatenate(
                [pltpu.roll(rad_in[...], (target + (2 * CR - ((2 * a + h) * 8 + f))) % CR, 1) for h in range(2)],
                axis=0,
            )
            sect_out[f, a] = (
                mid * q + ax_up * ahead + ax_down * behind
                + az_up * pltpu.roll(q, CAZ - 1, 0) + az_down * pltpu.roll(q, 1, 0)
                + rad_up * pltpu.roll(q, CR - 1, 1) + rad_down * pltpu.roll(q, 1, 1)
                + across * edge
                + added[SOURCE_OF[f]][a * CAZ : (a + 1) * CAZ]
            )
            sect_out[f, a, 0:1] += az_down_edge * az_prev[f, a : a + 1]
            sect_out[f, a, CAZ - 1 : CAZ] += az_up_edge * az_next[f, a : a + 1]


def lined(pieces, line_ref):
    low = iota((LINES, 2 * CAZ), 1) < CAZ
    for i in range(N_AZ // 2):
        t0, t1 = pieces(2 * i), pieces(2 * i + 1)
        cols = slice(i * 2 * CAZ, (i + 1) * 2 * CAZ)
        line_ref[0:LINES, cols] = jnp.where(low, t0, pltpu.roll(t1, CAZ, 1))
        line_ref[BAND : BAND + LINES, cols] = jnp.where(low, pltpu.roll(t0, CAZ, 1), t1)


def filter_body(
    az_ref, width_ref, basis_ref, turned_ref, got_ref, moved_ref,
    send_out, onward_out, line_ref, ends_ref, piece_ref,
):
    onward_out[...] = moved_ref[1]
    quad = az_ref[0] % QUADS
    low = iota((LINES, 2 * CAZ), 1) < CAZ
    line_ref[...] = jnp.zeros_like(line_ref)
    ends_ref[...] = jnp.zeros_like(ends_ref)
    for s in range(N_AZ):
        packed = got_ref[s, LINES : LINES + 4, :]
        for f in range(FIELDS):
            piece_ref[s, f * 4 : f * 4 + 4, :] = pltpu.roll(packed, 2 * CAZ - 2 * f, 1) if f else packed
    lined(lambda s: got_ref[s, 0:LINES, :], line_ref)
    lined(lambda s: piece_ref[s], ends_ref)
    z = iota((2 * BAND, NAZ), 1) % CAZ
    ends = ends_ref[...]
    lines = (
        line_ref[...]
        + jnp.where(z == CAZ - 1, pltpu.roll(ends, NAZ - 1, 1), 0.0)
        + jnp.where(z == 0, pltpu.roll(ends, 1, 1), 0.0)
    )
    rows = 2 * BAND
    both = jnp.concatenate(halves(lines), axis=0)
    whole = jnp.dot(both, turned_ref[...], preferred_element_type=F32)
    coefs = whole[:rows, :MODES] + whole[rows:, :MODES] + whole[:rows, MODES:]
    column = iota((rows, MODES), 1)
    cycle = iota((rows, MODES), 0) % 4
    mode = jnp.where(column < HALF, column, column - HALF + 1)
    width = jnp.zeros((rows, MODES), jnp.int32)
    for i in range(4):
        width = jnp.where(cycle == i, width_ref[quad * 4 + i], width)
    weight = jnp.where(mode == 0, 1.0 / NAZ, 2.0 / NAZ)
    coefs = coefs * jnp.where(mode < width, weight, 0.0)
    high, rest = halves(coefs)
    line_ref[...] = jnp.dot(
        jnp.concatenate([high, high], axis=1), basis_ref[...], preferred_element_type=F32
    ) + jnp.dot(rest, basis_ref[:MODES], preferred_element_type=F32)
    for i in range(N_AZ // 2):
        cols = slice(i * 2 * CAZ, (i + 1) * 2 * CAZ)
        t0, t1 = line_ref[0:LINES, cols], line_ref[BAND : BAND + LINES, cols]
        send_out[2 * i, 0:LINES] = jnp.where(low, t0, pltpu.roll(t1, CAZ, 1))
        send_out[2 * i + 1, 0:LINES] = jnp.where(low, pltpu.roll(t0, CAZ, 1), t1)


def merge_body(
    rad_ref, odd_ref, sect_ref, got_ref, stay_ref, moved_ref, onward_ref, gas_out, parcels_out, flip_ref
):
    odd = odd_ref[0] == 1
    parcels_out[:, 0:BLK_DEV, :] = stay_ref[...]
    first, second = moved_ref[0], onward_ref[...]
    parcels_out[:, BLK_DEV : BLK_DEV + MOVEB, :] = jnp.where(odd, first, second)
    parcels_out[:, BLK_DEV + MOVEB :, :] = jnp.where(odd, second, first)
    near = (iota((2 * CAZ, CR), 1) < CYCLES) & (rad_ref[0] == 0)
    tiles = []
    for pair in range(PAIRS):
        flip_ref[pair, FIELDS * CYCLES :, :] = jnp.zeros((CR - FIELDS * CYCLES, CR), F32)
        for f in range(FIELDS):
            for quad in range(QUADS):
                first = f * CYCLES + quad * 4
                flip_ref[pair, first : first + 4, :] = got_ref[pair * QUADS + quad, f * 4 : f * 4 + 4, :]
        tiles.append(flip_ref[pair].T)
    for f in range(FIELDS):
        for pair in range(PAIRS):
            moved = pltpu.roll(tiles[pair], CR - f * CYCLES, 1) if f else tiles[pair]
            kept = sect_ref[f, 2 * pair : 2 * pair + 2].reshape(2 * CAZ, CR)
            gas_out[f, 2 * pair : 2 * pair + 2] = jnp.where(near, moved, kept).reshape(2, CAZ, CR)


def shards(fields, coeffs, parcels, cells, counts, moves, widths):
    rad_index = lax.axis_index("rad").astype(jnp.int32).reshape(1)
    az_index = lax.axis_index("az").astype(jnp.int32).reshape(1)
    odd = (lax.axis_index("ax").astype(jnp.int32) % 2).reshape(1)
    n_ax, n_az, n_rad = (lax.axis_size(axis) for axis in ("ax", "az", "rad"))
    parcels = parcels.reshape(4, BLK_DEV, BLK)
    cells = cells.reshape(BLK_DEV, BLK)
    counts = counts.reshape(1)
    moves = moves.reshape(BLK_DEV)
    inner = [(i, i ^ 1) for i in range(n_ax)]
    outer = [(i, ((i + 1) ^ 1) - 1) for i in range(1, n_ax - 1)]
    along = [(i, i + 2) for i in range(0, n_ax - 2, 2)] + [(i, i - 2) for i in range(3, n_ax, 2)]
    inner_az = [(i, i ^ 1) for i in range(n_az)]
    outer_az = [(i, (((i + 1) ^ 1) - 1) % n_az) for i in range(n_az)]
    across = [(i, i ^ 1) for i in range(n_rad)]
    gas_shape = (FIELDS, CAX, CAZ, CR)

    first, second, az_first, az_second = call(
        edges_body, [(FIELDS, CAZ, CR)] * 2 + [(FIELDS, CAX, CR)] * 2, [SMEM, SMEM, VMEM], 10**6, 10**6, mib=4
    )(odd, az_index, fields)
    first = lax.ppermute(first, "ax", inner)
    second = lax.ppermute(second, "ax", outer)
    az_first = lax.ppermute(az_first, "az", inner_az)
    az_second = lax.ppermute(az_second, "az", outer_az)

    tiles, near = call(
        near_parcels_body,
        [(CR, ROWS), (4 * CYCLES, ROWS)],
        [SMEM] + [VMEM] * 3, 3 * 10**9, 2 * 10**6,
        [
            pltpu.VMEM((3, BLK_DEV, BLK), F32),
            pltpu.VMEM((ROWS, PARCELS), BF16),
            pltpu.VMEM((8 * CYCLES, PARCELS), BF16),
        ],
        mib=16,
    )(counts, fields, parcels, cells)

    (to_owner,) = call(
        near_body,
        [(N_AZ, LINES + 4, 2 * CAZ)],
        [SMEM, SMEM] + [VMEM] * 4, 10**7, 4 * 10**6,
        [
            pltpu.VMEM((N_AZ, LINES + 4, 2 * CAZ), F32),
            pltpu.SemaphoreType.DMA((PAIRS,)),
        ],
        mib=8,
        hbm_first=True,
    )(odd, coeffs, first, second, tiles, near)
    lines = lax.all_to_all(to_owner, "az", 0, 0, tiled=True)

    src, stay, leaving, rad_edge = call(
        parcels_body,
        [(4, BLK_DEV, BLK), (4, BLK_DEV, BLK), (2, 4, MOVEB, BLK), (32, CR)],
        [SMEM] * 4 + [VMEM] * 3, 6 * 10**9, 2 * 10**6,
        [
            pltpu.VMEM((3, BLK_DEV, BLK), F32),
            pltpu.VMEM((4, BLK_DEV, BLK), F32),
            pltpu.VMEM((2, 4, 2 * MOVEB, BLK), F32),
        ],
        mib=16,
    )(rad_index, odd, counts, moves, fields, parcels, cells)
    rad_got = lax.ppermute(rad_edge, "rad", across)
    moved = lax.ppermute(leaving, "ax", inner)

    basis, basis_turned = basis_parts()
    to_home, onward = call(
        filter_body,
        [(N_AZ, LINES, 2 * CAZ), (4, MOVEB, BLK)],
        [SMEM, SMEM] + [VMEM] * 4, 10**8, 10**6,
        [
            pltpu.VMEM((2 * BAND, NAZ), F32),
            pltpu.VMEM((2 * BAND, NAZ), F32),
            pltpu.VMEM((N_AZ, LINES, 2 * CAZ), F32),
        ],
        mib=6,
    )(az_index, widths, basis, basis_turned, lines, moved)
    filtered = lax.all_to_all(to_home, "az", 0, 0, tiled=True)
    onward = lax.ppermute(onward, "ax", along)

    (sect,) = call(
        gas_body, [gas_shape], [SMEM] * 4 + [VMEM] * 8 + [ANY], 8 * 10**9, 4 * 10**6,
        [pltpu.VMEM((ROWS, PARCELS), BF16), pltpu.VMEM((4, 2 * CR, PARCELS), BF16)],
        mib=24,
    )(rad_index, odd, az_index, coeffs, fields, first, second, az_first, az_second, rad_got, src, cells, to_home)

    gas_out, parcels_out = call(
        merge_body,
        [gas_shape, (4, BLK_DEV + 2 * MOVEB, BLK)],
        [SMEM, SMEM] + [VMEM] * 5, 10**6, 4 * 10**6,
        [pltpu.VMEM((PAIRS, CR, CR), F32)],
        mib=8,
    )(rad_index, odd, sect, filtered, stay, moved, onward)
    return gas_out, parcels_out.reshape(4, BLK_DEV + 2 * MOVEB, 1, BLK)


def solution(mesh):
    block = P(None, "ax", "az", "rad")
    flat = P("ax", "az", "rad")
    return jax.shard_map(
        shards,
        mesh=mesh,
        in_specs=(block, P(), block, flat, flat, flat, P()),
        out_specs=(block, block),
        check_vma=False,
    )
```

```python
import math

import jax
import jax.numpy as jnp
import ml_dtypes
import numpy as np
from jax import lax
from jax.experimental import pallas as pl
from jax.experimental.pallas import tpu as pltpu
from jax.sharding import PartitionSpec as P

FIELDS = 5
CYCLES = 16
MODES = 128
HALF = MODES // 2
BLK = 128
BLK_DEV = 32
MOVEB = 4
CAX, CAZ, CR = 8, 64, 128
ROWS = CAX * CAZ
PARCELS = BLK * BLK_DEV
NAZ = 1024
N_AZ = 16
PAIRS = CAX // 2
QUADS = CYCLES // 4
LINES = FIELDS * 4
BAND = 24

STEP_SIZE = 0.5
EVAP_RATE = 0.5
COUPLING = 0.5

F32 = jnp.float32
BF16 = jnp.bfloat16
HIGHEST = lax.Precision.HIGHEST
VMEM = pl.BlockSpec(memory_space=pltpu.VMEM)
SMEM = pl.BlockSpec(memory_space=pltpu.SMEM)
ANY = pl.BlockSpec(memory_space=pl.ANY)
HBM = pl.BlockSpec(memory_space=pltpu.HBM)
NT = (((1,), (1,)), ((), ()))


def basis_parts():
    column = np.arange(MODES)
    mode = np.where(column < HALF, column, column - HALF + 1)
    phases = (mode[:, None] * np.arange(NAZ)[None, :]) % NAZ
    angles = phases.astype(np.float32) * np.float32(2.0 * math.pi / NAZ)
    table = np.where(column[:, None] < HALF, np.cos(angles), np.sin(angles)).astype(np.float32)
    high = table.astype(ml_dtypes.bfloat16)
    low = (table - high.astype(np.float32)).astype(ml_dtypes.bfloat16)
    parts = np.concatenate([high, low])
    return jnp.asarray(parts), jnp.asarray(np.ascontiguousarray(parts.T))


def iota(shape, axis):
    return lax.broadcasted_iota(jnp.int32, shape, axis)


def halves(value):
    high = value.astype(BF16)
    return high, (value - high.astype(F32)).astype(BF16)


def call(body, out_shape, in_specs, flops, nbytes, scratch=(), mib=24, hbm_first=False):
    return pl.pallas_call(
        body,
        out_shape=[jax.ShapeDtypeStruct(shape, F32) for shape in out_shape],
        in_specs=in_specs,
        out_specs=[HBM if hbm_first and i == 0 else VMEM for i in range(len(out_shape))],
        scratch_shapes=list(scratch),
        compiler_params=pltpu.CompilerParams(vmem_limit_bytes=mib * 2**20),
        cost_estimate=pl.CostEstimate(flops=flops, bytes_accessed=nbytes, transcendentals=0),
    )


def turned(parts):
    lane = iota((2 * CAZ, CR), 1)
    packed = jnp.zeros((2 * CAZ, CR), F32)
    for f, part in enumerate(parts):
        moved = pltpu.roll(part, f * BAND, 1) if f else part
        packed = jnp.where((lane >= f * BAND) & (lane < (f + 1) * BAND), moved, packed)
    return packed.T


def edges_body(odd_ref, az_ref, q_ref, first_out, second_out, az_first, az_second):
    odd, odd_az = odd_ref[0] == 1, az_ref[0] % 2 == 1
    low, high = q_ref[:, 0], q_ref[:, CAX - 1]
    first_out[...] = jnp.where(odd, low, high)
    second_out[...] = jnp.where(odd, high, low)
    low, high = q_ref[:, :, 0, :], q_ref[:, :, CAZ - 1, :]
    az_first[...] = jnp.where(odd_az, low, high)
    az_second[...] = jnp.where(odd_az, high, low)


def tiles_body(q_ref, tiles_out):
    for p in range(PAIRS):
        tiles_out[:, p * 2 * CAZ : (p + 1) * 2 * CAZ] = turned(
            [q_ref[f, 2 * p : 2 * p + 2].reshape(2 * CAZ, CR) for f in range(FIELDS)]
        )


def lane_row(cells_ref, first, blocks):
    return jnp.concatenate([cells_ref[first + i : first + i + 1, :] for i in range(blocks)], axis=1)


def equals(count, row):
    numbers = iota((count, row.shape[1]), 0).astype(F32).astype(BF16)
    return numbers == row.astype(F32).astype(BF16)


def one_hot_rows(cells_ref, first, blocks):
    cells = lane_row(cells_ref, first, blocks)
    one, zero = jnp.ones((), BF16), jnp.zeros((), BF16)
    half = ROWS // 2
    parts = [jnp.where(equals(half, (cells >> 7) - half * i), one, zero) for i in range(2)]
    return jnp.concatenate(parts, axis=0), cells & (CR - 1)


def step(count_ref, parcel_ref, gas_ref):
    slot = iota((BLK_DEV, BLK), 0) * BLK + iota((BLK_DEV, BLK), 1)
    alive = slot < count_ref[0]
    diam = parcel_ref[3]
    vel = [parcel_ref[i] for i in range(3)]
    gas = [gas_ref[i] for i in range(3)]
    slip = [g - u for g, u in zip(gas, vel)]
    slip_sq = slip[0] * slip[0] + slip[1] * slip[1] + slip[2] * slip[2]
    new_vel = [(u * diam + STEP_SIZE * g) / (diam + STEP_SIZE) for u, g in zip(vel, gas)]
    new_diam = diam / (1.0 + STEP_SIZE * EVAP_RATE * (1.0 + slip_sq))
    sources = [(diam - new_diam) * COUPLING] + [
        -(diam * (v - u)) * COUPLING for v, u in zip(new_vel, vel)
    ]
    state = [jnp.where(alive, s, 0.0) for s in new_vel + [new_diam]]
    return state, [jnp.where(alive, s, 0.0) for s in sources]


def pick(rows, first, spans, mask, gas_ref):
    for f, (start, stop) in enumerate(spans):
        found = jnp.sum(jnp.where(mask, rows[start:stop], 0.0), axis=0, keepdims=True)
        for i in range(4):
            gas_ref[f, first + i : first + i + 1, :] = found[:, i * BLK : (i + 1) * BLK]


def parcels_body(
    rad_ref, odd_ref, count_ref, move_ref, q_ref, parcel_ref, cells_ref,
    src_out, stay_out, leave_out, rad_out, gas_ref, state_ref, leave_ref,
):
    rad_edges(rad_ref[0], q_ref, rad_out)
    table = jnp.concatenate(
        [jnp.concatenate(halves(q_ref[f + 1].reshape(ROWS, CR).T), axis=1) for f in range(3)], axis=0
    )
    spans = [(f * CR, (f + 1) * CR) for f in range(3)]
    ready = one_hot_rows(cells_ref, 0, 4)
    for first in range(0, BLK_DEV, 4):
        hot, lanes = ready
        rows = jnp.dot(table, jnp.concatenate([hot, hot], axis=0), preferred_element_type=F32)
        if first + 4 < BLK_DEV:
            ready = one_hot_rows(cells_ref, first + 4, 4)
        pick(rows, first, spans, iota((CR, 4 * BLK), 0) == lanes, gas_ref)
    state, sources = step(count_ref, parcel_ref, gas_ref)
    for i in range(4):
        src_out[i] = sources[i]
        state_ref[i] = state[i]
    leave_ref[...] = jnp.zeros_like(leave_ref)
    up, down, spare = jnp.int32(0), jnp.int32(0), 2 * MOVEB - 1
    for block in range(BLK_DEV):
        move = move_ref[block]
        row = state_ref[:, block : block + 1, :]
        stay_out[:, block : block + 1, :] = jnp.where(move == 0, row, 0.0)
        to_up = jnp.where(move == 1, jnp.minimum(up, MOVEB - 1), spare)
        to_down = jnp.where(move == -1, jnp.minimum(down, MOVEB - 1), spare)
        leave_ref[0, :, pl.ds(to_up, 1), :] = row
        leave_ref[1, :, pl.ds(to_down, 1), :] = row
        up = up + jnp.where(move == 1, 1, 0)
        down = down + jnp.where(move == -1, 1, 0)
    odd = odd_ref[0] == 1
    up, down = leave_ref[0, :, :MOVEB], leave_ref[1, :, :MOVEB]
    leave_out[0] = jnp.where(odd, down, up)
    leave_out[1] = jnp.where(odd, up, down)


SOURCE_OF = (0, 1, 2, 3, 0)


def near_parcels_body(count_ref, tiles_ref, parcel_ref, cells_ref, near_out, gas_ref, hot_ref, spread_ref):
    start = 16
    table = jnp.concatenate(halves(tiles_ref[start : 4 * BAND]), axis=0)
    depth = 4 * BAND - start
    spans = [((f + 1) * BAND - start, (f + 1) * BAND - start + CYCLES) for f in range(3)]
    for first in range(0, BLK_DEV, 4):
        hot, lanes = one_hot_rows(cells_ref, first, 4)
        hot_ref[:, first * BLK : (first + 4) * BLK] = hot
        rows = jnp.dot(table, hot, preferred_element_type=F32)
        rows = rows[:depth] + rows[depth:]
        pick(rows, first, spans, iota((CYCLES, 4 * BLK), 0) == lanes, gas_ref)
    _, sources = step(count_ref, parcel_ref, gas_ref)
    rows = [s.astype(BF16) for s in sources]
    rows = [r.astype(F32) for r in rows] + [s - r.astype(F32) for s, r in zip(sources, rows)]
    zero = jnp.zeros((), BF16)
    for first in range(0, BLK_DEV, 4):
        mask = equals(CYCLES, lane_row(cells_ref, first, 4) & (CR - 1))
        for i, row in enumerate(rows):
            row = jnp.concatenate([row[first + j : first + j + 1] for j in range(4)], axis=1).astype(BF16)
            spread_ref[i * CYCLES : (i + 1) * CYCLES, first * BLK : (first + 4) * BLK] = jnp.where(mask, row, zero)
    total = lax.dot_general(spread_ref[...], hot_ref[...], NT, preferred_element_type=F32)
    near_out[...] = total[: 4 * CYCLES] + total[4 * CYCLES :]


def near_body(
    odd_ref, coef_ref, first_ref, second_ref, tiles_ref, near_ref, send_hbm, send_out, sems
):
    copies = []
    lane = iota((CR, 2 * CAZ), 1)
    z = lane % CAZ
    tiles = [tiles_ref[:, p * 2 * CAZ : (p + 1) * 2 * CAZ] for p in range(PAIRS)]
    odd = odd_ref[0] == 1
    first, second = first_ref[...], second_ref[...]
    before, after = jnp.where(odd, first, second), jnp.where(odd, second, first)
    halo = turned([jnp.concatenate([before[f], after[f]], axis=0) for f in range(FIELDS)])

    column = iota((CR, 1), 0)
    radius = column
    c = [jnp.zeros((CR, 1), F32) for _ in range(6)]
    for f in range(FIELDS):
        here = (column >= f * BAND) & (column < (f + 1) * BAND)
        radius = jnp.where(here, column - f * BAND, radius)
        c = [jnp.where(here, coef_ref[f, i], c[i]) for i in range(6)]
    metric = 4.0 / (radius.astype(F32) + 4.0)
    mid = (1.0 - c[1] - c[5]) - c[3] * metric
    az_up, az_down = (0.5 * (c[2] + c[3])) * metric, (0.5 * (c[3] - c[2])) * metric
    ax_up, ax_down = 0.5 * (c[0] + c[1]), 0.5 * (c[1] - c[0])
    rad_up = 0.5 * (c[4] + c[5])
    rad_down = jnp.where(radius == 0, 0.0, 0.5 * (c[5] - c[4]))
    low = lane < CAZ
    swapped = [pltpu.roll(t, CAZ, 1) for t in tiles]
    for p in range(PAIRS):
        q = tiles[p]
        ahead = jnp.where(low, swapped[p], swapped[p + 1] if p + 1 < PAIRS else halo)
        behind = jnp.where(low, swapped[p - 1] if p else halo, swapped[p])
        az_a = jnp.where(z == CAZ - 1, 0.0, pltpu.roll(q, 2 * CAZ - 1, 1))
        az_b = jnp.where(z == 0, 0.0, pltpu.roll(q, 1, 1))
        r_a = pltpu.roll(q, CR - 1, 0)
        r_b = pltpu.roll(q, 1, 0)
        out = (
            mid * q + ax_up * ahead + ax_down * behind + az_up * az_a + az_down * az_b
            + rad_up * r_a + rad_down * r_b
        )
        ends = jnp.where(z == 0, az_up * q, jnp.where(z == CAZ - 1, az_down * q, 0.0))
        ends = sum(
            pltpu.roll(ends[f * BAND : f * BAND + CYCLES], 2 * f, 1) if f else ends[:CYCLES]
            for f in range(FIELDS)
        )
        for f in range(FIELDS):
            s = SOURCE_OF[f] * CYCLES
            block = out[f * BAND : f * BAND + CYCLES] + near_ref[
                s : s + CYCLES, p * 2 * CAZ : (p + 1) * 2 * CAZ
            ]
            for quad in range(QUADS):
                send_out[p * QUADS + quad, f * 4 : f * 4 + 4, :] = block[quad * 4 : quad * 4 + 4]
        for quad in range(QUADS):
            send_out[p * QUADS + quad, LINES : LINES + 4, :] = ends[quad * 4 : quad * 4 + 4]
        span = pl.ds(p * QUADS, QUADS)
        copies.append(pltpu.make_async_copy(send_out.at[span], send_hbm.at[span], sems.at[p]))
        copies[p].start()
    for copy in copies:
        copy.wait()


def rad_edges(rad, q_ref, rad_out):
    extra = jnp.where(rad == 0, 1, 0)
    lane = iota((32, CR), 1)
    packed = jnp.zeros((32, CR), F32)
    for f in range(FIELDS):
        for g in range(16):
            part = q_ref[f, g // 2, (g % 2) * 32 : (g % 2) * 32 + 32, :]
            spot = g * 8 + f
            packed = jnp.where(lane == spot, pltpu.roll(part, spot + extra, 1), packed)
    rad_out[...] = packed


def gas_body(
    rad_ref, odd_ref, az_ref, coef_ref, q_ref, first_ref, second_ref, az_first, az_second, rad_in, src_ref,
    cells_ref, _,
    sect_out, hot_ref, spread_ref,
):
    width = 4
    zero = jnp.zeros((), BF16)

    def scattered(i):
        for first in range(0, BLK_DEV, width):
            cols = slice(first * BLK, (first + width) * BLK)
            if i == 0:
                hot_ref[:, cols] = one_hot_rows(cells_ref, first, width)[0]
            mask = equals(CR, lane_row(cells_ref, first, width) & (CR - 1))
            row = jnp.concatenate([src_ref[i, first + j : first + j + 1, :] for j in range(width)], axis=1)
            high = row.astype(BF16)
            low = (row - high.astype(F32)).astype(BF16)
            spread_ref[i, 0:CR, cols] = jnp.where(mask, high, zero)
            spread_ref[i, CR:, cols] = jnp.where(mask, low, zero)
        total = lax.dot_general(hot_ref[...], spread_ref[i], NT, preferred_element_type=F32)
        return total[:, :CR] + total[:, CR:]

    rad = rad_ref[0]
    odd = odd_ref[0] == 1
    row = iota((CAZ, CR), 0)
    lane = iota((1, CR), 1)
    metric = 4.0 / ((rad * CR + lane).astype(F32) + 4.0)
    target = jnp.where(rad == 0, CR - 1, 0)
    odd_az = az_ref[0] % 2 == 1
    az_prev = jnp.where(odd_az, az_first[...], az_second[...])
    az_next = jnp.where(odd_az, az_second[...], az_first[...])
    added = {0: scattered(0)}
    for f in (0, 4, 1, 2, 3):
        if f in (0, 1, 2):
            added[f + 1] = scattered(f + 1)
        c = [coef_ref[f, i] for i in range(6)]
        mid = (1.0 - c[1] - c[5]) - c[3] * metric
        az_up_edge, az_down_edge = (0.5 * (c[2] + c[3])) * metric, (0.5 * (c[3] - c[2])) * metric
        az_up = jnp.where(row == CAZ - 1, 0.0, az_up_edge)
        az_down = jnp.where(row == 0, 0.0, az_down_edge)
        ax_up, ax_down = 0.5 * (c[0] + c[1]), 0.5 * (c[1] - c[0])
        rad_up = jnp.where(lane == CR - 1, 0.0, 0.5 * (c[4] + c[5]))
        rad_down = jnp.where(lane == 0, 0.0, 0.5 * (c[5] - c[4]))
        across = 0.5 * jnp.where(rad == 0, c[4] + c[5], c[5] - c[4])
        across = jnp.where(lane == target, across, 0.0)
        for a in range(CAX):
            q = q_ref[f, a]
            ahead = q_ref[f, a + 1] if a + 1 < CAX else jnp.where(odd, second_ref[f], first_ref[f])
            behind = q_ref[f, a - 1] if a else jnp.where(odd, first_ref[f], second_ref[f])
            edge = jnp.concatenate(
                [pltpu.roll(rad_in[...], (target + (2 * CR - ((2 * a + h) * 8 + f))) % CR, 1) for h in range(2)],
                axis=0,
            )
            sect_out[f, a] = (
                mid * q + ax_up * ahead + ax_down * behind
                + az_up * pltpu.roll(q, CAZ - 1, 0) + az_down * pltpu.roll(q, 1, 0)
                + rad_up * pltpu.roll(q, CR - 1, 1) + rad_down * pltpu.roll(q, 1, 1)
                + across * edge
                + added[SOURCE_OF[f]][a * CAZ : (a + 1) * CAZ]
            )
            sect_out[f, a, 0:1] += az_down_edge * az_prev[f, a : a + 1]
            sect_out[f, a, CAZ - 1 : CAZ] += az_up_edge * az_next[f, a : a + 1]


def lined(pieces, line_ref):
    low = iota((LINES, 2 * CAZ), 1) < CAZ
    for i in range(N_AZ // 2):
        t0, t1 = pieces(2 * i), pieces(2 * i + 1)
        cols = slice(i * 2 * CAZ, (i + 1) * 2 * CAZ)
        line_ref[0:LINES, cols] = jnp.where(low, t0, pltpu.roll(t1, CAZ, 1))
        line_ref[BAND : BAND + LINES, cols] = jnp.where(low, pltpu.roll(t0, CAZ, 1), t1)


def filter_body(
    az_ref, width_ref, basis_ref, turned_ref, got_ref, moved_ref,
    send_out, onward_out, line_ref, ends_ref, piece_ref,
):
    onward_out[...] = moved_ref[1]
    quad = az_ref[0] % QUADS
    low = iota((LINES, 2 * CAZ), 1) < CAZ
    line_ref[...] = jnp.zeros_like(line_ref)
    ends_ref[...] = jnp.zeros_like(ends_ref)
    for s in range(N_AZ):
        packed = got_ref[s, LINES : LINES + 4, :]
        for f in range(FIELDS):
            piece_ref[s, f * 4 : f * 4 + 4, :] = pltpu.roll(packed, 2 * CAZ - 2 * f, 1) if f else packed
    lined(lambda s: got_ref[s, 0:LINES, :], line_ref)
    lined(lambda s: piece_ref[s], ends_ref)
    z = iota((2 * BAND, NAZ), 1) % CAZ
    ends = ends_ref[...]
    lines = (
        line_ref[...]
        + jnp.where(z == CAZ - 1, pltpu.roll(ends, NAZ - 1, 1), 0.0)
        + jnp.where(z == 0, pltpu.roll(ends, 1, 1), 0.0)
    )
    rows = 2 * BAND
    both = jnp.concatenate(halves(lines), axis=0)
    whole = jnp.dot(both, turned_ref[...], preferred_element_type=F32)
    coefs = whole[:rows, :MODES] + whole[rows:, :MODES] + whole[:rows, MODES:]
    column = iota((rows, MODES), 1)
    cycle = iota((rows, MODES), 0) % 4
    mode = jnp.where(column < HALF, column, column - HALF + 1)
    width = jnp.zeros((rows, MODES), jnp.int32)
    for i in range(4):
        width = jnp.where(cycle == i, width_ref[quad * 4 + i], width)
    weight = jnp.where(mode == 0, 1.0 / NAZ, 2.0 / NAZ)
    coefs = coefs * jnp.where(mode < width, weight, 0.0)
    high, rest = halves(coefs)
    line_ref[...] = jnp.dot(
        jnp.concatenate([high, high], axis=1), basis_ref[...], preferred_element_type=F32
    ) + jnp.dot(rest, basis_ref[:MODES], preferred_element_type=F32)
    for i in range(N_AZ // 2):
        cols = slice(i * 2 * CAZ, (i + 1) * 2 * CAZ)
        t0, t1 = line_ref[0:LINES, cols], line_ref[BAND : BAND + LINES, cols]
        send_out[2 * i, 0:LINES] = jnp.where(low, t0, pltpu.roll(t1, CAZ, 1))
        send_out[2 * i + 1, 0:LINES] = jnp.where(low, pltpu.roll(t0, CAZ, 1), t1)


def merge_body(
    rad_ref, odd_ref, sect_ref, got_ref, stay_ref, moved_ref, onward_ref, gas_out, parcels_out, flip_ref
):
    odd = odd_ref[0] == 1
    parcels_out[:, 0:BLK_DEV, :] = stay_ref[...]
    first, second = moved_ref[0], onward_ref[...]
    parcels_out[:, BLK_DEV : BLK_DEV + MOVEB, :] = jnp.where(odd, first, second)
    parcels_out[:, BLK_DEV + MOVEB :, :] = jnp.where(odd, second, first)
    near = (iota((2 * CAZ, CR), 1) < CYCLES) & (rad_ref[0] == 0)
    tiles = []
    for pair in range(PAIRS):
        flip_ref[pair, FIELDS * CYCLES :, :] = jnp.zeros((CR - FIELDS * CYCLES, CR), F32)
        for f in range(FIELDS):
            for quad in range(QUADS):
                first = f * CYCLES + quad * 4
                flip_ref[pair, first : first + 4, :] = got_ref[pair * QUADS + quad, f * 4 : f * 4 + 4, :]
        tiles.append(flip_ref[pair].T)
    for f in range(FIELDS):
        for pair in range(PAIRS):
            moved = pltpu.roll(tiles[pair], CR - f * CYCLES, 1) if f else tiles[pair]
            kept = sect_ref[f, 2 * pair : 2 * pair + 2].reshape(2 * CAZ, CR)
            gas_out[f, 2 * pair : 2 * pair + 2] = jnp.where(near, moved, kept).reshape(2, CAZ, CR)


def shards(fields, coeffs, parcels, cells, counts, moves, widths):
    rad_index = lax.axis_index("rad").astype(jnp.int32).reshape(1)
    az_index = lax.axis_index("az").astype(jnp.int32).reshape(1)
    odd = (lax.axis_index("ax").astype(jnp.int32) % 2).reshape(1)
    n_ax, n_az, n_rad = (lax.axis_size(axis) for axis in ("ax", "az", "rad"))
    parcels = parcels.reshape(4, BLK_DEV, BLK)
    cells = cells.reshape(BLK_DEV, BLK)
    counts = counts.reshape(1)
    moves = moves.reshape(BLK_DEV)
    inner = [(i, i ^ 1) for i in range(n_ax)]
    outer = [(i, ((i + 1) ^ 1) - 1) for i in range(1, n_ax - 1)]
    along = [(i, i + 2) for i in range(0, n_ax - 2, 2)] + [(i, i - 2) for i in range(3, n_ax, 2)]
    inner_az = [(i, i ^ 1) for i in range(n_az)]
    outer_az = [(i, (((i + 1) ^ 1) - 1) % n_az) for i in range(n_az)]
    across = [(i, i ^ 1) for i in range(n_rad)]
    gas_shape = (FIELDS, CAX, CAZ, CR)

    first, second, az_first, az_second = call(
        edges_body, [(FIELDS, CAZ, CR)] * 2 + [(FIELDS, CAX, CR)] * 2, [SMEM, SMEM, VMEM], 10**6, 10**6, mib=4
    )(odd, az_index, fields)
    first = lax.ppermute(first, "ax", inner)
    second = lax.ppermute(second, "ax", outer)
    az_first = lax.ppermute(az_first, "az", inner_az)
    az_second = lax.ppermute(az_second, "az", outer_az)

    (tiles,) = call(tiles_body, [(CR, ROWS)], [VMEM], 10**6, 10**6, mib=4)(fields)
    (near,) = call(
        near_parcels_body,
        [(4 * CYCLES, ROWS)],
        [SMEM] + [VMEM] * 3, 3 * 10**9, 2 * 10**6,
        [
            pltpu.VMEM((3, BLK_DEV, BLK), F32),
            pltpu.VMEM((ROWS, PARCELS), BF16),
            pltpu.VMEM((8 * CYCLES, PARCELS), BF16),
        ],
        mib=16,
    )(counts, tiles, parcels, cells)

    (to_owner,) = call(
        near_body,
        [(N_AZ, LINES + 4, 2 * CAZ)],
        [SMEM, SMEM] + [VMEM] * 4, 10**7, 4 * 10**6,
        [
            pltpu.VMEM((N_AZ, LINES + 4, 2 * CAZ), F32),
            pltpu.SemaphoreType.DMA((PAIRS,)),
        ],
        mib=8,
        hbm_first=True,
    )(odd, coeffs, first, second, tiles, near)
    lines = lax.all_to_all(to_owner, "az", 0, 0, tiled=True)

    src, stay, leaving, rad_edge = call(
        parcels_body,
        [(4, BLK_DEV, BLK), (4, BLK_DEV, BLK), (2, 4, MOVEB, BLK), (32, CR)],
        [SMEM] * 4 + [VMEM] * 3, 6 * 10**9, 2 * 10**6,
        [
            pltpu.VMEM((3, BLK_DEV, BLK), F32),
            pltpu.VMEM((4, BLK_DEV, BLK), F32),
            pltpu.VMEM((2, 4, 2 * MOVEB, BLK), F32),
        ],
        mib=16,
    )(rad_index, odd, counts, moves, fields, parcels, cells)
    rad_got = lax.ppermute(rad_edge, "rad", across)
    moved = lax.ppermute(leaving, "ax", inner)

    basis, basis_turned = basis_parts()
    to_home, onward = call(
        filter_body,
        [(N_AZ, LINES, 2 * CAZ), (4, MOVEB, BLK)],
        [SMEM, SMEM] + [VMEM] * 4, 10**8, 10**6,
        [
            pltpu.VMEM((2 * BAND, NAZ), F32),
            pltpu.VMEM((2 * BAND, NAZ), F32),
            pltpu.VMEM((N_AZ, LINES, 2 * CAZ), F32),
        ],
        mib=6,
    )(az_index, widths, basis, basis_turned, lines, moved)
    filtered = lax.all_to_all(to_home, "az", 0, 0, tiled=True)
    onward = lax.ppermute(onward, "ax", along)

    (sect,) = call(
        gas_body, [gas_shape], [SMEM] * 4 + [VMEM] * 8 + [ANY], 8 * 10**9, 4 * 10**6,
        [pltpu.VMEM((ROWS, PARCELS), BF16), pltpu.VMEM((4, 2 * CR, PARCELS), BF16)],
        mib=24,
    )(rad_index, odd, az_index, coeffs, fields, first, second, az_first, az_second, rad_got, src, cells, to_home)

    gas_out, parcels_out = call(
        merge_body,
        [gas_shape, (4, BLK_DEV + 2 * MOVEB, BLK)],
        [SMEM, SMEM] + [VMEM] * 5, 10**6, 4 * 10**6,
        [pltpu.VMEM((PAIRS, CR, CR), F32)],
        mib=8,
    )(rad_index, odd, sect, filtered, stay, moved, onward)
    return gas_out, parcels_out.reshape(4, BLK_DEV + 2 * MOVEB, 1, BLK)


def solution(mesh):
    block = P(None, "ax", "az", "rad")
    flat = P("ax", "az", "rad")
    return jax.shard_map(
        shards,
        mesh=mesh,
        in_specs=(block, P(), block, flat, flat, flat, P()),
        out_specs=(block, block),
        check_vma=False,
    )
```
